32 devices in a mesh: phase: 4 (over y, x), slab: 8 (over z, core).
Axes of the slice: x: 2, y: 2, z: 4, core: 2. Of those that a mesh axis runs over, the one named last changes fastest.
Arguments:
- normed: bfloat16 [16, 16, 128, 1024], P('phase', 'slab'), may hold values from -5 to 5
- block_list: int32 [16, 16, 5], P('phase', 'slab'), may hold values from 0 to 255, as said below
- registers: bfloat16 [256, 1024], replicated, may hold values from -5 to 5
- w_query: bfloat16 [1024, 1024], replicated, may hold values from -0.25 to 0.25
- w_key: bfloat16 [1024, 1024], replicated, may hold values from -0.25 to 0.25
- w_value: bfloat16 [1024, 1024], replicated, may hold values from -0.1875 to 0.1875
- w_out: bfloat16 [1024, 1024], replicated, may hold values from -0.1875 to 0.1875
Outputs:
- mixed: bfloat16 [16, 16, 128, 1024], P('phase', 'slab')
- register_out: bfloat16 [256, 1024], replicated
The draws below stay inside these ranges and needn't reach their ends.
Inputs may be any that keep to these rules, and one draw needn't show every extreme that they name: Entry 0 of block_list[p, z] is p * 16 + z itself; the 5 entries of a list are distinct, and each names a block (p2, z2) with p2 one of p - 1, p, p + 1 taken modulo 16 and z2 one of z - 1, z, z + 1 within 0 to 15.
All inputs are finite; a program needn't handle non-finite values.
Results may differ from the reference program's by a relative error of at most 0.01.
Values may be sent and summed in bfloat16 or wider, within the bound.
No kernel may reach another device: no remote copies, remote signals or barrier semaphores. Data moves between devices by JAX's collectives and lax.ppermute only.
A program may use at most 192 MiB of HBM per device.

```python
import jax
import jax.numpy as jnp
from jax import lax

D = 1024
HEADS = 16
REG = 256
BLK = 128
LIST = 5
PH_DEV = 4
SB = 2
NPH = 16
NZB = 16
N_PHASE = 4
N_SLAB = 8


def draw_normed(key, part):
    key = jax.random.fold_in(key, 11)
    noise_key = jax.random.fold_in(key, 0)
    phase_ramp = jnp.arange(NPH, dtype=jnp.float32) / max(NPH - 1, 1)
    depth_ramp = jnp.arange(NZB, dtype=jnp.float32) / max(NZB - 1, 1)
    spread = 0.5 * 3.0 ** (0.5 * (phase_ramp[:, None] + depth_ramp[None, :]))
    background = jnp.clip(jax.random.normal(noise_key, (NPH, NZB, BLK, D), jnp.float32), -3.0, 3.0)
    result = background * spread[:, :, None, None]
    return result.astype(jnp.bfloat16)


def draw_registers(key, part):
    key = jax.random.fold_in(key, 13)
    noise_key = jax.random.fold_in(key, 0)
    result = jnp.clip(jax.random.normal(noise_key, (REG, D), jnp.float32), -3.0, 3.0)
    return result.astype(jnp.bfloat16)


def projection_draw(key, salt):
    key = jax.random.fold_in(key, salt)
    result = jnp.clip(jax.random.normal(key, (D, D), jnp.float32), -6.0, 6.0) * D ** (-0.5)
    return jnp.clip(result, -0.25, 0.25).astype(jnp.bfloat16)


def draw_w_query(key, part):
    return projection_draw(key, 21)


def draw_w_key(key, part):
    return projection_draw(key, 23)


def draw_block_list(key, part):
    key = jax.random.fold_in(key, 5)
    phase_step = jnp.array([-1, -1, -1, 0, 0, 0, 1, 1, 1], jnp.int32)
    depth_step = jnp.array([-1, 0, 1, -1, 0, 1, -1, 0, 1], jnp.int32)
    ranking = jax.random.randint(key, (NPH, NZB, 9), 0, 4096) * 16 + jnp.arange(9, dtype=jnp.int32)
    depth_all = jnp.arange(NZB, dtype=jnp.int32)[None, :, None] + depth_step[None, None, :]
    inside = (depth_all >= 0) & (depth_all < NZB)
    ranking = jnp.where(inside, ranking, 1 << 20)
    ranking = jnp.where(jnp.arange(9, dtype=jnp.int32) == 4, -1, ranking)
    order = jnp.argsort(ranking, axis=-1, stable=True)[..., :LIST]
    phase_sel = (jnp.arange(NPH, dtype=jnp.int32)[:, None, None] + phase_step[order]) % NPH
    depth_sel = jnp.arange(NZB, dtype=jnp.int32)[None, :, None] + depth_step[order]
    return (phase_sel * NZB + depth_sel).astype(jnp.int32)


def bell_draw(own_key, extent, scale, limit, held_as=jnp.bfloat16):
    values = scale * jax.random.normal(own_key, extent, jnp.float32)
    return jnp.clip(values, min=-limit, max=limit).astype(held_as)


def setup_inputs(seed: int = 0) -> dict:
    streams_of = jax.random.split(jax.random.key(seed), 8)
    return {
        "normed": draw_normed(jax.random.fold_in(streams_of[7], 71), 0),
        "block_list": draw_block_list(jax.random.fold_in(streams_of[7], 71), 0),
        "registers": draw_registers(jax.random.fold_in(streams_of[7], 71), 0),
        "w_query": draw_w_query(jax.random.fold_in(streams_of[7], 71), 0),
        "w_key": draw_w_key(jax.random.fold_in(streams_of[7], 71), 0),
        "w_value": bell_draw(streams_of[5], (D, D), D ** -0.5, 0.1875),
        "w_out": bell_draw(streams_of[6], (D, D), D ** -0.5, 0.1875),
    }


def project(token_rows, weight):
    return jnp.dot(token_rows, weight, preferred_element_type=jnp.float32).astype(jnp.bfloat16)


def window_attend(group_queries, key_rows, value_rows, register_keys, register_values, score_scale):
    query_float = group_queries.astype(jnp.float32)
    local_scores = jnp.einsum("gqhe,gkhe->ghqk", query_float, key_rows.astype(jnp.float32)) * score_scale
    remote = jnp.einsum("gqhe,rhe->ghqr", query_float, register_keys.astype(jnp.float32)) * score_scale
    scores = jnp.concatenate([local_scores, remote], axis=-1)
    row_peak = jnp.max(scores, axis=-1, keepdims=True)
    shifted = jnp.exp(scores - row_peak)
    probabilities = (shifted / jnp.sum(shifted, axis=-1, keepdims=True)).astype(jnp.bfloat16)
    key_count = key_rows.shape[1]
    context = jnp.einsum("ghqk,gkhe->gqhe", probabilities[..., :key_count].astype(jnp.float32), value_rows.astype(jnp.float32))
    context = context + jnp.einsum("ghqr,rhe->gqhe", probabilities[..., key_count:].astype(jnp.float32), register_values.astype(jnp.float32))
    return context.astype(jnp.bfloat16)


def reference(normed, block_list, registers, w_query, w_key, w_value, w_out):
    phase_count, depth_blocks, block_len, model_width = normed.shape
    head_count = HEADS
    head_width = model_width // head_count
    score_scale = head_width ** -0.5
    token_rows = normed.reshape(-1, model_width)
    queries = project(token_rows, w_query).reshape(phase_count, depth_blocks, block_len, head_count, head_width)
    all_keys = project(token_rows, w_key).reshape(phase_count * depth_blocks, block_len, head_count, head_width)
    all_values = project(token_rows, w_value).reshape(phase_count * depth_blocks, block_len, head_count, head_width)
    register_query = project(registers, w_query).reshape(-1, head_count, head_width)
    register_keys = project(registers, w_key).reshape(-1, head_count, head_width)
    register_values = project(registers, w_value).reshape(-1, head_count, head_width)

    def one_phase(inputs):
        phase_queries, phase_lists = inputs
        chosen_keys = all_keys[phase_lists].reshape(depth_blocks, LIST * block_len, head_count, head_width)
        chosen_values = all_values[phase_lists].reshape(depth_blocks, LIST * block_len, head_count, head_width)
        context = window_attend(phase_queries, chosen_keys, chosen_values, register_keys, register_values, score_scale)
        return project(context.reshape(depth_blocks * block_len, model_width), w_out).reshape(depth_blocks, block_len, model_width)

    mixed = lax.map(one_phase, (queries, block_list))

    group_shape = (N_PHASE, PH_DEV, N_SLAB, SB, block_len, head_count, head_width)
    grouped_keys = all_keys.reshape(group_shape).transpose(0, 2, 1, 3, 4, 5, 6).reshape(N_PHASE * N_SLAB, -1, head_count, head_width)
    grouped_values = all_values.reshape(group_shape).transpose(0, 2, 1, 3, 4, 5, 6).reshape(N_PHASE * N_SLAB, -1, head_count, head_width)

    def one_group(inputs):
        group_keys, group_values = inputs
        scores = jnp.einsum("rhe,the->hrt", register_query.astype(jnp.float32), group_keys.astype(jnp.float32)) * score_scale
        row_peak = jnp.max(scores, axis=-1)
        weights = jnp.exp(scores - row_peak[:, :, None]).astype(jnp.bfloat16)
        weight_sum = jnp.sum(weights.astype(jnp.float32), axis=-1)
        weighted = jnp.einsum("hrt,the->rhe", weights.astype(jnp.float32), group_values.astype(jnp.float32))
        return row_peak, weight_sum, weighted

    group_peaks, group_sums, group_values = lax.map(one_group, (grouped_keys, grouped_values))
    global_peak = jnp.max(group_peaks, axis=0)
    factor = jnp.exp(group_peaks - global_peak[None])
    register_sum = jnp.sum(group_sums * factor, axis=0)
    register_value = jnp.sum(group_values * jnp.transpose(factor, (0, 2, 1))[:, :, :, None], axis=0)
    register_context = (register_value / register_sum.T[:, :, None]).astype(jnp.bfloat16).reshape(-1, model_width)
    register_out = project(register_context, w_out)
    return mixed, register_out
```

```python
import functools

import jax
import jax.numpy as jnp
from jax import lax
from jax.experimental import pallas as pl
from jax.experimental.pallas import tpu as pltpu
from jax.sharding import PartitionSpec as P

HEADS = 16
LIST = 5
QUAD = 4
LOG2E = 1.4426950408889634
F32, BF16 = jnp.float32, jnp.bfloat16
VMEM_LIMIT = 56 * 1024 * 1024


def params():
    return pltpu.CompilerParams(vmem_limit_bytes=VMEM_LIMIT)


def cost(macs, size, exps=0):
    return pl.CostEstimate(flops=2 * macs, bytes_accessed=size, transcendentals=exps)


def matmul(a, b):
    return jnp.dot(a, b, preferred_element_type=F32)


def matmul_t(a, b):
    return lax.dot_general(a, b, (((1,), (1,)), ((), ())), preferred_element_type=F32)


def own_kernel(steps, scale, x_ref, reg_ref, wq_ref, wk_ref, wv_ref, q_ref, kv_ref):
    width = wq_ref.shape[1]

    def work(rows):
        q_ref[...] = (matmul(rows, wq_ref[...]) * scale).astype(BF16)
        blk = kv_ref.shape[1]
        for half in range(rows.shape[0] // blk):
            part = rows[half * blk : (half + 1) * blk]
            kv_ref[half, :, :width] = matmul(part, wk_ref[...]).astype(BF16)
            kv_ref[half, :, width:] = matmul(part, wv_ref[...]).astype(BF16)

    @pl.when(pl.program_id(0) == 0)
    def _():
        work(reg_ref[...])

    @pl.when(pl.program_id(0) > 0)
    def _():
        work(x_ref[...])


def own_project(rows, registers, w_query, w_key, w_value, slots, blk, scale):
    count, width = rows.shape
    tile = registers.shape[0]
    steps = count // tile
    whole = pl.BlockSpec((width, width), lambda i: (0, 0))
    per = tile // blk
    return pl.pallas_call(
        functools.partial(own_kernel, steps, scale),
        grid=(steps + 1,),
        in_specs=[
            pl.BlockSpec((tile, width), lambda i: (jnp.maximum(i - 1, 0), 0)),
            pl.BlockSpec((tile, width), lambda i: (0, 0)),
            whole,
            whole,
            whole,
        ],
        out_specs=[
            pl.BlockSpec((tile, width), lambda i: (i, 0)),
            pl.BlockSpec((per, blk, 2 * width), lambda i: (i, 0, 0)),
        ],
        out_shape=[
            jax.ShapeDtypeStruct((count + tile, width), BF16),
            jax.ShapeDtypeStruct((slots, blk, 2 * width), BF16),
        ],
        compiler_params=params(),
        cost_estimate=cost((count + tile) * width * width * 3, 18 << 20),
        name="own_project",
    )(rows, registers, w_query, w_key, w_value)


def halo_kernel(per_piece, pieces, *refs):
    xs, (wk_ref, wv_ref, _, kv_ref) = refs[:pieces], refs[pieces:]
    width = wk_ref.shape[1]
    for piece in range(pieces):

        @pl.when(pl.program_id(0) // per_piece == piece)
        def _():
            rows, blk, _ = kv_ref.shape
            x = xs[piece][...].reshape(rows * blk, width)
            kv_ref[:, :, :width] = matmul(x, wk_ref[...]).astype(BF16).reshape(rows, blk, width)
            kv_ref[:, :, width:] = matmul(x, wv_ref[...]).astype(BF16).reshape(rows, blk, width)


def halo_project(table, pieces, first_slot, w_key, w_value):
    slots, blk, _ = table.shape
    width = w_key.shape[0]
    each = pieces[0].shape[0]
    group = 2 if each % 2 == 0 and first_slot % 2 == 0 else 1
    per_piece = each // group
    whole = pl.BlockSpec((width, width), lambda i: (0, 0))

    def piece_map(piece):
        return lambda i: (jnp.clip(i - piece * per_piece, 0, per_piece - 1), 0, 0)

    first = first_slot // group
    return pl.pallas_call(
        functools.partial(halo_kernel, per_piece, len(pieces)),
        grid=(per_piece * len(pieces),),
        in_specs=[pl.BlockSpec((group, blk, width), piece_map(n)) for n in range(len(pieces))]
        + [whole, whole, pl.BlockSpec(memory_space=pl.ANY)],
        out_specs=pl.BlockSpec((group, blk, 2 * width), lambda i: (first + i, 0, 0)),
        out_shape=jax.ShapeDtypeStruct(table.shape, BF16),
        input_output_aliases={len(pieces) + 2: 0},
        compiler_params=params(),
        cost_estimate=cost(each * len(pieces) * blk * width * width * 2, 10 << 20),
        name="halo_project",
    )(*pieces, w_key, w_value, table)


def head_masks(rows, lanes, head_width):
    lane = lax.broadcasted_iota(jnp.int32, (rows, lanes), 1)
    return [lane // head_width == h for h in range(lanes // head_width)]


def attend(q, k, v, masks):
    rows = q.shape[0]
    stack = jnp.concatenate([jnp.where(m, q, jnp.zeros_like(q)) for m in masks], axis=0)
    s = matmul_t(stack, k)
    peak = jnp.max(s, axis=-1, keepdims=True)
    p = jnp.exp2(s - peak)
    total = jnp.sum(p, axis=-1, keepdims=True)
    o = matmul(p.astype(BF16), v) * (1.0 / total)
    out = o[:rows]
    for h in range(1, len(masks)):
        out = jnp.where(masks[h], o[h * rows : (h + 1) * rows], out)
    return out, peak, total


def window_kernel(head_width, idx_ref, q_ref, *refs):
    k_refs, (reg_ref, wo_ref) = refs[:LIST], refs[LIST : LIST + 2]
    o_ref, ctx_ref = refs[-2:]
    rows, width = q_ref.shape
    lanes = QUAD * head_width
    masks = head_masks(rows, lanes, head_width)
    for g in range(width // lanes):
        at = slice(g * lanes, (g + 1) * lanes)
        at_v = slice(width + g * lanes, width + (g + 1) * lanes)
        k = jnp.concatenate(
            [r[0, :, at] for r in k_refs] + [reg_ref[n, :, at] for n in range(reg_ref.shape[0])], axis=0
        )
        v = jnp.concatenate(
            [r[0, :, at_v] for r in k_refs] + [reg_ref[n, :, at_v] for n in range(reg_ref.shape[0])], axis=0
        )
        out, _, _ = attend(q_ref[:, at], k, v, masks)
        ctx_ref[:, at] = out.astype(BF16)
    o_ref[0] = matmul(ctx_ref[...], wo_ref[...]).astype(BF16)


def window_attend(queries, table, slots, order, w_out, blk, reg_slots, head_width, previous):
    total, width = queries.shape[0] // blk - reg_slots, w_out.shape[0]
    n = len(order)
    start, stride = order[0], (order[1] - order[0] if n > 1 else 1)
    run = 1
    while run < n and order[run] == order[run - 1] + 1:
        run += 1
    jump = order[run] - order[0] if run < n else 0

    def block(i):
        return start + (i // run) * jump + i % run

    def list_map(entry):
        return lambda i, idx: (idx[block(i) * LIST + entry], 0, 0)

    operands = [slots, queries] + [table] * LIST + [table, w_out]
    in_specs = (
        [pl.BlockSpec((blk, width), lambda i, idx: (reg_slots + block(i), 0))]
        + [pl.BlockSpec((1, blk, 2 * width), list_map(e)) for e in range(LIST)]
        + [
            pl.BlockSpec((reg_slots, blk, 2 * width), lambda i, idx: (0, 0, 0)),
            pl.BlockSpec((width, width), lambda i, idx: (0, 0)),
        ]
    )
    aliases = {}
    if previous is not None:
        aliases = {len(operands): 0}
        operands.append(previous)
        in_specs.append(pl.BlockSpec(memory_space=pl.ANY))
    keys = (LIST + reg_slots) * blk
    return pl.pallas_call(
        functools.partial(window_kernel, head_width),
        grid_spec=pltpu.PrefetchScalarGridSpec(
            num_scalar_prefetch=1,
            grid=(n,),
            in_specs=in_specs,
            out_specs=pl.BlockSpec((1, blk, width), lambda i, idx: (block(i), 0, 0)),
            scratch_shapes=[pltpu.VMEM((blk, width), BF16)],
        ),
        out_shape=jax.ShapeDtypeStruct((total, blk, width), BF16),
        input_output_aliases=aliases,
        compiler_params=params(),
        cost_estimate=cost(n * blk * width * (8 * keys + width), n * 3 << 20, n * blk * HEADS * keys),
        name="window_attend",
    )(*operands)


def pack_levels(level):
    hi = level.astype(BF16)
    rest = level - hi.astype(F32)
    mid = rest.astype(BF16)
    low = (rest - mid.astype(F32)).astype(BF16)
    pad = jnp.zeros((level.shape[0], 128 - 3 * level.shape[1]), BF16)
    return jnp.concatenate([hi, mid, low, pad], axis=1)


def unpack_levels(cols):
    wide = cols.astype(F32)
    return wide[:, :HEADS] + wide[:, HEADS : 2 * HEADS] + wide[:, 2 * HEADS : 3 * HEADS]


def register_kernel(head_width, q_ref, kv_ref, o_ref):
    slots, blk, width2 = kv_ref.shape
    rows, width = q_ref.shape
    lanes = QUAD * head_width
    masks = head_masks(rows, lanes, head_width)
    levels = []
    for g in range(width // lanes):
        at = slice(g * lanes, (g + 1) * lanes)
        at_v = slice(width + g * lanes, width + (g + 1) * lanes)
        k = kv_ref[:, :, at].reshape(slots * blk, lanes)
        v = kv_ref[:, :, at_v].reshape(slots * blk, lanes)
        out, peak, total = attend(q_ref[:, at], k, v, masks)
        o_ref[:, at] = out.astype(BF16)
        level = peak + jnp.log2(total)
        levels += [level[h * rows : (h + 1) * rows] for h in range(len(masks))]
    o_ref[:, width:] = pack_levels(jnp.concatenate(levels, axis=1))


def register_attend(queries, table, rows, own_slots, head_width):
    _, blk, width2 = table.shape
    width = width2 // 2
    reg_slots = rows // blk
    assert own_slots % reg_slots == 0
    keys = own_slots * blk

    def body(*refs):
        q_ref, kv_refs, o_ref, scratch = refs[0], refs[1:-2], refs[-2], refs[-1]
        for n, r in enumerate(kv_refs):
            scratch[n * reg_slots : (n + 1) * reg_slots] = r[...]
        register_kernel(head_width, q_ref, scratch, o_ref)

    parts = own_slots // reg_slots
    return pl.pallas_call(
        body,
        grid=(1,),
        in_specs=[pl.BlockSpec((rows, width), lambda i: (0, 0))]
        + [
            pl.BlockSpec((reg_slots, blk, width2), functools.partial(lambda n, i: (n + 1, 0, 0), n))
            for n in range(parts)
        ],
        out_specs=pl.BlockSpec((rows, width + 128), lambda i: (0, 0)),
        out_shape=jax.ShapeDtypeStruct((rows, width + 128), BF16),
        scratch_shapes=[pltpu.VMEM((own_slots, blk, width2), BF16)],
        compiler_params=params(),
        cost_estimate=cost(rows * keys * width * 8, 6 << 20, rows * keys * HEADS),
        name="register_attend",
    )(queries, *[table] * parts)


def merged(a_ref, b_ref, width):
    la, lb = unpack_levels(a_ref[:, width:]), unpack_levels(b_ref[:, width:])
    top = jnp.maximum(la, lb)
    ea, eb = jnp.exp2(la - top), jnp.exp2(lb - top)
    total = ea + eb
    fa = ea / total
    fb = eb / total
    rows = a_ref.shape[0]
    head_width = width // HEADS
    lower = lax.broadcasted_iota(jnp.int32, (rows, 2 * head_width), 1) < head_width
    cols = []
    for pair in range(HEADS // 2):
        at = slice(pair * 2 * head_width, (pair + 1) * 2 * head_width)

        def spread(f):
            return jnp.where(lower, f[:, 2 * pair : 2 * pair + 1], f[:, 2 * pair + 1 : 2 * pair + 2])

        mix = a_ref[:, at].astype(F32) * spread(fa) + b_ref[:, at].astype(F32) * spread(fb)
        cols.append(mix.astype(BF16))
    return jnp.concatenate(cols, axis=1), top + jnp.log2(total)


def split_kernel(chunk, bit_ref, x_ref, keep_ref, send_ref):
    bit = bit_ref[0]
    for j in range(keep_ref.shape[0] // chunk):
        at = slice(j * chunk, (j + 1) * chunk)
        keep_ref[at] = x_ref[pl.ds(pl.multiple_of((2 * j + bit) * chunk, chunk), chunk)]
        send_ref[at] = x_ref[pl.ds(pl.multiple_of((2 * j + 1 - bit) * chunk, chunk), chunk)]


def small_call(body, out_shape, scratch, name, *operands):
    vmem = pl.BlockSpec(memory_space=pltpu.VMEM)
    return pl.pallas_call(
        body,
        in_specs=[pl.BlockSpec(memory_space=pltpu.SMEM)] + [vmem] * (len(operands) - 1),
        out_specs=jax.tree.map(lambda _: vmem, out_shape),
        out_shape=out_shape,
        scratch_shapes=scratch,
        compiler_params=params(),
        cost_estimate=cost(1 << 20, 1 << 20),
        name=name,
    )(*operands)


def register_merge(partial, w_out):
    rows, wide = partial.shape
    width = w_out.shape[0]
    slabs, phases = lax.axis_size("slab"), lax.axis_size("phase")
    slab = lax.axis_index("slab")
    chunk = rows // slabs

    def half(n):
        return [jax.ShapeDtypeStruct((n // 2, wide), BF16)] * 2

    rounds = slabs.bit_length() - 1
    bits = [((slab >> r) & 1).astype(jnp.int32).reshape(1) for r in range(rounds)]
    keep, send = small_call(
        functools.partial(split_kernel, chunk), half(rows), [], "register_split", bits[0], partial
    )
    for r in range(rounds):
        got = lax.ppermute(send, "slab", [(i, i ^ (1 << r)) for i in range(slabs)])
        held = keep.shape[0]
        if r + 1 < rounds:

            def body(bit_ref, a_ref, b_ref, keep_ref, send_ref, full_ref):
                mix, level = merged(a_ref, b_ref, width)
                full_ref[:, :width] = mix
                full_ref[:, width:] = pack_levels(level)
                split_kernel(chunk, bit_ref, full_ref, keep_ref, send_ref)

            keep, send = small_call(
                body, half(held), [pltpu.VMEM((held, wide), BF16)], "register_merge", bits[r + 1], keep, got
            )
        else:

            def body_all(bit_ref, a_ref, b_ref, full_ref):
                mix, level = merged(a_ref, b_ref, width)
                full_ref[:, :width] = mix
                full_ref[:, width:] = pack_levels(level)

            keep = small_call(
                body_all, jax.ShapeDtypeStruct((held, wide), BF16), [], "register_merge", bits[0], keep, got
            )
    turns = phases.bit_length() - 1
    for r in range(turns):
        got = lax.ppermute(keep, "phase", [(i, i ^ (1 << r)) for i in range(phases)])
        held = keep.shape[0]
        if r + 1 < turns:
            keep = small_call(
                body_all, jax.ShapeDtypeStruct((held, wide), BF16), [], "register_merge", bits[0], keep, got
            )
        else:

            def body_out(bit_ref, a_ref, b_ref, w_ref, out_ref):
                mix, _ = merged(a_ref, b_ref, width)
                out_ref[...] = matmul(mix, w_ref[...]).astype(BF16)

            keep = small_call(
                body_out,
                jax.ShapeDtypeStruct((held, width), BF16),
                [],
                "register_out",
                bits[0],
                keep,
                got,
                w_out,
            )
    return lax.all_gather(keep, "slab", axis=0, tiled=True)


def shards(normed, block_list, registers, w_query, w_key, w_value, w_out):
    own_phases, slab_blocks, blk, width = normed.shape
    head_width = width // HEADS
    scale = head_width ** (-0.5) * LOG2E
    phases, slabs = lax.axis_size("phase"), lax.axis_size("slab")
    rows = registers.shape[0]
    reg_slots = rows // blk
    own = own_phases * slab_blocks

    def around(x, axis, step, closed):
        n = lax.axis_size(axis)
        return lax.ppermute(
            x, axis, [(i, (i + step) % n) for i in range(n) if closed or 0 <= i + step < n]
        )

    before = around(normed[-1], "phase", 1, True)
    after = around(normed[0], "phase", -1, True)
    left = around(normed[:, -1], "slab", 1, False)
    right = around(normed[:, 0], "slab", -1, False)
    corner_left = around(jnp.stack([before[-1], after[-1]]), "slab", 1, False)
    corner_right = around(jnp.stack([before[0], after[0]]), "slab", -1, False)

    at_left = reg_slots + own
    at_right = at_left + own_phases
    at_before = at_right + own_phases
    at_after = at_before + slab_blocks
    at_corner = at_after + slab_blocks
    slots = at_corner + 4

    total_phases, depth_blocks = own_phases * phases, slab_blocks * slabs
    p = (block_list // depth_blocks - lax.axis_index("phase") * own_phases + 1) % total_phases - 1
    z = block_list % depth_blocks - lax.axis_index("slab") * slab_blocks
    is_left, is_right = z < 0, z >= slab_blocks
    is_before, is_after = p < 0, p >= own_phases
    inner = jnp.where(
        is_left, at_left + p, jnp.where(is_right, at_right + p, reg_slots + p * slab_blocks + z)
    )
    outer = jnp.where(
        is_left | is_right,
        at_corner + jnp.where(is_right, 2, 0) + jnp.where(is_after, 1, 0),
        jnp.where(is_after, at_after, at_before) + z,
    )
    slot_list = jnp.where(is_before | is_after, outer, inner).astype(jnp.int32).reshape(-1)

    queries, table = own_project(
        normed.reshape(-1, width), registers, w_query, w_key, w_value, slots, blk, scale
    )
    partial = register_attend(queries, table, rows, own, head_width)
    register_out = register_merge(partial, w_out)

    table = halo_project(table, [left, right], at_left, w_key, w_value)
    middle = list(range(slab_blocks, own - slab_blocks))
    edge = list(range(slab_blocks)) + list(range(own - slab_blocks, own))
    mixed = window_attend(
        queries, table, slot_list, middle, w_out, blk, reg_slots, head_width, None
    )
    table = halo_project(table, [before, after], at_before, w_key, w_value)
    table = halo_project(table, [corner_left, corner_right], at_corner, w_key, w_value)
    mixed = window_attend(
        queries, table, slot_list, edge, w_out, blk, reg_slots, head_width, mixed
    )
    return mixed.reshape(own_phases, slab_blocks, blk, width), register_out


def solution(mesh):
    placed = (P("phase", "slab", None, None), P("phase", "slab", None), P(), P(), P(), P(), P())
    return jax.shard_map(
        shards,
        mesh=mesh,
        in_specs=placed,
        out_specs=(P("phase", "slab", None, None), P()),
        check_vma=False,
    )
```

```python
import functools

import jax
import jax.numpy as jnp
from jax import lax
from jax.experimental import pallas as pl
from jax.experimental.pallas import tpu as pltpu
from jax.sharding import PartitionSpec as P

HEADS = 16
LIST = 5
QUAD = 4
LOG2E = 1.4426950408889634
F32, BF16 = jnp.float32, jnp.bfloat16
ANY = pl.BlockSpec(memory_space=pl.ANY)
TOKEN = jax.ShapeDtypeStruct((8, 128), jnp.float32)


def params(mib):
    return pltpu.CompilerParams(vmem_limit_bytes=mib << 20)


def cost():
    return pl.CostEstimate(flops=1 << 20, bytes_accessed=1 << 16, transcendentals=0)


def matmul(a, b):
    return jnp.dot(a, b, preferred_element_type=F32)


def matmul_t(a, b):
    return lax.dot_general(a, b, (((1,), (1,)), ((), ())), preferred_element_type=F32)


def t_matmul(a, b):
    return lax.dot_general(a, b, (((0,), (0,)), ((), ())), preferred_element_type=F32)


def spread_heads(q, head_width, heads):
    lane = lax.broadcasted_iota(jnp.int32, q.shape, 1) // head_width
    return jnp.concatenate([jnp.where(lane == h, q, jnp.zeros_like(q)) for h in heads], axis=0)


def soften(s):
    peak = jnp.max(s, axis=0, keepdims=True)
    p = jnp.exp2(s - peak)
    total = jnp.sum(p, axis=0, keepdims=True)
    return p.astype(BF16), peak, total


def pair_context(v, p, inverse, head_width):
    o = t_matmul(v, p)
    count = p.shape[1] // 2
    return [
        o[j * head_width : (j + 1) * head_width, j * count : (j + 1) * count]
        * inverse[:, j * count : (j + 1) * count]
        for j in range(2)
    ]


def pack_levels(level):
    hi = level.astype(BF16)
    rest = level - hi.astype(F32)
    mid = rest.astype(BF16)
    low = (rest - mid.astype(F32)).astype(BF16)
    pad = jnp.zeros((level.shape[0], 128 - 3 * level.shape[1]), BF16)
    return jnp.concatenate([hi, mid, low, pad], axis=1)


def unpack_levels(cols):
    wide = cols.astype(F32)
    return wide[:, :HEADS] + wide[:, HEADS : 2 * HEADS] + wide[:, 2 * HEADS : 3 * HEADS]


def own_kernel(scale, head_width, slabs, slab_ref, *refs):
    x_ref, reg_ref, wq_ref, wk_ref, wv_ref = refs[:5]
    q_ref, kv_ref, reg_kv_ref = refs[5:8]
    part_refs = refs[8 : 8 + slabs]
    rows_ref, ctx_ref, level_ref = refs[8 + slabs :]
    step = pl.program_id(0)
    count, width = x_ref.shape
    regs = reg_ref.shape[0]
    blk, lanes = kv_ref.shape[2:]

    @pl.when(step == 0)
    def _():
        rows_ref[:count] = x_ref[...]
        rows_ref[count:] = reg_ref[...]

    k = matmul(rows_ref[...], wk_ref[...]).astype(BF16)
    q_reg = (matmul(reg_ref[...], wq_ref[...]) * scale).astype(BF16)
    pairs = [(h, h + 1) for h in range(0, lanes // head_width, 2)]

    def score(pair):
        return matmul_t(k[:count], spread_heads(q_reg, head_width, pair))

    s = score(pairs[0])
    v = matmul(rows_ref[...], wv_ref[...]).astype(BF16)
    pending = None
    outs, levels = [], []
    for n, pair in enumerate(pairs):
        following = score(pairs[n + 1]) if n + 1 < len(pairs) else None
        p, peak, total = soften(s)
        at = slice(pair[0] * head_width, (pair[1] + 1) * head_width)
        if n == 0:
            q_ref[...] = (matmul(x_ref[...], wq_ref[...]) * scale).astype(BF16)
        outs += pair_context(v[:count, at], p, 1.0 / total, head_width)
        level = peak + jnp.log2(total)
        levels += [level[:, :regs], level[:, regs:]]
        s = following
    for n in range(kv_ref.shape[1]):
        kv_ref[0, n] = k[n * blk : (n + 1) * blk]
        kv_ref[1, n] = v[n * blk : (n + 1) * blk]
    for n in range(reg_kv_ref.shape[1]):
        kv_at = slice(count + n * blk, count + (n + 1) * blk)
        reg_kv_ref[0, n] = k[kv_at]
        reg_kv_ref[1, n] = v[kv_at]
    out = jnp.concatenate(outs, axis=0).astype(BF16).T
    level_block = jnp.concatenate(levels + [jnp.zeros((8 - len(levels), regs), F32)], axis=0)
    for g in range(width // lanes):

        @pl.when(step == g)
        def _():
            ctx_ref[:, g * lanes : (g + 1) * lanes] = out
            level_ref[g] = level_block

    @pl.when(step == width // lanes - 1)
    def _():
        each = lanes // head_width
        stacked = jnp.concatenate([level_ref[g][:each] for g in range(width // lanes)], axis=0)
        ctx_ref[:, width:] = pack_levels(stacked.T)
        chunk = regs // slabs
        for shift in range(slabs):
            target = lax.rem(slab_ref[0] + shift, slabs)
            part_refs[shift][...] = ctx_ref[pl.ds(pl.multiple_of(target * chunk, chunk), chunk)]


def own_project(slab, rows, registers, w_query, w_key, w_value, slots, blk, head_width, slabs):
    count, width = rows.shape
    regs = registers.shape[0]
    lanes = QUAD * head_width
    chunk = regs // slabs
    tile = pl.BlockSpec((width, lanes), lambda i, s: (0, i))
    outs = pl.pallas_call(
        functools.partial(own_kernel, head_width ** (-0.5) * LOG2E, head_width, slabs),
        grid_spec=pltpu.PrefetchScalarGridSpec(
            num_scalar_prefetch=1,
            grid=(width // lanes,),
            in_specs=[
                pl.BlockSpec((count, width), lambda i, s: (0, 0)),
                pl.BlockSpec((regs, width), lambda i, s: (0, 0)),
                tile,
                tile,
                tile,
            ],
            out_specs=[
                pl.BlockSpec((count, lanes), lambda i, s: (0, i)),
                pl.BlockSpec((2, count // blk, blk, lanes), lambda i, s: (0, 0, 0, i)),
                pl.BlockSpec((2, regs // blk, blk, lanes), lambda i, s: (0, 0, 0, i)),
            ]
            + [pl.BlockSpec((chunk, width + 128), lambda i, s: (0, 0))] * slabs,
            scratch_shapes=[
                pltpu.VMEM((count + regs, width), BF16),
                pltpu.VMEM((regs, width + 128), BF16),
                pltpu.VMEM((width // lanes, 8, regs), F32),
            ],
        ),
        out_shape=[
            jax.ShapeDtypeStruct((count, width), BF16),
            jax.ShapeDtypeStruct((2, slots, blk, width), BF16),
            jax.ShapeDtypeStruct((2, regs // blk, blk, width), BF16),
        ]
        + [jax.ShapeDtypeStruct((chunk, width + 128), BF16)] * slabs,
        compiler_params=params(48),
        cost_estimate=cost(),
        name="own_project",
    )(slab, rows, registers, w_query, w_key, w_value)
    return outs[0], outs[1], outs[2], outs[3:]


def halo_kernel(pieces, deps, *refs):
    xs, wk_ref, wv_ref = refs[:pieces], refs[pieces], refs[pieces + 1]
    kv_ref, _, rows_ref, sems = refs[pieces + 3 + deps :]
    blk = kv_ref.shape[2]

    @pl.when(pl.program_id(0) == 0)
    def _():
        copies, at = [], 0
        for n, x in enumerate(xs):
            copies.append(pltpu.make_async_copy(x, rows_ref.at[pl.ds(at, x.shape[0])], sems.at[n]))
            at += x.shape[0]
        for c in copies:
            c.start()
        for c in copies:
            c.wait()

    for side, w_ref in ((0, wk_ref), (1, wv_ref)):
        out = matmul(rows_ref[...], w_ref[...]).astype(BF16)
        for n in range(kv_ref.shape[1]):
            kv_ref[side, n] = out[n * blk : (n + 1) * blk]


def halo_project(table, pieces, index, w_key, w_value, lanes, deps):
    _, slots, blk, width = table.shape
    pieces = [x.reshape(-1, width) for x in pieces]
    rows = sum(x.shape[0] for x in pieces)
    tile = pl.BlockSpec((width, lanes), lambda i: (0, i))
    return pl.pallas_call(
        functools.partial(halo_kernel, len(pieces), len(deps)),
        grid=(width // lanes,),
        in_specs=[ANY] * len(pieces) + [tile, tile, ANY] + [ANY] * len(deps),
        out_specs=[pl.BlockSpec((2, rows // blk, blk, lanes), lambda i: (0, index, 0, i)), ANY],
        out_shape=[jax.ShapeDtypeStruct(table.shape, BF16), TOKEN],
        scratch_shapes=[pltpu.VMEM((rows, width), BF16), pltpu.SemaphoreType.DMA((len(pieces),))],
        input_output_aliases={len(pieces) + 2: 0},
        compiler_params=params(40),
        cost_estimate=cost(),
        name="halo_project",
    )(*pieces, w_key, w_value, table, *deps)


def window_kernel(head_width, idx_ref, q_ref, *refs):
    kv_refs, (reg_ref, wo_ref) = refs[:LIST], refs[LIST : LIST + 2]
    o_ref, _, ctx_ref = refs[-3:]
    width = q_ref.shape[1]
    lanes = QUAD * head_width
    groups = width // lanes

    def gathered(side, at):
        return jnp.concatenate(
            [r[side, 0, :, at] for r in kv_refs]
            + [reg_ref[side, n, :, at] for n in range(reg_ref.shape[1])],
            axis=0,
        )

    def score(g):
        at = slice(g * lanes, (g + 1) * lanes)
        return matmul_t(gathered(0, at), spread_heads(q_ref[:, at], head_width, range(QUAD)))

    def context(g, p, inverse):
        outs = []
        rows = q_ref.shape[0]
        for h in range(0, QUAD, 2):
            start = g * lanes + h * head_width
            at = slice(h * rows, (h + 2) * rows)
            outs += pair_context(
                gathered(1, slice(start, start + 2 * head_width)), p[:, at], inverse[:, at], head_width
            )
        ctx_ref[:, g * lanes : (g + 1) * lanes] = jnp.concatenate(outs, axis=0).astype(BF16).T

    following, pending = score(0), None
    for g in range(groups):
        s = following
        if g + 1 < groups:
            following = score(g + 1)
        if pending is not None:
            context(*pending)
        p, _, total = soften(s)
        pending = (g, p, 1.0 / total)
    context(*pending)
    o_ref[0] = matmul(ctx_ref[...], wo_ref[...]).astype(BF16)


def window_attend(queries, table, reg_kv, slot_list, block, n, w_out, head_width, previous, deps):
    _, _, blk, width = table.shape
    total = queries.shape[0] // blk

    def list_map(entry):
        return lambda i, idx: (0, idx[block(i) * LIST + entry], 0, 0)

    operands = [slot_list, queries] + [table] * LIST + [reg_kv, w_out]
    in_specs = (
        [pl.BlockSpec((blk, width), lambda i, idx: (block(i), 0))]
        + [pl.BlockSpec((2, 1, blk, width), list_map(e)) for e in range(LIST)]
        + [
            pl.BlockSpec(reg_kv.shape, lambda i, idx: (0, 0, 0, 0)),
            pl.BlockSpec((width, width), lambda i, idx: (0, 0)),
        ]
    )
    aliases = {}
    if previous is not None:
        aliases = {len(operands): 0}
        operands.append(previous)
        in_specs.append(ANY)
    operands += deps
    in_specs += [ANY] * len(deps)
    return pl.pallas_call(
        functools.partial(window_kernel, head_width),
        grid_spec=pltpu.PrefetchScalarGridSpec(
            num_scalar_prefetch=1,
            grid=(n,),
            in_specs=in_specs,
            out_specs=[pl.BlockSpec((1, blk, width), lambda i, idx: (block(i), 0, 0)), ANY],
            scratch_shapes=[pltpu.VMEM((blk, width), BF16)],
        ),
        out_shape=[jax.ShapeDtypeStruct((total, blk, width), BF16), TOKEN],
        input_output_aliases=aliases,
        compiler_params=params(48),
        cost_estimate=cost(),
        name="window_attend",
    )(*operands)


def merged(refs, width):
    levels = [unpack_levels(r[:, width:]) for r in refs]
    top = functools.reduce(jnp.maximum, levels)
    weights = [jnp.exp2(level - top) for level in levels]
    total = functools.reduce(jnp.add, weights)
    inverse = 1.0 / total
    weights = [w * inverse for w in weights]
    rows = refs[0].shape[0]
    head_width = width // HEADS
    lower = lax.broadcasted_iota(jnp.int32, (rows, 2 * head_width), 1) < head_width
    cols = []
    for pair in range(HEADS // 2):
        at = slice(pair * 2 * head_width, (pair + 1) * 2 * head_width)
        mix = jnp.zeros((rows, 2 * head_width), F32)
        for r, w in zip(refs, weights):
            spread = jnp.where(lower, w[:, 2 * pair : 2 * pair + 1], w[:, 2 * pair + 1 : 2 * pair + 2])
            mix = mix + r[:, at].astype(F32) * spread
        cols.append(mix.astype(BF16))
    return jnp.concatenate(cols, axis=1), top + jnp.log2(total)


def vmem_call(body, out_shape, name, operands, deps):
    vmem = pl.BlockSpec(memory_space=pltpu.VMEM)

    def wrapped(*refs):
        body(*refs[: len(operands)], *refs[len(operands) + len(deps) :])

    return pl.pallas_call(
        wrapped,
        in_specs=[vmem] * len(operands) + [ANY] * len(deps),
        out_specs=vmem,
        out_shape=out_shape,
        compiler_params=params(16),
        cost_estimate=cost(),
        name=name,
    )(*operands, *deps)


def shift_all(parts, axis):
    n = lax.axis_size(axis)
    return [parts[0]] + [
        lax.ppermute(parts[j], axis, [(i, (i + j) % n) for i in range(n)]) for j in range(1, n)
    ]


def merge_slab(parts, deps):
    rows, wide = parts[0].shape
    width = wide - 128

    def body(*refs):
        mix, level = merged(refs[:-1], width)
        refs[-1][:, :width] = mix
        refs[-1][:, width:] = pack_levels(level)

    return vmem_call(body, jax.ShapeDtypeStruct((rows, wide), BF16), "register_merge", parts, deps)


def merge_phase(parts, w_out, deps):
    rows, wide = parts[0].shape
    width = wide - 128

    def body(*refs):
        mix, _ = merged(refs[:-2], width)
        refs[-1][...] = matmul(mix, refs[-2][...]).astype(BF16)

    return vmem_call(
        body, jax.ShapeDtypeStruct((rows, width), BF16), "register_out", [*parts, w_out], deps
    )


def assemble(slab, parts, deps):
    rows, width = parts[0].shape
    slabs = len(parts)

    def body(slab_ref, *refs):
        out_ref = refs[-1]
        for j in range(slabs):
            source = lax.rem(slab_ref[0] + slabs - j, slabs)
            out_ref[pl.ds(pl.multiple_of(source * rows, rows), rows)] = refs[j][...]

    vmem = pl.BlockSpec(memory_space=pltpu.VMEM)
    return pl.pallas_call(
        body,
        in_specs=[pl.BlockSpec(memory_space=pltpu.SMEM)] + [vmem] * slabs + [ANY] * len(deps),
        out_specs=vmem,
        out_shape=jax.ShapeDtypeStruct((rows * slabs, width), BF16),
        compiler_params=params(16),
        cost_estimate=cost(),
        name="register_assemble",
    )(slab, *parts, *deps)


def shards(normed, block_list, registers, w_query, w_key, w_value, w_out):
    own_phases, slab_blocks, blk, width = normed.shape
    head_width = width // HEADS
    lanes = QUAD * head_width
    phases, slabs = lax.axis_size("phase"), lax.axis_size("slab")
    own = own_phases * slab_blocks
    slab = lax.axis_index("slab").astype(jnp.int32)

    def around(x, axis, step, closed):
        n = lax.axis_size(axis)
        return lax.ppermute(
            x, axis, [(i, (i + step) % n) for i in range(n) if closed or 0 <= i + step < n]
        )

    before = around(normed[-1], "phase", 1, True)
    after = around(normed[0], "phase", -1, True)
    left = around(normed[:, -1], "slab", 1, False)
    right = around(normed[:, 0], "slab", -1, False)
    corner_left = around(jnp.stack([before[-1], after[-1]]), "slab", 1, False)
    corner_right = around(jnp.stack([before[0], after[0]]), "slab", -1, False)

    at_left = own
    at_right = at_left + own_phases
    at_before = at_right + own_phases
    at_after = at_before + slab_blocks
    at_corner = at_after + slab_blocks
    slots = at_corner + 4
    assert own == at_before - at_left == slots - at_before

    total_phases, depth_blocks = own_phases * phases, slab_blocks * slabs
    p = (block_list // depth_blocks - lax.axis_index("phase") * own_phases + 1) % total_phases - 1
    z = block_list % depth_blocks - slab * slab_blocks
    is_left, is_right = z < 0, z >= slab_blocks
    is_before, is_after = p < 0, p >= own_phases
    inner = jnp.where(is_left, at_left + p, jnp.where(is_right, at_right + p, p * slab_blocks + z))
    outer = jnp.where(
        is_left | is_right,
        at_corner + jnp.where(is_right, 2, 0) + jnp.where(is_after, 1, 0),
        jnp.where(is_after, at_after, at_before) + z,
    )
    slot_list = jnp.where(is_before | is_after, outer, inner).astype(jnp.int32).reshape(-1)

    queries, table, reg_kv, parts = own_project(
        slab.reshape(1),
        normed.reshape(-1, width),
        registers,
        w_query,
        w_key,
        w_value,
        slots,
        blk,
        head_width,
        slabs,
    )
    parts = shift_all(parts, "slab")
    table, _ = halo_project(table, [left, right], 1, w_key, w_value, lanes, [])
    middle = own - 2 * slab_blocks
    mixed, token = window_attend(
        queries,
        table,
        reg_kv,
        slot_list,
        lambda i: i + slab_blocks,
        middle,
        w_out,
        head_width,
        None,
        [before, after],
    )
    one = merge_slab(parts, [token])
    ones = shift_all([one] * phases, "phase")
    table, token = halo_project(
        table, [before, after, corner_left, corner_right], 2, w_key, w_value, lanes, [one]
    )
    share = merge_phase(ones, w_out, [token])
    shares = shift_all([share] * slabs, "slab")
    mixed, token = window_attend(
        queries,
        table,
        reg_kv,
        slot_list,
        lambda i: i + jnp.where(i >= slab_blocks, middle, 0),
        own - middle,
        w_out,
        head_width,
        mixed,
        [share],
    )
    register_out = assemble(slab.reshape(1), shares, [token])
    return mixed.reshape(own_phases, slab_blocks, blk, width), register_out


def solution(mesh):
    placed = (P("phase", "slab", None, None), P("phase", "slab", None), P(), P(), P(), P(), P())
    return jax.shard_map(
        shards,
        mesh=mesh,
        in_specs=placed,
        out_specs=(P("phase", "slab", None, None), P()),
        check_vma=False,
    )
```

```python
import functools

import jax
import jax.numpy as jnp
from jax import lax
from jax.experimental import pallas as pl
from jax.experimental.pallas import tpu as pltpu
from jax.sharding import PartitionSpec as P

HEADS = 16
LIST = 5
QUAD = 4
LOG2E = 1.4426950408889634
F32, BF16 = jnp.float32, jnp.bfloat16
ANY = pl.BlockSpec(memory_space=pl.ANY)
VMEM = pl.BlockSpec(memory_space=pltpu.VMEM)
TOKEN = jax.ShapeDtypeStruct((8, 128), jnp.float32)


def params(mib):
    return pltpu.CompilerParams(vmem_limit_bytes=mib << 20)


def cost():
    return pl.CostEstimate(flops=1 << 20, bytes_accessed=1 << 16, transcendentals=0)


def matmul(a, b):
    return jnp.dot(a, b, preferred_element_type=F32)


def matmul_t(a, b):
    return lax.dot_general(a, b, (((1,), (1,)), ((), ())), preferred_element_type=F32)


def t_matmul(a, b):
    return lax.dot_general(a, b, (((0,), (0,)), ((), ())), preferred_element_type=F32)


def spread_heads(q, head_width, heads):
    lane = lax.broadcasted_iota(jnp.int32, q.shape, 1) // head_width
    return jnp.concatenate([jnp.where(lane == h, q, jnp.zeros_like(q)) for h in heads], axis=0)


def soften(s):
    peak = jnp.max(s, axis=0, keepdims=True)
    p = jnp.exp2(s - peak)
    total = jnp.sum(p, axis=0, keepdims=True)
    return p.astype(BF16), peak, total


def pair_context(v, p, inverse, head_width):
    o = t_matmul(v, p)
    count = p.shape[1] // 2
    return [
        o[j * head_width : (j + 1) * head_width, j * count : (j + 1) * count]
        * inverse[:, j * count : (j + 1) * count]
        for j in range(2)
    ]


def pack_levels(level):
    hi = level.astype(BF16)
    rest = level - hi.astype(F32)
    mid = rest.astype(BF16)
    low = (rest - mid.astype(F32)).astype(BF16)
    pad = jnp.zeros((level.shape[0], 128 - 3 * level.shape[1]), BF16)
    return jnp.concatenate([hi, mid, low, pad], axis=1)


def unpack_levels(cols):
    wide = cols.astype(F32)
    return wide[:, :HEADS] + wide[:, HEADS : 2 * HEADS] + wide[:, 2 * HEADS : 3 * HEADS]


def own_kernel(scale, head_width, core_ref, *refs):
    x_ref, reg_ref, wq_ref, wk_ref, wv_ref = refs[:5]
    q_ref, kv_ref, reg_kv_ref, keep_ref, send_ref = refs[5:10]
    rows_ref, ctx_ref, level_ref = refs[10:]
    step = pl.program_id(0)
    count, width = x_ref.shape
    regs = reg_ref.shape[0]
    blk, lanes = kv_ref.shape[2:]
    each = lanes // head_width

    @pl.when(step == 0)
    def _():
        rows_ref[:count] = x_ref[...]
        rows_ref[count:] = reg_ref[...]

    tile = pl.ds(pl.multiple_of(step * lanes, lanes), lanes)
    k = matmul(rows_ref[...], wk_ref[...]).astype(BF16)
    q_reg = (matmul(reg_ref[...], wq_ref[...]) * scale).astype(BF16)
    pairs = [(h, h + 1) for h in range(0, each, 2)]

    def score(pair):
        quad = pair[0] // QUAD * QUAD
        at = slice(quad * head_width, (quad + QUAD) * head_width)
        return matmul_t(
            k[:count, at], spread_heads(q_reg[:, at], head_width, [h - quad for h in pair])
        )

    outs, levels = [], []

    def context(pair, p, peak, total):
        at = slice(pair[0] * head_width, (pair[1] + 1) * head_width)
        outs.extend(pair_context(v[:count, at], p, 1.0 / total, head_width))
        level = peak + jnp.log2(total)
        levels.extend([level[:, :regs], level[:, regs:]])

    following, pending = score(pairs[0]), None
    v = matmul(rows_ref[...], wv_ref[...]).astype(BF16)
    for n, pair in enumerate(pairs):
        s = following
        if n + 1 < len(pairs):
            following = score(pairs[n + 1])
        else:
            q_ref[...] = (matmul(x_ref[...], wq_ref[...]) * scale).astype(BF16)
        if pending is not None:
            context(*pending)
        pending = (pair, *soften(s))
    context(*pending)
    for n in range(kv_ref.shape[1]):
        kv_ref[0, n] = k[n * blk : (n + 1) * blk]
        kv_ref[1, n] = v[n * blk : (n + 1) * blk]
    for n in range(reg_kv_ref.shape[1]):
        kv_at = slice(count + n * blk, count + (n + 1) * blk)
        reg_kv_ref[0, n] = k[kv_at]
        reg_kv_ref[1, n] = v[kv_at]
    ctx_ref[:, tile] = jnp.concatenate(outs, axis=0).astype(BF16).T
    level_ref[step] = jnp.concatenate(levels, axis=0)

    @pl.when(step == width // lanes - 1)
    def _():
        stacked = jnp.concatenate([level_ref[g] for g in range(width // lanes)], axis=0)
        ctx_ref[:, width:] = pack_levels(stacked.T)
        half = regs // 2
        core = core_ref[0]
        keep_ref[...] = ctx_ref[pl.ds(pl.multiple_of(core * half, half), half)]
        send_ref[...] = ctx_ref[pl.ds(pl.multiple_of((1 - core) * half, half), half)]


def own_project(core, rows, registers, w_query, w_key, w_value, slots, blk, head_width, lanes):
    count, width = rows.shape
    regs = registers.shape[0]
    half = jax.ShapeDtypeStruct((regs // 2, width + 128), BF16)
    return pl.pallas_call(
        functools.partial(own_kernel, head_width ** (-0.5) * LOG2E, head_width),
        grid_spec=pltpu.PrefetchScalarGridSpec(
            num_scalar_prefetch=1,
            grid=(width // lanes,),
            in_specs=[pl.BlockSpec((count, width), lambda i, s: (0, 0)), pl.BlockSpec((regs, width), lambda i, s: (0, 0))]
            + [pl.BlockSpec((width, lanes), lambda i, s: (0, i))] * 3,
            out_specs=[
                pl.BlockSpec((count, lanes), lambda i, s: (0, i)),
                pl.BlockSpec((2, count // blk, blk, lanes), lambda i, s: (0, 0, 0, i)),
                pl.BlockSpec((2, regs // blk, blk, lanes), lambda i, s: (0, 0, 0, i)),
                pl.BlockSpec(half.shape, lambda i, s: (0, 0)),
                pl.BlockSpec(half.shape, lambda i, s: (0, 0)),
            ],
            scratch_shapes=[
                pltpu.VMEM((count + regs, width), BF16),
                pltpu.VMEM((regs, width + 128), BF16),
                pltpu.VMEM((width // lanes, lanes // head_width, regs), F32),
            ],
        ),
        out_shape=[
            jax.ShapeDtypeStruct((count, width), BF16),
            pltpu.HBM((2, slots, blk, width), BF16),
            jax.ShapeDtypeStruct((2, regs // blk, blk, width), BF16),
            half,
            half,
        ],
        compiler_params=params(52),
        cost_estimate=cost(),
        name="own_project",
    )(core, rows, registers, w_query, w_key, w_value)


def halo_kernel(pieces, deps, *refs):
    xs, wk_ref, wv_ref = refs[:pieces], refs[pieces], refs[pieces + 1]
    kv_ref, _, rows_ref, sems = refs[pieces + 3 + deps :]
    blk = kv_ref.shape[2]

    @pl.when(pl.program_id(0) == 0)
    def _():
        copies, at = [], 0
        for n, x in enumerate(xs):
            copies.append(pltpu.make_async_copy(x, rows_ref.at[pl.ds(at, x.shape[0])], sems.at[n]))
            at += x.shape[0]
        for c in copies:
            c.start()
        for c in copies:
            c.wait()

    for side, w_ref in ((0, wk_ref), (1, wv_ref)):
        out = matmul(rows_ref[...], w_ref[...]).astype(BF16)
        for n in range(kv_ref.shape[1]):
            kv_ref[side, n] = out[n * blk : (n + 1) * blk]


def halo_project(table, pieces, index, w_key, w_value, lanes, deps):
    _, slots, blk, width = table.shape
    pieces = [x.reshape(-1, width) for x in pieces]
    rows = sum(x.shape[0] for x in pieces)
    tile = pl.BlockSpec((width, lanes), lambda i: (0, i))
    return pl.pallas_call(
        functools.partial(halo_kernel, len(pieces), len(deps)),
        grid=(width // lanes,),
        in_specs=[ANY] * len(pieces) + [tile, tile, ANY] + [ANY] * len(deps),
        out_specs=[pl.BlockSpec((2, rows // blk, blk, lanes), lambda i: (0, index, 0, i)), ANY],
        out_shape=[pltpu.HBM(table.shape, BF16), TOKEN],
        scratch_shapes=[pltpu.VMEM((rows, width), BF16), pltpu.SemaphoreType.DMA((len(pieces),))],
        input_output_aliases={len(pieces) + 2: 0},
        compiler_params=params(52),
        cost_estimate=cost(),
        name="halo_project",
    )(*pieces, w_key, w_value, table, *deps)


def window_kernel(head_width, idx_ref, q_ref, *refs):
    kv_refs, (reg_ref, wo_ref) = refs[:LIST], refs[LIST : LIST + 2]
    o_ref, _, ctx_ref = refs[-3:]
    width = q_ref.shape[1]
    lanes = QUAD * head_width
    groups = width // lanes

    def gathered(side, at):
        return jnp.concatenate(
            [r[side, 0, :, at] for r in kv_refs]
            + [reg_ref[side, n, :, at] for n in range(reg_ref.shape[1])],
            axis=0,
        )

    def score(g):
        at = slice(g * lanes, (g + 1) * lanes)
        return matmul_t(gathered(0, at), spread_heads(q_ref[:, at], head_width, range(QUAD)))

    def context(g, p, inverse):
        outs = []
        rows = q_ref.shape[0]
        for h in range(0, QUAD, 2):
            start = g * lanes + h * head_width
            at = slice(h * rows, (h + 2) * rows)
            outs += pair_context(
                gathered(1, slice(start, start + 2 * head_width)), p[:, at], inverse[:, at], head_width
            )
        ctx_ref[:, g * lanes : (g + 1) * lanes] = jnp.concatenate(outs, axis=0).astype(BF16).T

    following, pending = score(0), None
    for g in range(groups):
        s = following
        if g + 1 < groups:
            following = score(g + 1)
        if pending is not None:
            context(*pending)
        p, _, total = soften(s)
        pending = (g, p, 1.0 / total)
    context(*pending)
    o_ref[0] = matmul(ctx_ref[...], wo_ref[...]).astype(BF16)


def window_attend(queries, table, reg_kv, slot_list, block, n, w_out, head_width, previous, deps):
    _, _, blk, width = table.shape
    total = queries.shape[0] // blk

    def list_map(entry):
        return lambda i, idx: (0, idx[block(i) * LIST + entry], 0, 0)

    operands = [slot_list, queries] + [table] * LIST + [reg_kv, w_out]
    in_specs = (
        [pl.BlockSpec((blk, width), lambda i, idx: (block(i), 0))]
        + [pl.BlockSpec((2, 1, blk, width), list_map(e)) for e in range(LIST)]
        + [VMEM, VMEM]
    )
    aliases = {}
    if previous is not None:
        aliases = {len(operands): 0}
        operands.append(previous)
        in_specs.append(ANY)
    operands += deps
    in_specs += [ANY] * len(deps)
    return pl.pallas_call(
        functools.partial(window_kernel, head_width),
        grid_spec=pltpu.PrefetchScalarGridSpec(
            num_scalar_prefetch=1,
            grid=(n,),
            in_specs=in_specs,
            out_specs=[pl.BlockSpec((1, blk, width), lambda i, idx: (block(i), 0, 0)), ANY],
            scratch_shapes=[pltpu.VMEM((blk, width), BF16)],
        ),
        out_shape=[jax.ShapeDtypeStruct((total, blk, width), BF16), TOKEN],
        input_output_aliases=aliases,
        compiler_params=params(52),
        cost_estimate=cost(),
        name="window_attend",
    )(*operands)


def merged(flag, mine_ref, got_ref, width):
    first = jnp.where(flag == 0, mine_ref[...], got_ref[...])
    second = jnp.where(flag == 0, got_ref[...], mine_ref[...])
    levels = [unpack_levels(x[:, width:]) for x in (first, second)]
    top = jnp.maximum(*levels)
    weights = [jnp.exp2(level - top) for level in levels]
    total = weights[0] + weights[1]
    weights = [w / total for w in weights]
    rows = first.shape[0]
    head_width = width // HEADS
    lower = lax.broadcasted_iota(jnp.int32, (rows, 2 * head_width), 1) < head_width
    cols = []
    for pair in range(HEADS // 2):
        at = slice(pair * 2 * head_width, (pair + 1) * 2 * head_width)

        def spread(w):
            return jnp.where(lower, w[:, 2 * pair : 2 * pair + 1], w[:, 2 * pair + 1 : 2 * pair + 2])

        mix = first[:, at].astype(F32) * spread(weights[0]) + second[:, at].astype(F32) * spread(weights[1])
        cols.append(mix.astype(BF16))
    return jnp.concatenate(cols, axis=1), top + jnp.log2(total)


def small_call(body, out_shape, name, flag, operands, deps):
    def wrapped(*refs):
        body(*refs[: 1 + len(operands)], refs[-2])

    return pl.pallas_call(
        wrapped,
        in_specs=[pl.BlockSpec(memory_space=pltpu.SMEM)] + [VMEM] * len(operands) + [ANY] * len(deps),
        out_specs=[VMEM, ANY],
        out_shape=[out_shape, TOKEN],
        compiler_params=params(16),
        cost_estimate=cost(),
        name=name,
    )(flag, *operands, *deps)


def register_rounds(slab, keep, send, w_out):
    half, wide = keep.shape
    width = wide - 128
    slabs, phases = lax.axis_size("slab"), lax.axis_size("phase")
    phase = lax.axis_index("phase").astype(jnp.int32)
    turns = [("slab", slab, b) for b in range(slabs.bit_length() - 1)]
    turns += [("phase", phase, b) for b in range(phases.bit_length() - 1)]

    def swap(x, axis, bit):
        return lax.ppermute(x, axis, [(i, i ^ (1 << bit)) for i in range(lax.axis_size(axis))])

    def merge_body(flag_ref, mine_ref, got_ref, out_ref):
        mix, level = merged(flag_ref[0], mine_ref, got_ref, width)
        out_ref[:, :width] = mix
        out_ref[:, width:] = pack_levels(level)

    def last_body(flag_ref, mine_ref, got_ref, w_ref, out_ref):
        mix, _ = merged(flag_ref[0], mine_ref, got_ref, width)
        out_ref[...] = matmul(mix, w_ref[...]).astype(BF16)

    def join_body(core_ref, mine_ref, got_ref, out_ref):
        core = core_ref[0]
        out_ref[pl.ds(pl.multiple_of(core * half, half), half)] = mine_ref[...]
        out_ref[pl.ds(pl.multiple_of((1 - core) * half, half), half)] = got_ref[...]

    mine, token = keep, None
    for n, (axis, place, bit) in enumerate(turns):
        got = swap(send if n == 0 else mine, axis, bit)
        token = yield token
        flag = ((place >> bit) & 1).reshape(1)
        if n + 1 < len(turns):
            shape = jax.ShapeDtypeStruct((half, wide), BF16)
            mine, token = small_call(merge_body, shape, "register_merge", flag, [mine, got], [token])
        else:
            shape = jax.ShapeDtypeStruct((half, width), BF16)
            mine, token = small_call(last_body, shape, "register_out", flag, [mine, got, w_out], [token])
    got = swap(mine, "slab", 0)
    token = yield token
    shape = jax.ShapeDtypeStruct((2 * half, width), BF16)
    out, _ = small_call(join_body, shape, "register_join", (slab & 1).reshape(1), [mine, got], [token])
    yield out


def shards(normed, block_list, registers, w_query, w_key, w_value, w_out):
    own_phases, slab_blocks, blk, width = normed.shape
    head_width = width // HEADS
    lanes = QUAD * head_width
    phases, slabs = lax.axis_size("phase"), lax.axis_size("slab")
    own = own_phases * slab_blocks
    slab = lax.axis_index("slab").astype(jnp.int32)

    def around(x, axis, step, closed):
        n = lax.axis_size(axis)
        return lax.ppermute(
            x, axis, [(i, (i + step) % n) for i in range(n) if closed or 0 <= i + step < n]
        )

    before = around(normed[-1], "phase", 1, True)
    after = around(normed[0], "phase", -1, True)
    left = around(normed[:, -1], "slab", 1, False)
    right = around(normed[:, 0], "slab", -1, False)
    corner_left = around(jnp.stack([before[-1], after[-1]]), "slab", 1, False)
    corner_right = around(jnp.stack([before[0], after[0]]), "slab", -1, False)

    at_left = own
    at_right = at_left + own_phases
    at_before = at_right + own_phases
    at_after = at_before + slab_blocks
    at_corner = at_after + slab_blocks
    slots = at_corner + 4
    assert own == at_before - at_left == slots - at_before

    total_phases, depth_blocks = own_phases * phases, slab_blocks * slabs
    p = (block_list // depth_blocks - lax.axis_index("phase") * own_phases + 1) % total_phases - 1
    z = block_list % depth_blocks - slab * slab_blocks
    is_left, is_right = z < 0, z >= slab_blocks
    is_before, is_after = p < 0, p >= own_phases
    inner = jnp.where(is_left, at_left + p, jnp.where(is_right, at_right + p, p * slab_blocks + z))
    outer = jnp.where(
        is_left | is_right,
        at_corner + jnp.where(is_right, 2, 0) + jnp.where(is_after, 1, 0),
        jnp.where(is_after, at_after, at_before) + z,
    )
    slot_list = jnp.where(is_before | is_after, outer, inner).astype(jnp.int32).reshape(-1)

    queries, table, reg_kv, keep, send = own_project(
        (slab & 1).reshape(1),
        normed.reshape(-1, width),
        registers,
        w_query,
        w_key,
        w_value,
        slots,
        blk,
        head_width,
        2 * lanes,
    )
    rounds = register_rounds(slab, keep, send, w_out)
    next(rounds)
    count = (slabs * phases).bit_length()

    def window(table, start, mixed, deps):
        return window_attend(
            queries,
            table,
            reg_kv,
            slot_list,
            lambda i: start + i,
            slab_blocks,
            w_out,
            head_width,
            mixed,
            deps,
        )

    table, token = halo_project(table, [left, right], 1, w_key, w_value, 2 * lanes, [])
    token = rounds.send(token)
    mixed, starts = None, [n * slab_blocks for n in range(own_phases)]
    for n, start in enumerate(starts[1:-1]):
        deps = [token, before, after] if n == 0 else [token]
        mixed, token = window(table, start, mixed, deps)
        token = rounds.send(token)
    table, token = halo_project(
        table, [before, after, corner_left, corner_right], 2, w_key, w_value, 2 * lanes, [token]
    )
    token = rounds.send(token)
    mixed, token = window(table, starts[0], mixed, [token])
    for _ in range(count - own_phases - 1):
        token = rounds.send(token)
    mixed, token = window(table, starts[-1], mixed, [token])
    register_out = rounds.send(token)
    return mixed.reshape(own_phases, slab_blocks, blk, width), register_out


def solution(mesh):
    placed = (P("phase", "slab", None, None), P("phase", "slab", None), P(), P(), P(), P(), P())
    return jax.shard_map(
        shards,
        mesh=mesh,
        in_specs=placed,
        out_specs=(P("phase", "slab", None, None), P()),
        check_vma=False,
    )
```

```python
import functools

import jax
import jax.numpy as jnp
from jax import lax
from jax.experimental import pallas as pl
from jax.experimental.pallas import tpu as pltpu
from jax.sharding import PartitionSpec as P

HEADS = 16
LIST = 5
QUAD = 4
LOG2E = 1.4426950408889634
F32, BF16 = jnp.float32, jnp.bfloat16
ANY = pl.BlockSpec(memory_space=pl.ANY)
VMEM = pl.BlockSpec(memory_space=pltpu.VMEM)
TOKEN = jax.ShapeDtypeStruct((8, 128), jnp.float32)


def params(mib):
    return pltpu.CompilerParams(vmem_limit_bytes=mib << 20)


def cost():
    return pl.CostEstimate(flops=1 << 20, bytes_accessed=1 << 16, transcendentals=0)


def matmul(a, b):
    return jnp.dot(a, b, preferred_element_type=F32)


def matmul_t(a, b):
    return lax.dot_general(a, b, (((1,), (1,)), ((), ())), preferred_element_type=F32)


def t_matmul(a, b):
    return lax.dot_general(a, b, (((0,), (0,)), ((), ())), preferred_element_type=F32)


def spread_heads(q, head_width, heads):
    lane = lax.broadcasted_iota(jnp.int32, q.shape, 1) // head_width
    return jnp.concatenate([jnp.where(lane == h, q, jnp.zeros_like(q)) for h in heads], axis=0)


def soften(s):
    peak = jnp.max(s, axis=0, keepdims=True)
    p = jnp.exp2(s - peak)
    total = jnp.sum(p, axis=0, keepdims=True)
    return p.astype(BF16), peak, total


def pair_context(v, p, inverse, head_width):
    o = t_matmul(v, p)
    count = p.shape[1] // 2
    return [
        o[j * head_width : (j + 1) * head_width, j * count : (j + 1) * count]
        * inverse[:, j * count : (j + 1) * count]
        for j in range(2)
    ]


def pack_levels(level):
    hi = level.astype(BF16)
    rest = level - hi.astype(F32)
    mid = rest.astype(BF16)
    low = (rest - mid.astype(F32)).astype(BF16)
    pad = jnp.zeros((level.shape[0], 128 - 3 * level.shape[1]), BF16)
    return jnp.concatenate([hi, mid, low, pad], axis=1)


def unpack_levels(cols):
    wide = cols.astype(F32)
    return wide[:, :HEADS] + wide[:, HEADS : 2 * HEADS] + wide[:, 2 * HEADS : 3 * HEADS]


def own_kernel(scale, head_width, core_ref, *refs):
    x_ref, reg_ref, wq_ref, wk_ref, wv_ref = refs[:5]
    kv_ref, reg_kv_ref, keep_ref, send_ref, rows_ref, ctx_ref, level_ref = refs[-7:]
    step = pl.program_id(0)
    count, width = x_ref.shape
    regs = reg_ref.shape[0]
    blk, lanes = kv_ref.shape[2:]
    each = lanes // head_width

    @pl.when(step == 0)
    def _():
        rows_ref[:count] = x_ref[...]
        rows_ref[count:] = reg_ref[...]

    tile = pl.ds(pl.multiple_of(step * lanes, lanes), lanes)
    k = matmul(rows_ref[...], wk_ref[...]).astype(BF16)
    q_reg = (matmul(reg_ref[...], wq_ref[...]) * scale).astype(BF16)
    pairs = [(h, h + 1) for h in range(0, each, 2)]

    def score(pair):
        quad = pair[0] // QUAD * QUAD
        at = slice(quad * head_width, (quad + QUAD) * head_width)
        return matmul_t(
            k[:count, at], spread_heads(q_reg[:, at], head_width, [h - quad for h in pair])
        )

    outs, levels = [], []

    def context(pair, p, peak, total):
        at = slice(pair[0] * head_width, (pair[1] + 1) * head_width)
        outs.extend(pair_context(v[:count, at], p, 1.0 / total, head_width))
        level = peak + jnp.log2(total)
        levels.extend([level[:, :regs], level[:, regs:]])

    following, pending = score(pairs[0]), None
    v = matmul(rows_ref[...], wv_ref[...]).astype(BF16)
    for n, pair in enumerate(pairs):
        s = following
        if n + 1 < len(pairs):
            following = score(pairs[n + 1])
        if pending is not None:
            context(*pending)
        pending = (pair, *soften(s))
    context(*pending)
    for n in range(kv_ref.shape[1]):
        kv_ref[0, n] = k[n * blk : (n + 1) * blk]
        kv_ref[1, n] = v[n * blk : (n + 1) * blk]
    for n in range(reg_kv_ref.shape[1]):
        kv_at = slice(count + n * blk, count + (n + 1) * blk)
        reg_kv_ref[0, n] = k[kv_at]
        reg_kv_ref[1, n] = v[kv_at]
    ctx_ref[:, tile] = jnp.concatenate(outs, axis=0).astype(BF16).T
    level_ref[step] = jnp.concatenate(levels, axis=0)

    @pl.when(step == width // lanes - 1)
    def _():
        stacked = jnp.concatenate([level_ref[g] for g in range(width // lanes)], axis=0)
        ctx_ref[:, width:] = pack_levels(stacked.T)
        half = regs // 2
        core = core_ref[0]
        keep_ref[...] = ctx_ref[pl.ds(pl.multiple_of(core * half, half), half)]
        send_ref[...] = ctx_ref[pl.ds(pl.multiple_of((1 - core) * half, half), half)]


def own_project(core, rows, registers, w_query, w_key, w_value, slots, blk, head_width, lanes, scale, deps):
    count, width = rows.shape
    regs = registers.shape[0]
    half = jax.ShapeDtypeStruct((regs // 2, width + 128), BF16)
    return pl.pallas_call(
        functools.partial(own_kernel, scale, head_width),
        grid_spec=pltpu.PrefetchScalarGridSpec(
            num_scalar_prefetch=1,
            grid=(width // lanes,),
            in_specs=[pl.BlockSpec((count, width), lambda i, s: (0, 0)), pl.BlockSpec((regs, width), lambda i, s: (0, 0))]
            + [pl.BlockSpec((width, lanes), lambda i, s: (0, i))] * 3
            + [ANY] * len(deps),
            out_specs=[
                pl.BlockSpec((2, count // blk, blk, lanes), lambda i, s: (0, 0, 0, i)),
                pl.BlockSpec((2, regs // blk, blk, lanes), lambda i, s: (0, 0, 0, i)),
                pl.BlockSpec(half.shape, lambda i, s: (0, 0)),
                pl.BlockSpec(half.shape, lambda i, s: (0, 0)),
            ],
            scratch_shapes=[
                pltpu.VMEM((count + regs, width), BF16),
                pltpu.VMEM((regs, width + 128), BF16),
                pltpu.VMEM((width // lanes, lanes // head_width, regs), F32),
            ],
        ),
        out_shape=[
            pltpu.HBM((2, slots, blk, width), BF16),
            jax.ShapeDtypeStruct((2, regs // blk, blk, width), BF16),
            half,
            half,
        ],
        compiler_params=params(52),
        cost_estimate=cost(),
        name="own_project",
    )(core, rows, registers, w_query, w_key, w_value, *deps)


def attend_kernel(head_width, start, loaded, pieces, skipped, idx_ref, *refs):
    refs = iter(refs)

    def take(count):
        return [next(refs) for _ in range(count)]

    q_ref, reg_ref = take(2)
    xs, w_refs = take(pieces), take(2 if pieces else 0)
    table_ref, wo_ref = take(2)
    take(skipped)
    (new_table_ref,) = take(1) if pieces else (None,)
    o_ref, _ = take(2)
    tabs = take(2)
    ctx_ref, wo_scratch, in_sems, wo_sem = take(4)
    if pieces:
        rows_ref, x_sems, out_sems = take(3)
    step, last = pl.program_id(0), pl.num_programs(0) - 1
    buf = lax.rem(step, 2)
    slots, blk, lanes = tabs[0].shape[1:]
    blocks = o_ref.shape[0]

    def columns(g):
        return pl.ds(pl.multiple_of(g * lanes, lanes), lanes)

    def bring(g, b):
        return [
            pltpu.make_async_copy(
                table_ref.at[side, pl.ds(0, loaded), :, columns(g)],
                tabs[side].at[b, pl.ds(0, loaded)],
                in_sems.at[side, b],
            )
            for side in range(2)
        ]

    def give(g, b):
        return [
            pltpu.make_async_copy(
                tabs[side].at[b, pl.ds(loaded, slots - loaded)],
                new_table_ref.at[side, pl.ds(loaded, slots - loaded), :, columns(g)],
                out_sems.at[side, b],
            )
            for side in range(2)
        ]

    def output_weight():
        return pltpu.make_async_copy(wo_ref, wo_scratch, wo_sem.at[0])

    @pl.when(step == 0)
    def _():
        copies, at = [], 0
        for n, x in enumerate(xs):
            copies.append(pltpu.make_async_copy(x, rows_ref.at[pl.ds(at, x.shape[0])], x_sems.at[n]))
            at += x.shape[0]
        for c in copies + bring(0, 0):
            c.start()
        output_weight().start()
        for c in copies:
            c.wait()

    @pl.when(step < last)
    def _():
        for c in bring(step + 1, 1 - buf):
            c.start()

    if pieces:

        @pl.when(step >= 2)
        def _():
            for c in give(step - 2, buf):
                c.wait()

    def project(side):
        if pieces:
            new = matmul(rows_ref[...], w_refs[side][...]).astype(BF16)
            for n in range(slots - loaded):
                tabs[side][buf, loaded + n] = new[n * blk : (n + 1) * blk]

    project(0)
    for c in bring(step, buf):
        c.wait()

    def gathered(side, block, at):
        listed = [idx_ref[(start + block) * LIST + e] for e in range(LIST)]
        return jnp.concatenate(
            [tabs[side][buf, slot, :, at] for slot in listed]
            + [reg_ref[side, n, :, at] for n in range(reg_ref.shape[1])],
            axis=0,
        )

    everything = slice(0, lanes)

    def score(block):
        q = q_ref[block * blk : (block + 1) * blk]
        return matmul_t(gathered(0, block, everything), spread_heads(q, head_width, range(QUAD)))

    def context(block, p, inverse):
        outs = []
        for h in range(0, QUAD, 2):
            at = slice(h * blk, (h + 2) * blk)
            v = gathered(1, block, slice(h * head_width, (h + 2) * head_width))
            outs += pair_context(v, p[:, at], inverse[:, at], head_width)
        ctx_ref[block * blk : (block + 1) * blk, columns(step)] = (
            jnp.concatenate(outs, axis=0).astype(BF16).T
        )

    following, pending = score(0), None
    project(1)
    for block in range(blocks):
        s = following
        if block + 1 < blocks:
            following = score(block + 1)
        if pending is not None:
            context(*pending)
        p, _, total = soften(s)
        pending = (block, p, 1.0 / total)
    context(*pending)
    if pieces:
        for c in give(step, buf):
            c.start()

    @pl.when(step == last)
    def _():
        output_weight().wait()
        out = matmul(ctx_ref[...], wo_scratch[...]).astype(BF16)
        for block in range(blocks):
            o_ref[block] = out[block * blk : (block + 1) * blk]
        if pieces:
            for c in give(step - 1, 1 - buf) + give(step, buf):
                c.wait()


def attend(
    queries, table, reg_kv, slot_list, start, blocks, loaded, pieces, w_key, w_value, w_out, head_width, previous, deps
):
    _, all_slots, blk, width = table.shape
    lanes = QUAD * head_width
    rows = blocks * blk
    pieces = [x.reshape(-1, width) for x in pieces]
    new_rows = sum(x.shape[0] for x in pieces)
    slots = loaded + new_rows // blk
    assert start % blocks == 0 and width // lanes >= 2
    operands = [slot_list, queries, reg_kv, *pieces]
    in_specs = [
        pl.BlockSpec((rows, lanes), lambda i, idx: (start // blocks, i)),
        pl.BlockSpec((*reg_kv.shape[:3], lanes), lambda i, idx: (0, 0, 0, i)),
    ] + [ANY] * len(pieces)
    if pieces:
        operands += [w_key, w_value]
        in_specs += [pl.BlockSpec((width, lanes), lambda i, idx: (0, i))] * 2
    aliases, out_specs, out_shape = {}, [], []
    if pieces:
        aliases[len(operands)] = 0
        out_specs.append(pl.BlockSpec(memory_space=pltpu.HBM))
        out_shape.append(pltpu.HBM(table.shape, BF16))
    operands += [table, w_out]
    in_specs += [pl.BlockSpec(memory_space=pltpu.HBM), ANY]
    if previous is not None:
        aliases[len(operands)] = len(out_specs)
        operands.append(previous)
        in_specs.append(ANY)
    operands += deps
    in_specs += [ANY] * len(deps)
    skipped = len(deps) + (previous is not None)
    out_specs += [pl.BlockSpec((blocks, blk, width), lambda i, idx: (start // blocks, 0, 0)), ANY]
    out_shape += [jax.ShapeDtypeStruct((queries.shape[0] // blk, blk, width), BF16), TOKEN]
    tab = pltpu.VMEM((2, slots, blk, lanes), BF16)
    sems = pltpu.SemaphoreType.DMA
    scratch = [tab, tab, pltpu.VMEM((rows, width), BF16), pltpu.VMEM((width, width), BF16), sems((2, 2)), sems((1,))]
    if pieces:
        scratch += [pltpu.VMEM((new_rows, width), BF16), sems((len(pieces),)), sems((2, 2))]
    out = pl.pallas_call(
        functools.partial(attend_kernel, head_width, start, loaded, len(pieces), skipped),
        grid_spec=pltpu.PrefetchScalarGridSpec(
            num_scalar_prefetch=1,
            grid=(width // lanes,),
            in_specs=in_specs,
            out_specs=out_specs,
            scratch_shapes=scratch,
        ),
        out_shape=out_shape,
        input_output_aliases=aliases,
        compiler_params=params(52),
        cost_estimate=cost(),
        name="attend",
    )(*operands)
    return out if pieces else [table, *out]


def tree(values):
    while len(values) > 1:
        values = [values[n] + values[n + 1] for n in range(0, len(values), 2)]
    return values[0]


def merged(place, refs, all_ref, width):
    for n, r in enumerate(refs):
        all_ref[place ^ n] = r[...]
    count, rows, _ = all_ref.shape
    levels = [unpack_levels(all_ref[n, :, width:]) for n in range(count)]
    top = functools.reduce(jnp.maximum, levels)
    weights = [jnp.exp2(level - top) for level in levels]
    total = tree(weights)
    weights = [w / total for w in weights]
    head_width = width // HEADS
    lower = lax.broadcasted_iota(jnp.int32, (rows, 2 * head_width), 1) < head_width
    cols = []
    for pair in range(HEADS // 2):
        at = slice(pair * 2 * head_width, (pair + 1) * 2 * head_width)

        def spread(w):
            return jnp.where(lower, w[:, 2 * pair : 2 * pair + 1], w[:, 2 * pair + 1 : 2 * pair + 2])

        mix = tree([all_ref[n, :, at].astype(F32) * spread(weights[n]) for n in range(count)])
        cols.append(mix.astype(BF16))
    return jnp.concatenate(cols, axis=1), top + jnp.log2(total)


def small_call(body, out_shape, scratch, name, flag, operands, deps):
    def wrapped(*refs):
        ins, outs = refs[: 1 + len(operands)], refs[1 + len(operands) + len(deps) :]
        body(*ins, outs[0], *outs[2:])

    return pl.pallas_call(
        wrapped,
        in_specs=[pl.BlockSpec(memory_space=pltpu.SMEM)] + [VMEM] * len(operands) + [ANY] * len(deps),
        out_specs=[VMEM, ANY],
        out_shape=[out_shape, TOKEN],
        scratch_shapes=scratch,
        compiler_params=params(16),
        cost_estimate=cost(),
        name=name,
    )(flag, *operands, *deps)


def register_rounds(slab, keep, send, w_out):
    half, wide = keep.shape
    width = wide - 128
    slabs, phases = lax.axis_size("slab"), lax.axis_size("phase")
    phase = lax.axis_index("phase").astype(jnp.int32)
    turns = [("slab", slab & 1, 0, 2), ("slab", slab >> 1, 1, slabs // 2)]
    turns += [("phase", phase, 0, phases)]

    def swap(x, axis, bit, n):
        return lax.ppermute(x, axis, [(i, i ^ (n << bit)) for i in range(lax.axis_size(axis))])

    def merge_body(place_ref, *refs):
        mix, level = merged(place_ref[0], refs[:-2], refs[-1], width)
        refs[-2][:, :width] = mix
        refs[-2][:, width:] = pack_levels(level)

    def last_body(place_ref, *refs):
        mix, _ = merged(place_ref[0], refs[:-3], refs[-1], width)
        refs[-2][...] = matmul(mix, refs[-3][...]).astype(BF16)

    def join_body(core_ref, mine_ref, got_ref, out_ref):
        core = core_ref[0]
        out_ref[pl.ds(pl.multiple_of(core * half, half), half)] = mine_ref[...]
        out_ref[pl.ds(pl.multiple_of((1 - core) * half, half), half)] = got_ref[...]

    mine, token = keep, None
    for n, (axis, place, bit, size) in enumerate(turns):
        got = [swap(send if n == 0 else mine, axis, bit, j) for j in range(1, size)]
        deps = yield token
        scratch = [pltpu.VMEM((size, half, wide), BF16)]
        place = place.reshape(1)
        if n + 1 < len(turns):
            shape = jax.ShapeDtypeStruct((half, wide), BF16)
            mine, token = small_call(merge_body, shape, scratch, "register_merge", place, [mine, *got], deps)
        else:
            shape = jax.ShapeDtypeStruct((half, width), BF16)
            mine, token = small_call(
                last_body, shape, scratch, "register_out", place, [mine, *got, w_out], deps
            )
    got = swap(mine, "slab", 0, 1)
    deps = yield token
    shape = jax.ShapeDtypeStruct((2 * half, width), BF16)
    out, _ = small_call(join_body, shape, [], "register_join", (slab & 1).reshape(1), [mine, got], deps)
    yield out


def shards(normed, block_list, registers, w_query, w_key, w_value, w_out):
    own_phases, slab_blocks, blk, width = normed.shape
    head_width = width // HEADS
    lanes = QUAD * head_width
    phases, slabs = lax.axis_size("phase"), lax.axis_size("slab")
    own = own_phases * slab_blocks
    slab = lax.axis_index("slab").astype(jnp.int32)
    scale = head_width ** (-0.5) * LOG2E

    def around(x, axis, step, closed):
        n = lax.axis_size(axis)
        return lax.ppermute(
            x, axis, [(i, (i + step) % n) for i in range(n) if closed or 0 <= i + step < n]
        )

    before = around(normed[-1], "phase", 1, True)
    after = around(normed[0], "phase", -1, True)
    left = around(normed[:, -1], "slab", 1, False)
    right = around(normed[:, 0], "slab", -1, False)
    corner_left = around(jnp.stack([before[-1], after[-1]]), "slab", 1, False)
    corner_right = around(jnp.stack([before[0], after[0]]), "slab", -1, False)

    at_left = own
    at_right = at_left + own_phases
    at_before = at_right + own_phases
    at_after = at_before + slab_blocks
    at_corner = at_after + slab_blocks
    slots = at_corner + 4
    assert own == at_before - at_left == slots - at_before

    total_phases, depth_blocks = own_phases * phases, slab_blocks * slabs
    p = (block_list // depth_blocks - lax.axis_index("phase") * own_phases + 1) % total_phases - 1
    z = block_list % depth_blocks - slab * slab_blocks
    is_left, is_right = z < 0, z >= slab_blocks
    is_before, is_after = p < 0, p >= own_phases
    inner = jnp.where(is_left, at_left + p, jnp.where(is_right, at_right + p, p * slab_blocks + z))
    outer = jnp.where(
        is_left | is_right,
        at_corner + jnp.where(is_right, 2, 0) + jnp.where(is_after, 1, 0),
        jnp.where(is_after, at_after, at_before) + z,
    )
    slot_list = jnp.where(is_before | is_after, outer, inner).astype(jnp.int32).reshape(-1)

    rows = normed.reshape(-1, width)
    queries = (matmul(rows, w_query) * scale).astype(BF16)
    table, reg_kv, keep, send = own_project(
        (slab & 1).reshape(1),
        rows,
        registers,
        w_query,
        w_key,
        w_value,
        slots,
        blk,
        head_width,
        2 * lanes,
        scale,
        [queries],
    )
    rounds = register_rounds(slab, keep, send, w_out)
    next(rounds)

    def windows(table, phase, loaded, pieces, mixed, deps):
        return attend(
            queries,
            table,
            reg_kv,
            slot_list,
            phase * slab_blocks,
            slab_blocks,
            loaded,
            pieces,
            w_key,
            w_value,
            w_out,
            head_width,
            mixed,
            deps,
        )

    order = [*range(1, own_phases - 1), 0, own_phases - 1]
    assert len(order) == 4
    mixed, deps = None, []
    for n, at in enumerate(order):
        pieces, loaded = [], at_before if n < 3 else slots
        if n == 0:
            pieces, loaded = [left, right], at_left
        if n == 1:
            deps = [*deps, before, after]
        if n == 2:
            pieces = [before, after, corner_left, corner_right]
        table, mixed, token = windows(table, at, loaded, pieces, mixed, deps)
        token = rounds.send([token])
        deps = [token]
    return mixed.reshape(own_phases, slab_blocks, blk, width), token


def solution(mesh):
    placed = (P("phase", "slab", None, None), P("phase", "slab", None), P(), P(), P(), P(), P())
    return jax.shard_map(
        shards,
        mesh=mesh,
        in_specs=placed,
        out_specs=(P("phase", "slab", None, None), P()),
        check_vma=False,
    )
```

```python
import functools

import jax
import jax.numpy as jnp
from jax import lax
from jax.experimental import pallas as pl
from jax.experimental.pallas import tpu as pltpu
from jax.sharding import PartitionSpec as P

HEADS = 16
LIST = 5
QUAD = 4
TILE_QUADS = 2
LOG2E = 1.4426950408889634
F32, BF16 = jnp.float32, jnp.bfloat16
ANY = pl.BlockSpec(memory_space=pl.ANY)
VMEM = pl.BlockSpec(memory_space=pltpu.VMEM)
TOKEN = jax.ShapeDtypeStruct((8, 128), jnp.float32)


def params(mib):
    return pltpu.CompilerParams(vmem_limit_bytes=mib << 20)


def cost():
    return pl.CostEstimate(flops=1 << 20, bytes_accessed=1 << 16, transcendentals=0)


def matmul(a, b):
    return jnp.dot(a, b, preferred_element_type=F32)


def matmul_t(a, b):
    return lax.dot_general(a, b, (((1,), (1,)), ((), ())), preferred_element_type=F32)


def t_matmul(a, b):
    return lax.dot_general(a, b, (((0,), (0,)), ((), ())), preferred_element_type=F32)


def spread_heads(q, head_width, heads):
    lane = lax.broadcasted_iota(jnp.int32, q.shape, 1) // head_width
    return jnp.concatenate([jnp.where(lane == h, q, jnp.zeros_like(q)) for h in heads], axis=0)


def soften(s):
    peak = jnp.max(s, axis=0, keepdims=True)
    p = jnp.exp2(s - peak)
    total = jnp.sum(p, axis=0, keepdims=True)
    return p.astype(BF16), peak, total


def pair_context(v, p, inverse, head_width):
    o = t_matmul(v, p)
    count = p.shape[1] // 2
    return [
        o[j * head_width : (j + 1) * head_width, j * count : (j + 1) * count]
        * inverse[:, j * count : (j + 1) * count]
        for j in range(2)
    ]


def pack_levels(level):
    hi = level.astype(BF16)
    rest = level - hi.astype(F32)
    mid = rest.astype(BF16)
    low = (rest - mid.astype(F32)).astype(BF16)
    pad = jnp.zeros((level.shape[0], 128 - 3 * level.shape[1]), BF16)
    return jnp.concatenate([hi, mid, low, pad], axis=1)


def unpack_levels(cols):
    wide = cols.astype(F32)
    return wide[:, :HEADS] + wide[:, HEADS : 2 * HEADS] + wide[:, 2 * HEADS : 3 * HEADS]


def own_kernel(scale, head_width, core_ref, *refs):
    x_ref, reg_ref, wq_ref, wk_ref, wv_ref = refs[:5]
    kv_ref, reg_kv_ref, keep_ref, send_ref, _, rows_ref, ctx_ref, level_ref = refs[-8:]
    step = pl.program_id(0)
    count, width = x_ref.shape
    regs = reg_ref.shape[0]
    blk, lanes = kv_ref.shape[2:]
    each = lanes // head_width

    @pl.when(step == 0)
    def _():
        rows_ref[:count] = x_ref[...]
        rows_ref[count:] = reg_ref[...]

    tile = pl.ds(pl.multiple_of(step * lanes, lanes), lanes)
    k = matmul(rows_ref[...], wk_ref[...]).astype(BF16)
    q_reg = (matmul(reg_ref[...], wq_ref[...]) * scale).astype(BF16)
    pairs = [(h, h + 1) for h in range(0, each, 2)]

    def score(pair):
        quad = pair[0] // QUAD * QUAD
        at = slice(quad * head_width, (quad + QUAD) * head_width)
        return matmul_t(
            k[:count, at], spread_heads(q_reg[:, at], head_width, [h - quad for h in pair])
        )

    outs, levels = [], []

    def context(pair, p, peak, total):
        at = slice(pair[0] * head_width, (pair[1] + 1) * head_width)
        outs.extend(pair_context(v[:count, at], p, 1.0 / total, head_width))
        level = peak + jnp.log2(total)
        levels.extend([level[:, :regs], level[:, regs:]])

    following, pending = score(pairs[0]), None
    v = matmul(rows_ref[...], wv_ref[...]).astype(BF16)
    for n, pair in enumerate(pairs):
        s = following
        if n + 1 < len(pairs):
            following = score(pairs[n + 1])
        if pending is not None:
            context(*pending)
        pending = (pair, *soften(s))
    context(*pending)
    for n in range(kv_ref.shape[1]):
        kv_ref[0, n] = k[n * blk : (n + 1) * blk]
        kv_ref[1, n] = v[n * blk : (n + 1) * blk]
    for n in range(reg_kv_ref.shape[1]):
        kv_at = slice(count + n * blk, count + (n + 1) * blk)
        reg_kv_ref[0, n] = k[kv_at]
        reg_kv_ref[1, n] = v[kv_at]
    ctx_ref[:, tile] = jnp.concatenate(outs, axis=0).astype(BF16).T
    level_ref[step] = jnp.concatenate(levels, axis=0)

    @pl.when(step == width // lanes - 1)
    def _():
        stacked = jnp.concatenate([level_ref[g] for g in range(width // lanes)], axis=0)
        ctx_ref[:, width:] = pack_levels(stacked.T)
        half = regs // 2
        core = core_ref[0]
        keep_ref[...] = ctx_ref[pl.ds(pl.multiple_of(core * half, half), half)]
        send_ref[...] = ctx_ref[pl.ds(pl.multiple_of((1 - core) * half, half), half)]


def own_project(core, rows, registers, w_query, w_key, w_value, slots, blk, head_width, lanes, scale, deps):
    count, width = rows.shape
    regs = registers.shape[0]
    half = jax.ShapeDtypeStruct((regs // 2, width + 128), BF16)
    return pl.pallas_call(
        functools.partial(own_kernel, scale, head_width),
        grid_spec=pltpu.PrefetchScalarGridSpec(
            num_scalar_prefetch=1,
            grid=(width // lanes,),
            in_specs=[pl.BlockSpec((count, width), lambda i, s: (0, 0)), pl.BlockSpec((regs, width), lambda i, s: (0, 0))]
            + [pl.BlockSpec((width, lanes), lambda i, s: (0, i))] * 3
            + [ANY] * len(deps),
            out_specs=[
                pl.BlockSpec((2, count // blk, blk, lanes), lambda i, s: (0, 0, 0, i)),
                pl.BlockSpec((2, regs // blk, blk, lanes), lambda i, s: (0, 0, 0, i)),
                pl.BlockSpec(half.shape, lambda i, s: (0, 0)),
                pl.BlockSpec(half.shape, lambda i, s: (0, 0)),
                ANY,
            ],
            scratch_shapes=[
                pltpu.VMEM((count + regs, width), BF16),
                pltpu.VMEM((regs, width + 128), BF16),
                pltpu.VMEM((width // lanes, lanes // head_width, regs), F32),
            ],
        ),
        out_shape=[
            pltpu.HBM((2, slots, blk, width), BF16),
            jax.ShapeDtypeStruct((2, regs // blk, blk, width), BF16),
            half,
            half,
            TOKEN,
        ],
        compiler_params=params(52),
        cost_estimate=cost(),
        name="own_project",
    )(core, rows, registers, w_query, w_key, w_value, *deps)


def query_kernel(scale, x_ref, w_ref, *refs):
    refs[-2][...] = (matmul(x_ref[...], w_ref[...]) * scale).astype(BF16)


def query_project(rows, w_query, lanes, scale, deps):
    count, width = rows.shape
    return pl.pallas_call(
        functools.partial(query_kernel, scale),
        grid=(width // lanes,),
        in_specs=[
            pl.BlockSpec((count, width), lambda i: (0, 0)),
            pl.BlockSpec((width, lanes), lambda i: (0, i)),
        ]
        + [ANY] * len(deps),
        out_specs=[pl.BlockSpec((count, lanes), lambda i: (0, i)), ANY],
        out_shape=[jax.ShapeDtypeStruct((count, width), BF16), TOKEN],
        compiler_params=params(52),
        cost_estimate=cost(),
        name="query_project",
    )(rows, w_query, *deps)


def attend_kernel(head_width, phases, loaded, pieces, skipped, idx_ref, *refs):
    refs = iter(refs)

    def take(count):
        return [next(refs) for _ in range(count)]

    q_refs = take(len(phases))
    (reg_ref,) = take(1)
    xs, w_refs = take(pieces), take(2 if pieces else 0)
    table_ref, wo_ref = take(2)
    take(skipped)
    (new_table_ref,) = take(1) if pieces else (None,)
    o_ref, _ = take(2)
    tabs = take(2)
    ctx_ref, wo_scratch, in_sems, wo_sem, o_sems = take(5)
    if pieces:
        rows_ref, x_sems, out_sems = take(3)
    step, last = pl.program_id(0), pl.num_programs(0) - 1
    buf = lax.rem(step, 2)
    slots, blk, lanes = tabs[0].shape[1:]
    each = q_refs[0].shape[0] // blk
    blocks = each * len(phases)

    def columns(g):
        return pl.ds(pl.multiple_of(g * lanes, lanes), lanes)

    def bring(g, b):
        return [
            pltpu.make_async_copy(
                table_ref.at[side, pl.ds(0, loaded), :, columns(g)],
                tabs[side].at[b, pl.ds(0, loaded)],
                in_sems.at[side, b],
            )
            for side in range(2)
        ]

    def give(g, b):
        return [
            pltpu.make_async_copy(
                tabs[side].at[b, pl.ds(loaded, slots - loaded)],
                new_table_ref.at[side, pl.ds(loaded, slots - loaded), :, columns(g)],
                out_sems.at[side, b],
            )
            for side in range(2)
        ]

    def output_weight():
        return pltpu.make_async_copy(wo_ref, wo_scratch, wo_sem.at[0])

    @pl.when(step == 0)
    def _():
        copies, at = [], 0
        for n, x in enumerate(xs):
            copies.append(pltpu.make_async_copy(x, rows_ref.at[pl.ds(at, x.shape[0])], x_sems.at[n]))
            at += x.shape[0]
        for c in copies + bring(0, 0):
            c.start()
        output_weight().start()
        for c in copies:
            c.wait()

    @pl.when(step < last)
    def _():
        for c in bring(step + 1, 1 - buf):
            c.start()

    if pieces:

        @pl.when(step >= 2)
        def _():
            for c in give(step - 2, buf):
                c.wait()

    def project(side):
        if pieces:
            new = matmul(rows_ref[...], w_refs[side][...]).astype(BF16)
            for n in range(slots - loaded):
                tabs[side][buf, loaded + n] = new[n * blk : (n + 1) * blk]

    project(0)
    for c in bring(step, buf):
        c.wait()

    def gathered(side, block, at):
        place = phases[block // each] * each + block % each
        listed = [idx_ref[place * LIST + e] for e in range(LIST)]
        return jnp.concatenate(
            [tabs[side][buf, slot, :, at] for slot in listed]
            + [reg_ref[side, n, :, at] for n in range(reg_ref.shape[1])],
            axis=0,
        )

    quad = QUAD * head_width

    def score(block, group):
        at = slice(group * quad, (group + 1) * quad)
        inner = block % each * blk
        q = q_refs[block // each][inner : inner + blk, at]
        return matmul_t(gathered(0, block, at), spread_heads(q, head_width, range(QUAD)))

    def context(unit, p, inverse):
        block, group = unit
        outs = []
        for h in range(0, QUAD, 2):
            at = slice(h * blk, (h + 2) * blk)
            first = group * quad + h * head_width
            v = gathered(1, block, slice(first, first + 2 * head_width))
            outs += pair_context(v, p[:, at], inverse[:, at], head_width)
        at = pl.ds(pl.multiple_of(step * lanes + group * quad, quad), quad)
        ctx_ref[block * blk : (block + 1) * blk, at] = jnp.concatenate(outs, axis=0).astype(BF16).T

    units = [(block, group) for group in range(lanes // quad) for block in range(blocks)]
    following, pending = score(*units[0]), None
    project(1)
    for n, unit in enumerate(units):
        s = following
        if n + 1 < len(units):
            following = score(*units[n + 1])
        if pending is not None:
            context(*pending)
        p, _, total = soften(s)
        pending = (unit, p, 1.0 / total)
    context(*pending)
    if pieces:
        for c in give(step, buf):
            c.start()

    @pl.when(step == last)
    def _():
        output_weight().wait()
        ctx_ref[...] = matmul(ctx_ref[...], wo_scratch[...]).astype(BF16)
        rows = each * blk
        copies = [
            pltpu.make_async_copy(
                ctx_ref.at[pl.ds(n * rows, rows)], o_ref.at[pl.ds(phase * rows, rows)], o_sems.at[n]
            )
            for n, phase in enumerate(phases)
        ]
        for c in copies:
            c.start()
        for c in copies:
            c.wait()
        if pieces:
            for c in give(step, buf):
                c.wait()

    if pieces:

        @pl.when((step == last) & (last > 0))
        def _():
            for c in give(step - 1, 1 - buf):
                c.wait()


def attend(
    queries, table, reg_kv, slot_list, each, phases, loaded, pieces, w_key, w_value, w_out, head_width, previous, deps
):
    _, all_slots, blk, width = table.shape
    lanes = TILE_QUADS * QUAD * head_width
    rows = each * blk
    pieces = [x.reshape(-1, width) for x in pieces]
    new_rows = sum(x.shape[0] for x in pieces)
    slots = loaded + new_rows // blk
    assert width % lanes == 0
    operands = [slot_list, *[queries] * len(phases), reg_kv, *pieces]
    in_specs = [
        pl.BlockSpec((rows, lanes), functools.partial(lambda p, i, idx: (p, i), phase)) for phase in phases
    ] + [
        pl.BlockSpec((*reg_kv.shape[:3], lanes), lambda i, idx: (0, 0, 0, i)),
    ] + [ANY] * len(pieces)
    if pieces:
        operands += [w_key, w_value]
        in_specs += [pl.BlockSpec((width, lanes), lambda i, idx: (0, i))] * 2
    aliases, out_specs, out_shape = {}, [], []
    if pieces:
        aliases[len(operands)] = 0
        out_specs.append(pl.BlockSpec(memory_space=pltpu.HBM))
        out_shape.append(pltpu.HBM(table.shape, BF16))
    operands += [table, w_out]
    in_specs += [pl.BlockSpec(memory_space=pltpu.HBM), ANY]
    if previous is not None:
        aliases[len(operands)] = len(out_specs)
        operands.append(previous)
        in_specs.append(ANY)
    operands += deps
    in_specs += [ANY] * len(deps)
    skipped = len(deps) + (previous is not None)
    out_specs += [pl.BlockSpec(memory_space=pltpu.HBM), ANY]
    out_shape += [pltpu.HBM(queries.shape, BF16), TOKEN]
    tab = pltpu.VMEM((2, slots, blk, lanes), BF16)
    sems = pltpu.SemaphoreType.DMA
    scratch = [tab, tab, pltpu.VMEM((rows * len(phases), width), BF16), pltpu.VMEM((width, width), BF16)]
    scratch += [sems((2, 2)), sems((1,)), sems((len(phases),))]
    if pieces:
        scratch += [pltpu.VMEM((new_rows, width), BF16), sems((len(pieces),)), sems((2, 2))]
    out = pl.pallas_call(
        functools.partial(attend_kernel, head_width, phases, loaded, len(pieces), skipped),
        grid_spec=pltpu.PrefetchScalarGridSpec(
            num_scalar_prefetch=1,
            grid=(width // lanes,),
            in_specs=in_specs,
            out_specs=out_specs,
            scratch_shapes=scratch,
        ),
        out_shape=out_shape,
        input_output_aliases=aliases,
        compiler_params=params(52),
        cost_estimate=cost(),
        name="attend",
    )(*operands)
    return out if pieces else [table, *out]


def tree(values):
    while len(values) > 1:
        values = [values[n] + values[n + 1] for n in range(0, len(values), 2)]
    return values[0]


def merged(place, refs, all_ref, width):
    for n, r in enumerate(refs):
        all_ref[place ^ n] = r[...]
    count, rows, _ = all_ref.shape
    levels = [unpack_levels(all_ref[n, :, width:]) for n in range(count)]
    top = functools.reduce(jnp.maximum, levels)
    weights = [jnp.exp2(level - top) for level in levels]
    total = tree(weights)
    weights = [w / total for w in weights]
    head_width = width // HEADS
    lower = lax.broadcasted_iota(jnp.int32, (rows, 2 * head_width), 1) < head_width
    cols = []
    for pair in range(HEADS // 2):
        at = slice(pair * 2 * head_width, (pair + 1) * 2 * head_width)

        def spread(w):
            return jnp.where(lower, w[:, 2 * pair : 2 * pair + 1], w[:, 2 * pair + 1 : 2 * pair + 2])

        mix = tree([all_ref[n, :, at].astype(F32) * spread(weights[n]) for n in range(count)])
        cols.append(mix.astype(BF16))
    return jnp.concatenate(cols, axis=1), top + jnp.log2(total)


def small_call(body, out_shape, scratch, name, flag, operands, deps):
    def wrapped(*refs):
        ins, outs = refs[: 1 + len(operands)], refs[1 + len(operands) + len(deps) :]
        body(*ins, outs[0], *outs[2:])

    return pl.pallas_call(
        wrapped,
        in_specs=[pl.BlockSpec(memory_space=pltpu.SMEM)] + [VMEM] * len(operands) + [ANY] * len(deps),
        out_specs=[VMEM, ANY],
        out_shape=[out_shape, TOKEN],
        scratch_shapes=scratch,
        compiler_params=params(16),
        cost_estimate=cost(),
        name=name,
    )(flag, *operands, *deps)


def register_rounds(slab, keep, send, w_out):
    half, wide = keep.shape
    width = wide - 128
    slabs, phases = lax.axis_size("slab"), lax.axis_size("phase")
    phase = lax.axis_index("phase").astype(jnp.int32)
    turns = [("slab", slab & 1, 0, 2), ("slab", slab >> 1, 1, slabs // 2)]
    turns += [("phase", phase, 0, phases)]

    def swap(x, axis, bit, n):
        return lax.ppermute(x, axis, [(i, i ^ (n << bit)) for i in range(lax.axis_size(axis))])

    def merge_body(place_ref, *refs):
        mix, level = merged(place_ref[0], refs[:-2], refs[-1], width)
        refs[-2][:, :width] = mix
        refs[-2][:, width:] = pack_levels(level)

    def last_body(place_ref, *refs):
        mix, _ = merged(place_ref[0], refs[:-3], refs[-1], width)
        refs[-2][...] = matmul(mix, refs[-3][...]).astype(BF16)

    def join_body(core_ref, mine_ref, got_ref, out_ref):
        core = core_ref[0]
        out_ref[pl.ds(pl.multiple_of(core * half, half), half)] = mine_ref[...]
        out_ref[pl.ds(pl.multiple_of((1 - core) * half, half), half)] = got_ref[...]

    mine, token = keep, None
    for n, (axis, place, bit, size) in enumerate(turns):
        got = [swap(send if n == 0 else mine, axis, bit, j) for j in range(1, size)]
        deps = yield token
        scratch = [pltpu.VMEM((size, half, wide), BF16)]
        place = place.reshape(1)
        if n + 1 < len(turns):
            shape = jax.ShapeDtypeStruct((half, wide), BF16)
            mine, token = small_call(merge_body, shape, scratch, "register_merge", place, [mine, *got], deps)
        else:
            shape = jax.ShapeDtypeStruct((half, width), BF16)
            mine, token = small_call(
                last_body, shape, scratch, "register_out", place, [mine, *got, w_out], deps
            )
    got = swap(mine, "slab", 0, 1)
    deps = yield token
    shape = jax.ShapeDtypeStruct((2 * half, width), BF16)
    out, _ = small_call(join_body, shape, [], "register_join", (slab & 1).reshape(1), [mine, got], deps)
    yield out


def shards(normed, block_list, registers, w_query, w_key, w_value, w_out):
    own_phases, slab_blocks, blk, width = normed.shape
    head_width = width // HEADS
    lanes = QUAD * head_width
    phases, slabs = lax.axis_size("phase"), lax.axis_size("slab")
    own = own_phases * slab_blocks
    slab = lax.axis_index("slab").astype(jnp.int32)
    scale = head_width ** (-0.5) * LOG2E

    def around(x, axis, step, closed):
        n = lax.axis_size(axis)
        return lax.ppermute(
            x, axis, [(i, (i + step) % n) for i in range(n) if closed or 0 <= i + step < n]
        )

    before = around(normed[-1], "phase", 1, True)
    after = around(normed[0], "phase", -1, True)
    left = around(normed[:, -1], "slab", 1, False)
    right = around(normed[:, 0], "slab", -1, False)
    corner_left = around(jnp.stack([before[-1], after[-1]]), "slab", 1, False)
    corner_right = around(jnp.stack([before[0], after[0]]), "slab", -1, False)

    at_left = own
    at_right = at_left + own_phases
    at_before = at_right + own_phases
    at_after = at_before + slab_blocks
    at_corner = at_after + slab_blocks
    slots = at_corner + 4
    assert own == at_before - at_left == slots - at_before

    total_phases, depth_blocks = own_phases * phases, slab_blocks * slabs
    p = (block_list // depth_blocks - lax.axis_index("phase") * own_phases + 1) % total_phases - 1
    z = block_list % depth_blocks - slab * slab_blocks
    is_left, is_right = z < 0, z >= slab_blocks
    is_before, is_after = p < 0, p >= own_phases
    inner = jnp.where(is_left, at_left + p, jnp.where(is_right, at_right + p, p * slab_blocks + z))
    outer = jnp.where(
        is_left | is_right,
        at_corner + jnp.where(is_right, 2, 0) + jnp.where(is_after, 1, 0),
        jnp.where(is_after, at_after, at_before) + z,
    )
    slot_list = jnp.where(is_before | is_after, outer, inner).astype(jnp.int32).reshape(-1)

    rows = normed.reshape(-1, width)
    table, reg_kv, keep, send, token = own_project(
        (slab & 1).reshape(1),
        rows,
        registers,
        w_query,
        w_key,
        w_value,
        slots,
        blk,
        head_width,
        2 * lanes,
        scale,
        [],
    )
    rounds = register_rounds(slab, keep, send, w_out)
    next(rounds)
    queries, token = query_project(
        rows, w_query, 2 * lanes, scale, [token, left, right, before, after]
    )
    token = rounds.send([token])

    def windows(table, at, loaded, pieces, mixed, deps):
        return attend(
            queries,
            table,
            reg_kv,
            slot_list,
            slab_blocks,
            at,
            loaded,
            pieces,
            w_key,
            w_value,
            w_out,
            head_width,
            mixed,
            deps,
        )

    inner, outer = list(range(1, own_phases - 1)), [0, own_phases - 1]
    table, mixed, token = windows(table, inner, at_left, [left, right], None, [token])
    token = rounds.send([token])
    corners = [before, after, corner_left, corner_right]
    _, mixed, token = windows(table, outer, at_before, corners, mixed, [token])
    token = rounds.send([token])
    token = rounds.send([])
    return mixed.reshape(own_phases, slab_blocks, blk, width), token


def solution(mesh):
    placed = (P("phase", "slab", None, None), P("phase", "slab", None), P(), P(), P(), P(), P())
    return jax.shard_map(
        shards,
        mesh=mesh,
        in_specs=placed,
        out_specs=(P("phase", "slab", None, None), P()),
        check_vma=False,
    )
```

```python
import functools

import jax
import jax.numpy as jnp
from jax import lax
from jax.experimental import pallas as pl
from jax.experimental.pallas import tpu as pltpu
from jax.sharding import PartitionSpec as P

HEADS = 16
LIST = 5
QUAD = 4
TILE_QUADS = 4
LOG2E = 1.4426950408889634
F32, BF16 = jnp.float32, jnp.bfloat16
ANY = pl.BlockSpec(memory_space=pl.ANY)
VMEM = pl.BlockSpec(memory_space=pltpu.VMEM)
TOKEN = pltpu.HBM((8, 128), jnp.float32)


def params(mib):
    return pltpu.CompilerParams(vmem_limit_bytes=mib << 20)


def cost():
    return pl.CostEstimate(flops=1 << 20, bytes_accessed=1 << 16, transcendentals=0)


def matmul(a, b):
    return jnp.dot(a, b, preferred_element_type=F32)


def matmul_t(a, b):
    return lax.dot_general(a, b, (((1,), (1,)), ((), ())), preferred_element_type=F32)


def t_matmul(a, b):
    return lax.dot_general(a, b, (((0,), (0,)), ((), ())), preferred_element_type=F32)


def spread_heads(q, head_width, heads):
    lane = lax.broadcasted_iota(jnp.int32, q.shape, 1) // head_width
    return jnp.concatenate([jnp.where(lane == h, q, jnp.zeros_like(q)) for h in heads], axis=0)


def soften(s):
    peak = jnp.max(s, axis=0, keepdims=True)
    return jnp.exp2(s - peak).astype(BF16), peak


def pair_context(v, p, head_width):
    wide = 2 * head_width
    ones = jnp.ones((16, v.shape[0]), BF16)
    o = matmul(jnp.concatenate([v.T, ones], axis=0), p)
    total = o[wide : wide + 1]
    inverse = 1.0 / total
    count = p.shape[1] // 2
    outs = [
        o[j * head_width : (j + 1) * head_width, j * count : (j + 1) * count]
        * inverse[:, j * count : (j + 1) * count]
        for j in range(2)
    ]
    return outs, total


def pack_levels(level):
    hi = level.astype(BF16)
    rest = level - hi.astype(F32)
    mid = rest.astype(BF16)
    low = (rest - mid.astype(F32)).astype(BF16)
    pad = jnp.zeros((level.shape[0], 128 - 3 * level.shape[1]), BF16)
    return jnp.concatenate([hi, mid, low, pad], axis=1)


def unpack_levels(cols):
    wide = cols.astype(F32)
    return wide[:, :HEADS] + wide[:, HEADS : 2 * HEADS] + wide[:, 2 * HEADS : 3 * HEADS]


def own_kernel(scale, head_width, core_ref, *refs):
    x_ref, reg_ref, wq_ref, wk_ref, wv_ref = refs[:5]
    q_ref, kv_ref, reg_kv_ref, keep_ref, send_ref, rows_ref, ctx_ref, level_ref = refs[-8:]
    step = pl.program_id(0)
    count, width = x_ref.shape
    regs = reg_ref.shape[0]
    blk, lanes = kv_ref.shape[2:]
    each = lanes // head_width

    @pl.when(step == 0)
    def _():
        rows_ref[:count] = x_ref[...]
        rows_ref[count:] = reg_ref[...]

    tile = pl.ds(pl.multiple_of(step * lanes, lanes), lanes)
    k = matmul(rows_ref[...], wk_ref[...]).astype(BF16)
    q_reg = (matmul(reg_ref[...], wq_ref[...]) * scale).astype(BF16)
    pairs = [(h, h + 1) for h in range(0, each, 2)]

    def score(pair):
        quad = pair[0] // QUAD * QUAD
        at = slice(quad * head_width, (quad + QUAD) * head_width)
        return matmul_t(
            k[:count, at], spread_heads(q_reg[:, at], head_width, [h - quad for h in pair])
        )

    outs, levels = [], []

    def context(pair, p, peak):
        at = slice(pair[0] * head_width, (pair[1] + 1) * head_width)
        found, total = pair_context(v[:count, at], p, head_width)
        outs.extend(found)
        level = peak + jnp.log2(total)
        levels.extend([level[:, :regs], level[:, regs:]])

    following, pending = score(pairs[0]), None
    v = matmul(rows_ref[...], wv_ref[...]).astype(BF16)
    for n, pair in enumerate(pairs):
        s = following
        if n + 1 < len(pairs):
            following = score(pairs[n + 1])
        else:
            q_ref[...] = (matmul(x_ref[...], wq_ref[...]) * scale).astype(BF16)
        if pending is not None:
            context(*pending)
        pending = (pair, *soften(s))
    context(*pending)
    for n in range(kv_ref.shape[1]):
        kv_ref[0, n] = k[n * blk : (n + 1) * blk]
        kv_ref[1, n] = v[n * blk : (n + 1) * blk]
    for n in range(reg_kv_ref.shape[1]):
        kv_at = slice(count + n * blk, count + (n + 1) * blk)
        reg_kv_ref[0, n] = k[kv_at]
        reg_kv_ref[1, n] = v[kv_at]
    ctx_ref[:, tile] = jnp.concatenate(outs, axis=0).astype(BF16).T
    level_ref[step] = jnp.concatenate(levels, axis=0)

    @pl.when(step == width // lanes - 1)
    def _():
        stacked = jnp.concatenate([level_ref[g] for g in range(width // lanes)], axis=0)
        ctx_ref[:, width:] = pack_levels(stacked.T)
        half = regs // 2
        core = core_ref[0]
        keep_ref[...] = ctx_ref[pl.ds(pl.multiple_of(core * half, half), half)]
        send_ref[...] = ctx_ref[pl.ds(pl.multiple_of((1 - core) * half, half), half)]


def own_project(core, rows, registers, w_query, w_key, w_value, slots, blk, head_width, lanes, scale, deps):
    count, width = rows.shape
    regs = registers.shape[0]
    half = jax.ShapeDtypeStruct((regs // 2, width + 128), BF16)
    return pl.pallas_call(
        functools.partial(own_kernel, scale, head_width),
        grid_spec=pltpu.PrefetchScalarGridSpec(
            num_scalar_prefetch=1,
            grid=(width // lanes,),
            in_specs=[pl.BlockSpec((count, width), lambda i, s: (0, 0)), pl.BlockSpec((regs, width), lambda i, s: (0, 0))]
            + [pl.BlockSpec((width, lanes), lambda i, s: (0, i))] * 3
            + [ANY] * len(deps),
            out_specs=[
                pl.BlockSpec((count, lanes), lambda i, s: (0, i)),
                pl.BlockSpec((2, count // blk, blk, lanes), lambda i, s: (0, 0, 0, i)),
                pl.BlockSpec((2, regs // blk, blk, lanes), lambda i, s: (0, 0, 0, i)),
                pl.BlockSpec(half.shape, lambda i, s: (0, 0)),
                pl.BlockSpec(half.shape, lambda i, s: (0, 0)),
            ],
            scratch_shapes=[
                pltpu.VMEM((count + regs, width), BF16),
                pltpu.VMEM((regs, width + 128), BF16),
                pltpu.VMEM((width // lanes, lanes // head_width, regs), F32),
            ],
        ),
        out_shape=[
            jax.ShapeDtypeStruct((count, width), BF16),
            pltpu.HBM((2, slots, blk, width), BF16),
            jax.ShapeDtypeStruct((2, regs // blk, blk, width), BF16),
            half,
            half,
        ],
        compiler_params=params(52),
        cost_estimate=cost(),
        name="own_project",
    )(core, rows, registers, w_query, w_key, w_value, *deps)


def attend_kernel(head_width, each, phases, loaded, pieces, skipped, idx_ref, *refs):
    refs = iter(refs)

    def take(count):
        return [next(refs) for _ in range(count)]

    q_hbm, reg_hbm = take(2)
    xs, w_hbms = take(pieces), take(2 if pieces else 0)
    table_ref, wo_hbm = take(2)
    take(skipped)
    (new_table_ref,) = take(1) if pieces else (None,)
    o_ref, _ = take(2)
    tabs = take(2)
    q_ref, reg_ref, ctx_ref, wo_ref, q_sems, reg_sem, tab_sems, wo_sem, o_sems = take(9)
    if pieces:
        rows_ref, *w_refs = take(3)
        x_sems, w_sems, out_sems = take(3)
    halves, slots, blk, lanes = tabs[0].shape
    quad = QUAD * head_width
    rows = each * blk
    copy = pltpu.make_async_copy

    def columns(g):
        return pl.ds(g * lanes, lanes)

    bring = [
        [
            copy(
                table_ref.at[side, pl.ds(0, loaded), :, columns(g)],
                tabs[side].at[g, pl.ds(0, loaded)],
                tab_sems.at[side, g],
            )
            for g in range(halves)
        ]
        for side in range(2)
    ]
    get_q = [
        copy(q_hbm.at[pl.ds(phase * rows, rows)], q_ref.at[pl.ds(n * rows, rows)], q_sems.at[n])
        for n, phase in enumerate(phases)
    ]
    get_reg = copy(reg_hbm, reg_ref, reg_sem.at[0])
    get_wo = copy(wo_hbm, wo_ref, wo_sem.at[0])
    get_x, get_w = [], []
    if pieces:
        at = 0
        for n, x in enumerate(xs):
            get_x.append(copy(x, rows_ref.at[pl.ds(at, x.shape[0])], x_sems.at[n]))
            at += x.shape[0]
        get_w = [
            [copy(w_hbms[side].at[:, columns(g)], w_refs[side].at[g], w_sems.at[side, g]) for g in range(halves)]
            for side in range(2)
        ]
        give = [
            [
                copy(
                    tabs[side].at[g, pl.ds(loaded, slots - loaded)],
                    new_table_ref.at[side, pl.ds(loaded, slots - loaded), :, columns(g)],
                    out_sems.at[side, g],
                )
                for g in range(halves)
            ]
            for side in range(2)
        ]
    for c in get_x:
        c.start()
    for g in range(halves):
        for side in range(2):
            if pieces:
                get_w[side][g].start()
            bring[side][g].start()
            if g == 0 and side == 0:
                for c in (*get_q, get_reg):
                    c.start()
    get_wo.start()
    for c in get_x:
        c.wait()

    def project(side, g):
        if pieces:
            get_w[side][g].wait()
            new = matmul(rows_ref[...], w_refs[side][g]).astype(BF16)
            for n in range(slots - loaded):
                tabs[side][g, loaded + n] = new[n * blk : (n + 1) * blk]
            give[side][g].start()
        bring[side][g].wait()

    def gathered(side, block, group, start, width):
        g, within = divmod(group * quad, lanes)
        place = phases[block // each] * each + block % each
        listed = [idx_ref[place * LIST + e] for e in range(LIST)]
        here = slice(within + start, within + start + width)
        there = slice(group * quad + start, group * quad + start + width)
        return jnp.concatenate(
            [tabs[side][g, slot, :, here] for slot in listed]
            + [reg_ref[side, n, :, there] for n in range(reg_ref.shape[1])],
            axis=0,
        )

    def score(block, group):
        q = q_ref[block * blk : (block + 1) * blk, group * quad : (group + 1) * quad]
        return matmul_t(gathered(0, block, group, 0, quad), spread_heads(q, head_width, range(QUAD)))

    def context(unit, p):
        block, group = unit
        outs = []
        for h in range(0, QUAD, 2):
            at = slice(h * blk, (h + 2) * blk)
            v = gathered(1, block, group, h * head_width, 2 * head_width)
            outs += pair_context(v, p[:, at], head_width)[0]
        ctx_ref[block * blk : (block + 1) * blk, group * quad : (group + 1) * quad] = (
            jnp.concatenate(outs, axis=0).astype(BF16).T
        )

    blocks, per = each * len(phases), lanes // quad
    units = [(block, group) for group in range(halves * per) for block in range(blocks)]
    in_half = blocks * per
    project(0, 0)
    for c in (*get_q, get_reg):
        c.wait()
    project(1, 0)
    for g in range(1, halves):
        project(0, g)
        project(1, g)
    following, pending = score(*units[0]), None
    for n, unit in enumerate(units):
        half, step = divmod(n, in_half)
        s = following
        if n + 1 < len(units):
            following = score(*units[n + 1])
        if pending is not None:
            context(*pending)
        p, _ = soften(s)
        pending = (unit, p)
    context(*pending)
    get_wo.wait()
    puts = []
    for n, phase in enumerate(phases):
        at = pl.ds(n * rows, rows)
        q_ref[at] = matmul(ctx_ref[at], wo_ref[...]).astype(BF16)
        puts.append(copy(q_ref.at[at], o_ref.at[pl.ds(phase * rows, rows)], o_sems.at[n]))
        puts[-1].start()
    for c in puts:
        c.wait()
    if pieces:
        for c in (*give[0], *give[1]):
            c.wait()


def attend(
    queries, table, reg_kv, slot_list, each, phases, loaded, pieces, w_key, w_value, w_out, head_width, previous, deps
):
    _, all_slots, blk, width = table.shape
    lanes = TILE_QUADS * QUAD * head_width
    rows = each * blk * len(phases)
    pieces = [x.reshape(-1, width) for x in pieces]
    new_rows = sum(x.shape[0] for x in pieces)
    slots = loaded + new_rows // blk
    halves = width // lanes
    assert width % lanes == 0
    hbm = pl.BlockSpec(memory_space=pltpu.HBM)
    operands = [slot_list, queries, reg_kv, *pieces]
    if pieces:
        operands += [w_key, w_value]
    aliases, out_shape = {}, []
    in_specs = [ANY] * (len(operands) - 1)
    if pieces:
        aliases[len(operands)] = 0
        out_shape.append(pltpu.HBM(table.shape, BF16))
    operands += [table, w_out]
    in_specs += [hbm, ANY]
    if previous is not None:
        aliases[len(operands)] = len(out_shape)
        operands.append(previous)
        in_specs.append(hbm)
    operands += deps
    in_specs += [ANY] * len(deps)
    skipped = len(deps) + (previous is not None)
    out_specs = [hbm] * (len(out_shape) + 1) + [ANY]
    out_shape += [pltpu.HBM(queries.shape, BF16), TOKEN]
    tab = pltpu.VMEM((halves, slots, blk, lanes), BF16)
    sems = pltpu.SemaphoreType.DMA
    scratch = [tab, tab, pltpu.VMEM((rows, width), BF16), pltpu.VMEM(reg_kv.shape, BF16)]
    scratch += [pltpu.VMEM((rows, width), BF16), pltpu.VMEM((width, width), BF16)]
    scratch += [sems((len(phases),)), sems((1,)), sems((2, halves)), sems((1,)), sems((len(phases),))]
    if pieces:
        scratch += [pltpu.VMEM((new_rows, width), BF16), *[pltpu.VMEM((halves, width, lanes), BF16)] * 2]
        scratch += [sems((len(pieces),)), sems((2, halves)), sems((2, halves))]
    out = pl.pallas_call(
        functools.partial(attend_kernel, head_width, each, phases, loaded, len(pieces), skipped),
        grid_spec=pltpu.PrefetchScalarGridSpec(
            num_scalar_prefetch=1, grid=(1,), in_specs=in_specs, out_specs=out_specs, scratch_shapes=scratch
        ),
        out_shape=out_shape,
        input_output_aliases=aliases,
        compiler_params=params(56),
        cost_estimate=cost(),
        name="attend",
    )(*operands)
    return out if pieces else [table, *out]


def tree(values):
    while len(values) > 1:
        values = [values[n] + values[n + 1] for n in range(0, len(values), 2)]
    return values[0]


def merged(place, refs, all_ref, width):
    for n, r in enumerate(refs):
        all_ref[place ^ n] = r[...]
    count, rows, _ = all_ref.shape
    levels = [unpack_levels(all_ref[n, :, width:]) for n in range(count)]
    top = functools.reduce(jnp.maximum, levels)
    weights = [jnp.exp2(level - top) for level in levels]
    total = tree(weights)
    weights = [w / total for w in weights]
    head_width = width // HEADS
    lower = lax.broadcasted_iota(jnp.int32, (rows, 2 * head_width), 1) < head_width
    cols = []
    for pair in range(HEADS // 2):
        at = slice(pair * 2 * head_width, (pair + 1) * 2 * head_width)

        def spread(w):
            return jnp.where(lower, w[:, 2 * pair : 2 * pair + 1], w[:, 2 * pair + 1 : 2 * pair + 2])

        mix = tree([all_ref[n, :, at].astype(F32) * spread(weights[n]) for n in range(count)])
        cols.append(mix.astype(BF16))
    return jnp.concatenate(cols, axis=1), top + jnp.log2(total)


def small_call(body, out_shape, scratch, name, flag, operands, deps):
    def wrapped(*refs):
        ins, outs = refs[: 1 + len(operands)], refs[1 + len(operands) + len(deps) :]
        body(*ins, outs[0], *outs[2:])

    return pl.pallas_call(
        wrapped,
        in_specs=[pl.BlockSpec(memory_space=pltpu.SMEM)] + [VMEM] * len(operands) + [ANY] * len(deps),
        out_specs=[VMEM, ANY],
        out_shape=[out_shape, TOKEN],
        scratch_shapes=scratch,
        compiler_params=params(16),
        cost_estimate=cost(),
        name=name,
    )(flag, *operands, *deps)


def register_rounds(slab, keep, send, w_out):
    half, wide = keep.shape
    width = wide - 128
    slabs, phases = lax.axis_size("slab"), lax.axis_size("phase")
    phase = lax.axis_index("phase").astype(jnp.int32)
    turns = [("slab", slab & 1, 0, 2), ("slab", slab >> 1, 1, slabs // 2)]
    turns += [("phase", phase, 0, phases)]

    def swap(x, axis, bit, n):
        return lax.ppermute(x, axis, [(i, i ^ (n << bit)) for i in range(lax.axis_size(axis))])

    def merge_body(place_ref, *refs):
        mix, level = merged(place_ref[0], refs[:-2], refs[-1], width)
        refs[-2][:, :width] = mix
        refs[-2][:, width:] = pack_levels(level)

    def last_body(place_ref, *refs):
        mix, _ = merged(place_ref[0], refs[:-3], refs[-1], width)
        refs[-2][...] = matmul(mix, refs[-3][...]).astype(BF16)

    def join_body(core_ref, mine_ref, got_ref, out_ref):
        core = core_ref[0]
        out_ref[pl.ds(pl.multiple_of(core * half, half), half)] = mine_ref[...]
        out_ref[pl.ds(pl.multiple_of((1 - core) * half, half), half)] = got_ref[...]

    mine, token = keep, None
    for n, (axis, place, bit, size) in enumerate(turns):
        got = [swap(send if n == 0 else mine, axis, bit, j) for j in range(1, size)]
        deps = yield token
        scratch = [pltpu.VMEM((size, half, wide), BF16)]
        place = place.reshape(1)
        if n + 1 < len(turns):
            shape = jax.ShapeDtypeStruct((half, wide), BF16)
            mine, token = small_call(merge_body, shape, scratch, "register_merge", place, [mine, *got], deps)
        else:
            shape = jax.ShapeDtypeStruct((half, width), BF16)
            mine, token = small_call(
                last_body, shape, scratch, "register_out", place, [mine, *got, w_out], deps
            )
    got = swap(mine, "slab", 0, 1)
    deps = yield token
    shape = jax.ShapeDtypeStruct((2 * half, width), BF16)
    out, _ = small_call(join_body, shape, [], "register_join", (slab & 1).reshape(1), [mine, got], deps)
    yield out


def shards(normed, block_list, registers, w_query, w_key, w_value, w_out):
    own_phases, slab_blocks, blk, width = normed.shape
    head_width = width // HEADS
    lanes = QUAD * head_width
    phases, slabs = lax.axis_size("phase"), lax.axis_size("slab")
    own = own_phases * slab_blocks
    slab = lax.axis_index("slab").astype(jnp.int32)
    scale = head_width ** (-0.5) * LOG2E

    def around(x, axis, step, closed):
        n = lax.axis_size(axis)
        return lax.ppermute(
            x, axis, [(i, (i + step) % n) for i in range(n) if closed or 0 <= i + step < n]
        )

    before = around(normed[-1], "phase", 1, True)
    after = around(normed[0], "phase", -1, True)
    left = around(normed[:, -1], "slab", 1, False)
    right = around(normed[:, 0], "slab", -1, False)

    at_left = own
    at_right = at_left + own_phases
    at_before = at_right + own_phases
    at_after = at_before + slab_blocks
    at_corner = at_after + slab_blocks
    slots = at_corner + 4
    assert own == at_before - at_left == slots - at_before

    total_phases, depth_blocks = own_phases * phases, slab_blocks * slabs
    p = (block_list // depth_blocks - lax.axis_index("phase") * own_phases + 1) % total_phases - 1
    z = block_list % depth_blocks - slab * slab_blocks
    is_left, is_right = z < 0, z >= slab_blocks
    is_before, is_after = p < 0, p >= own_phases
    inner = jnp.where(is_left, at_left + p, jnp.where(is_right, at_right + p, p * slab_blocks + z))
    outer = jnp.where(
        is_left | is_right,
        at_corner + jnp.where(is_right, 2, 0) + jnp.where(is_after, 1, 0),
        jnp.where(is_after, at_after, at_before) + z,
    )
    slot_list = jnp.where(is_before | is_after, outer, inner).astype(jnp.int32).reshape(-1)

    rows = normed.reshape(-1, width)
    queries, table, reg_kv, keep, send = own_project(
        (slab & 1).reshape(1),
        rows,
        registers,
        w_query,
        w_key,
        w_value,
        slots,
        blk,
        head_width,
        2 * lanes,
        scale,
        [],
    )
    send, left, right, before, after = lax.optimization_barrier((send, left, right, before, after))
    corner_left = around(jnp.stack([before[-1], after[-1]]), "slab", 1, False)
    corner_right = around(jnp.stack([before[0], after[0]]), "slab", -1, False)
    rounds = register_rounds(slab, keep, send, w_out)
    next(rounds)
    token = rounds.send([])

    def windows(table, at, loaded, pieces, mixed, deps):
        return attend(
            queries,
            table,
            reg_kv,
            slot_list,
            slab_blocks,
            at,
            loaded,
            pieces,
            w_key,
            w_value,
            w_out,
            head_width,
            mixed,
            deps,
        )

    inner, outer = list(range(1, own_phases - 1)), [0, own_phases - 1]
    table, mixed, token = windows(table, inner, at_left, [left, right], None, [token])
    token = rounds.send([token])
    corners = [before, after, corner_left, corner_right]
    _, mixed, token = windows(table, outer, at_before, corners, mixed, [token])
    token = rounds.send([token])
    token = rounds.send([])
    return mixed.reshape(own_phases, slab_blocks, blk, width), token


def solution(mesh):
    placed = (P("phase", "slab", None, None), P("phase", "slab", None), P(), P(), P(), P(), P())
    return jax.shard_map(
        shards,
        mesh=mesh,
        in_specs=placed,
        out_specs=(P("phase", "slab", None, None), P()),
        check_vma=False,
    )
```

```python
import functools

import jax
import jax.numpy as jnp
from jax import lax
from jax.experimental import pallas as pl
from jax.experimental.pallas import tpu as pltpu
from jax.sharding import PartitionSpec as P

HEADS = 16
LIST = 5
QUAD = 4
TILE_QUADS = 4
LOG2E = 1.4426950408889634
F32, BF16 = jnp.float32, jnp.bfloat16
ANY = pl.BlockSpec(memory_space=pl.ANY)
VMEM = pl.BlockSpec(memory_space=pltpu.VMEM)
TOKEN = jax.ShapeDtypeStruct((8, 128), jnp.float32)


def params(mib):
    return pltpu.CompilerParams(vmem_limit_bytes=mib << 20)


def cost():
    return pl.CostEstimate(flops=1 << 20, bytes_accessed=1 << 16, transcendentals=0)


def matmul(a, b):
    return jnp.dot(a, b, preferred_element_type=F32)


def matmul_t(a, b):
    return lax.dot_general(a, b, (((1,), (1,)), ((), ())), preferred_element_type=F32)


def t_matmul(a, b):
    return lax.dot_general(a, b, (((0,), (0,)), ((), ())), preferred_element_type=F32)


def spread_heads(q, head_width, heads):
    lane = lax.broadcasted_iota(jnp.int32, q.shape, 1) // head_width
    return jnp.concatenate([jnp.where(lane == h, q, jnp.zeros_like(q)) for h in heads], axis=0)


def soften(s):
    peak = jnp.max(s, axis=0, keepdims=True)
    return jnp.exp2(s - peak).astype(BF16), peak


def pair_context(v, p, head_width):
    wide = 2 * head_width
    ones = jnp.ones((16, v.shape[0]), BF16)
    o = matmul(jnp.concatenate([v.T, ones], axis=0), p)
    total = o[wide : wide + 1]
    inverse = 1.0 / total
    count = p.shape[1] // 2
    outs = [
        o[j * head_width : (j + 1) * head_width, j * count : (j + 1) * count]
        * inverse[:, j * count : (j + 1) * count]
        for j in range(2)
    ]
    return outs, total


def pack_levels(level):
    hi = level.astype(BF16)
    rest = level - hi.astype(F32)
    mid = rest.astype(BF16)
    low = (rest - mid.astype(F32)).astype(BF16)
    pad = jnp.zeros((level.shape[0], 128 - 3 * level.shape[1]), BF16)
    return jnp.concatenate([hi, mid, low, pad], axis=1)


def unpack_levels(cols):
    wide = cols.astype(F32)
    return wide[:, :HEADS] + wide[:, HEADS : 2 * HEADS] + wide[:, 2 * HEADS : 3 * HEADS]


def own_kernel(scale, head_width, core_ref, *refs):
    x_ref, reg_ref, wq_ref, wk_ref, wv_ref = refs[:5]
    kv_ref, reg_kv_ref, keep_ref, send_ref, _, rows_ref, ctx_ref, level_ref = refs[-8:]
    step = pl.program_id(0)
    count, width = x_ref.shape
    regs = reg_ref.shape[0]
    blk, lanes = kv_ref.shape[2:]
    each = lanes // head_width

    @pl.when(step == 0)
    def _():
        rows_ref[:count] = x_ref[...]
        rows_ref[count:] = reg_ref[...]

    tile = pl.ds(pl.multiple_of(step * lanes, lanes), lanes)
    k = matmul(rows_ref[...], wk_ref[...]).astype(BF16)
    q_reg = (matmul(reg_ref[...], wq_ref[...]) * scale).astype(BF16)
    pairs = [(h, h + 1) for h in range(0, each, 2)]

    def score(pair):
        quad = pair[0] // QUAD * QUAD
        at = slice(quad * head_width, (quad + QUAD) * head_width)
        return matmul_t(
            k[:count, at], spread_heads(q_reg[:, at], head_width, [h - quad for h in pair])
        )

    outs, levels = [], []

    def context(pair, p, peak):
        at = slice(pair[0] * head_width, (pair[1] + 1) * head_width)
        found, total = pair_context(v[:count, at], p, head_width)
        outs.extend(found)
        level = peak + jnp.log2(total)
        levels.extend([level[:, :regs], level[:, regs:]])

    following, pending = score(pairs[0]), None
    v = matmul(rows_ref[...], wv_ref[...]).astype(BF16)
    for n, pair in enumerate(pairs):
        s = following
        if n + 1 < len(pairs):
            following = score(pairs[n + 1])
        if pending is not None:
            context(*pending)
        pending = (pair, *soften(s))
    context(*pending)
    for n in range(kv_ref.shape[1]):
        kv_ref[0, n] = k[n * blk : (n + 1) * blk]
        kv_ref[1, n] = v[n * blk : (n + 1) * blk]
    for n in range(reg_kv_ref.shape[1]):
        kv_at = slice(count + n * blk, count + (n + 1) * blk)
        reg_kv_ref[0, n] = k[kv_at]
        reg_kv_ref[1, n] = v[kv_at]
    ctx_ref[:, tile] = jnp.concatenate(outs, axis=0).astype(BF16).T
    level_ref[step] = jnp.concatenate(levels, axis=0)

    @pl.when(step == width // lanes - 1)
    def _():
        stacked = jnp.concatenate([level_ref[g] for g in range(width // lanes)], axis=0)
        ctx_ref[:, width:] = pack_levels(stacked.T)
        half = regs // 2
        core = core_ref[0]
        keep_ref[...] = ctx_ref[pl.ds(pl.multiple_of(core * half, half), half)]
        send_ref[...] = ctx_ref[pl.ds(pl.multiple_of((1 - core) * half, half), half)]


def own_project(core, rows, registers, w_query, w_key, w_value, slots, blk, head_width, lanes, scale, deps):
    count, width = rows.shape
    regs = registers.shape[0]
    half = jax.ShapeDtypeStruct((regs // 2, width + 128), BF16)
    return pl.pallas_call(
        functools.partial(own_kernel, scale, head_width),
        grid_spec=pltpu.PrefetchScalarGridSpec(
            num_scalar_prefetch=1,
            grid=(width // lanes,),
            in_specs=[pl.BlockSpec((count, width), lambda i, s: (0, 0)), pl.BlockSpec((regs, width), lambda i, s: (0, 0))]
            + [pl.BlockSpec((width, lanes), lambda i, s: (0, i))] * 3
            + [ANY] * len(deps),
            out_specs=[
                pl.BlockSpec((2, count // blk, blk, lanes), lambda i, s: (0, 0, 0, i)),
                pl.BlockSpec((2, regs // blk, blk, lanes), lambda i, s: (0, 0, 0, i)),
                pl.BlockSpec(half.shape, lambda i, s: (0, 0)),
                pl.BlockSpec(half.shape, lambda i, s: (0, 0)),
                ANY,
            ],
            scratch_shapes=[
                pltpu.VMEM((count + regs, width), BF16),
                pltpu.VMEM((regs, width + 128), BF16),
                pltpu.VMEM((width // lanes, lanes // head_width, regs), F32),
            ],
        ),
        out_shape=[
            pltpu.HBM((2, slots, blk, width), BF16),
            jax.ShapeDtypeStruct((2, regs // blk, blk, width), BF16),
            half,
            half,
            TOKEN,
        ],
        compiler_params=params(52),
        cost_estimate=cost(),
        name="own_project",
    )(core, rows, registers, w_query, w_key, w_value, *deps)


def query_kernel(scale, x_ref, w_ref, *refs):
    refs[-2][...] = (matmul(x_ref[...], w_ref[...]) * scale).astype(BF16)


def query_project(rows, w_query, lanes, scale, deps):
    count, width = rows.shape
    return pl.pallas_call(
        functools.partial(query_kernel, scale),
        grid=(width // lanes,),
        in_specs=[
            pl.BlockSpec((count, width), lambda i: (0, 0)),
            pl.BlockSpec((width, lanes), lambda i: (0, i)),
        ]
        + [ANY] * len(deps),
        out_specs=[pl.BlockSpec((count, lanes), lambda i: (0, i)), ANY],
        out_shape=[jax.ShapeDtypeStruct((count, width), BF16), TOKEN],
        compiler_params=params(52),
        cost_estimate=cost(),
        name="query_project",
    )(rows, w_query, *deps)


def attend_kernel(head_width, each, phases, loaded, pieces, skipped, idx_ref, *refs):
    refs = iter(refs)

    def take(count):
        return [next(refs) for _ in range(count)]

    q_hbm, reg_hbm = take(2)
    xs, w_hbms = take(pieces), take(2 if pieces else 0)
    table_ref, wo_hbm = take(2)
    take(skipped)
    (new_table_ref,) = take(1) if pieces else (None,)
    o_ref, _ = take(2)
    tabs = take(2)
    q_ref, reg_ref, ctx_ref, wo_ref, q_sems, reg_sem, tab_sems, wo_sem, o_sems = take(9)
    if pieces:
        rows_ref, *w_refs = take(3)
        x_sems, w_sems, out_sems = take(3)
    halves, slots, blk, lanes = tabs[0].shape
    quad = QUAD * head_width
    rows = each * blk
    copy = pltpu.make_async_copy

    def columns(g):
        return pl.ds(g * lanes, lanes)

    bring = [
        [
            copy(
                table_ref.at[side, pl.ds(0, loaded), :, columns(g)],
                tabs[side].at[g, pl.ds(0, loaded)],
                tab_sems.at[side, g],
            )
            for g in range(halves)
        ]
        for side in range(2)
    ]
    get_q = [
        copy(q_hbm.at[pl.ds(phase * rows, rows)], q_ref.at[pl.ds(n * rows, rows)], q_sems.at[n])
        for n, phase in enumerate(phases)
    ]
    get_reg = copy(reg_hbm, reg_ref, reg_sem.at[0])
    get_wo = copy(wo_hbm, wo_ref, wo_sem.at[0])
    get_x, get_w = [], []
    if pieces:
        at = 0
        for n, x in enumerate(xs):
            get_x.append(copy(x, rows_ref.at[pl.ds(at, x.shape[0])], x_sems.at[n]))
            at += x.shape[0]
        get_w = [
            [copy(w_hbms[side].at[:, columns(g)], w_refs[side].at[g], w_sems.at[side, g]) for g in range(halves)]
            for side in range(2)
        ]
        give = [
            [
                copy(
                    tabs[side].at[g, pl.ds(loaded, slots - loaded)],
                    new_table_ref.at[side, pl.ds(loaded, slots - loaded), :, columns(g)],
                    out_sems.at[side, g],
                )
                for g in range(halves)
            ]
            for side in range(2)
        ]
    for c in get_x:
        c.start()
    for g in range(halves):
        for side in range(2):
            if pieces:
                get_w[side][g].start()
            bring[side][g].start()
            if g == 0 and side == 0:
                for c in (*get_q, get_reg):
                    c.start()
    get_wo.start()
    for c in get_x:
        c.wait()

    def project(side, g):
        if pieces:
            get_w[side][g].wait()
            new = matmul(rows_ref[...], w_refs[side][g]).astype(BF16)
            for n in range(slots - loaded):
                tabs[side][g, loaded + n] = new[n * blk : (n + 1) * blk]
            give[side][g].start()
        bring[side][g].wait()

    def gathered(side, block, group, start, width):
        g, within = divmod(group * quad, lanes)
        place = phases[block // each] * each + block % each
        listed = [idx_ref[place * LIST + e] for e in range(LIST)]
        here = slice(within + start, within + start + width)
        there = slice(group * quad + start, group * quad + start + width)
        return jnp.concatenate(
            [tabs[side][g, slot, :, here] for slot in listed]
            + [reg_ref[side, n, :, there] for n in range(reg_ref.shape[1])],
            axis=0,
        )

    def score(block, group):
        q = q_ref[block * blk : (block + 1) * blk, group * quad : (group + 1) * quad]
        return matmul_t(gathered(0, block, group, 0, quad), spread_heads(q, head_width, range(QUAD)))

    def context(unit, p):
        block, group = unit
        outs = []
        for h in range(0, QUAD, 2):
            at = slice(h * blk, (h + 2) * blk)
            v = gathered(1, block, group, h * head_width, 2 * head_width)
            outs += pair_context(v, p[:, at], head_width)[0]
        ctx_ref[block * blk : (block + 1) * blk, group * quad : (group + 1) * quad] = (
            jnp.concatenate(outs, axis=0).astype(BF16).T
        )

    blocks, per = each * len(phases), lanes // quad
    units = [(block, group) for group in range(halves * per) for block in range(blocks)]
    in_half = blocks * per
    project(0, 0)
    for c in (*get_q, get_reg):
        c.wait()
    project(1, 0)
    for g in range(1, halves):
        project(0, g)
        project(1, g)
    following, pending = score(*units[0]), None
    for n, unit in enumerate(units):
        half, step = divmod(n, in_half)
        s = following
        if n + 1 < len(units):
            following = score(*units[n + 1])
        if pending is not None:
            context(*pending)
        p, _ = soften(s)
        pending = (unit, p)
    context(*pending)
    get_wo.wait()
    puts = []
    for n, phase in enumerate(phases):
        at = pl.ds(n * rows, rows)
        q_ref[at] = matmul(ctx_ref[at], wo_ref[...]).astype(BF16)
        puts.append(copy(q_ref.at[at], o_ref.at[pl.ds(phase * rows, rows)], o_sems.at[n]))
        puts[-1].start()
    for c in puts:
        c.wait()
    if pieces:
        for c in (*give[0], *give[1]):
            c.wait()


def attend(
    queries, table, reg_kv, slot_list, each, phases, loaded, pieces, w_key, w_value, w_out, head_width, previous, deps
):
    _, all_slots, blk, width = table.shape
    lanes = TILE_QUADS * QUAD * head_width
    rows = each * blk * len(phases)
    pieces = [x.reshape(-1, width) for x in pieces]
    new_rows = sum(x.shape[0] for x in pieces)
    slots = loaded + new_rows // blk
    halves = width // lanes
    assert width % lanes == 0
    hbm = pl.BlockSpec(memory_space=pltpu.HBM)
    operands = [slot_list, queries, reg_kv, *pieces]
    if pieces:
        operands += [w_key, w_value]
    aliases, out_shape = {}, []
    in_specs = [ANY] * (len(operands) - 1)
    if pieces:
        aliases[len(operands)] = 0
        out_shape.append(pltpu.HBM(table.shape, BF16))
    operands += [table, w_out]
    in_specs += [hbm, ANY]
    if previous is not None:
        aliases[len(operands)] = len(out_shape)
        operands.append(previous)
        in_specs.append(hbm)
    operands += deps
    in_specs += [ANY] * len(deps)
    skipped = len(deps) + (previous is not None)
    out_specs = [hbm] * (len(out_shape) + 1) + [ANY]
    out_shape += [pltpu.HBM(queries.shape, BF16), TOKEN]
    tab = pltpu.VMEM((halves, slots, blk, lanes), BF16)
    sems = pltpu.SemaphoreType.DMA
    scratch = [tab, tab, pltpu.VMEM((rows, width), BF16), pltpu.VMEM(reg_kv.shape, BF16)]
    scratch += [pltpu.VMEM((rows, width), BF16), pltpu.VMEM((width, width), BF16)]
    scratch += [sems((len(phases),)), sems((1,)), sems((2, halves)), sems((1,)), sems((len(phases),))]
    if pieces:
        scratch += [pltpu.VMEM((new_rows, width), BF16), *[pltpu.VMEM((halves, width, lanes), BF16)] * 2]
        scratch += [sems((len(pieces),)), sems((2, halves)), sems((2, halves))]
    out = pl.pallas_call(
        functools.partial(attend_kernel, head_width, each, phases, loaded, len(pieces), skipped),
        grid_spec=pltpu.PrefetchScalarGridSpec(
            num_scalar_prefetch=1, grid=(1,), in_specs=in_specs, out_specs=out_specs, scratch_shapes=scratch
        ),
        out_shape=out_shape,
        input_output_aliases=aliases,
        compiler_params=params(52),
        cost_estimate=cost(),
        name="attend",
    )(*operands)
    return out if pieces else [table, *out]


def tree(values):
    while len(values) > 1:
        values = [values[n] + values[n + 1] for n in range(0, len(values), 2)]
    return values[0]


def merged(place, refs, all_ref, width):
    for n, r in enumerate(refs):
        all_ref[place ^ n] = r[...]
    count, rows, _ = all_ref.shape
    levels = [unpack_levels(all_ref[n, :, width:]) for n in range(count)]
    top = functools.reduce(jnp.maximum, levels)
    weights = [jnp.exp2(level - top) for level in levels]
    total = tree(weights)
    weights = [w / total for w in weights]
    head_width = width // HEADS
    lower = lax.broadcasted_iota(jnp.int32, (rows, 2 * head_width), 1) < head_width
    cols = []
    for pair in range(HEADS // 2):
        at = slice(pair * 2 * head_width, (pair + 1) * 2 * head_width)

        def spread(w):
            return jnp.where(lower, w[:, 2 * pair : 2 * pair + 1], w[:, 2 * pair + 1 : 2 * pair + 2])

        mix = tree([all_ref[n, :, at].astype(F32) * spread(weights[n]) for n in range(count)])
        cols.append(mix.astype(BF16))
    return jnp.concatenate(cols, axis=1), top + jnp.log2(total)


def small_call(body, out_shape, scratch, name, flag, operands, deps):
    def wrapped(*refs):
        ins, outs = refs[: 1 + len(operands)], refs[1 + len(operands) + len(deps) :]
        body(*ins, outs[0], *outs[2:])

    return pl.pallas_call(
        wrapped,
        in_specs=[pl.BlockSpec(memory_space=pltpu.SMEM)] + [VMEM] * len(operands) + [ANY] * len(deps),
        out_specs=[VMEM, ANY],
        out_shape=[out_shape, TOKEN],
        scratch_shapes=scratch,
        compiler_params=params(16),
        cost_estimate=cost(),
        name=name,
    )(flag, *operands, *deps)


def register_rounds(slab, keep, send, w_out):
    half, wide = keep.shape
    width = wide - 128
    slabs, phases = lax.axis_size("slab"), lax.axis_size("phase")
    phase = lax.axis_index("phase").astype(jnp.int32)
    turns = [("slab", slab & 1, 0, 2), ("slab", slab >> 1, 1, slabs // 2)]
    turns += [("phase", phase, 0, phases)]

    def swap(x, axis, bit, n):
        return lax.ppermute(x, axis, [(i, i ^ (n << bit)) for i in range(lax.axis_size(axis))])

    def merge_body(place_ref, *refs):
        mix, level = merged(place_ref[0], refs[:-2], refs[-1], width)
        refs[-2][:, :width] = mix
        refs[-2][:, width:] = pack_levels(level)

    def last_body(place_ref, *refs):
        mix, _ = merged(place_ref[0], refs[:-3], refs[-1], width)
        refs[-2][...] = matmul(mix, refs[-3][...]).astype(BF16)

    def join_body(core_ref, mine_ref, got_ref, out_ref):
        core = core_ref[0]
        out_ref[pl.ds(pl.multiple_of(core * half, half), half)] = mine_ref[...]
        out_ref[pl.ds(pl.multiple_of((1 - core) * half, half), half)] = got_ref[...]

    mine, token = keep, None
    for n, (axis, place, bit, size) in enumerate(turns):
        got = [swap(send if n == 0 else mine, axis, bit, j) for j in range(1, size)]
        deps = yield token
        scratch = [pltpu.VMEM((size, half, wide), BF16)]
        place = place.reshape(1)
        if n + 1 < len(turns):
            shape = jax.ShapeDtypeStruct((half, wide), BF16)
            mine, token = small_call(merge_body, shape, scratch, "register_merge", place, [mine, *got], deps)
        else:
            shape = jax.ShapeDtypeStruct((half, width), BF16)
            mine, token = small_call(
                last_body, shape, scratch, "register_out", place, [mine, *got, w_out], deps
            )
    got = swap(mine, "slab", 0, 1)
    deps = yield token
    shape = jax.ShapeDtypeStruct((2 * half, width), BF16)
    out, _ = small_call(join_body, shape, [], "register_join", (slab & 1).reshape(1), [mine, got], deps)
    yield out


def shards(normed, block_list, registers, w_query, w_key, w_value, w_out):
    own_phases, slab_blocks, blk, width = normed.shape
    head_width = width // HEADS
    lanes = QUAD * head_width
    phases, slabs = lax.axis_size("phase"), lax.axis_size("slab")
    own = own_phases * slab_blocks
    slab = lax.axis_index("slab").astype(jnp.int32)
    scale = head_width ** (-0.5) * LOG2E

    def around(x, axis, step, closed):
        n = lax.axis_size(axis)
        return lax.ppermute(
            x, axis, [(i, (i + step) % n) for i in range(n) if closed or 0 <= i + step < n]
        )

    before = around(normed[-1], "phase", 1, True)
    after = around(normed[0], "phase", -1, True)
    left = around(normed[:, -1], "slab", 1, False)
    right = around(normed[:, 0], "slab", -1, False)
    corner_left = around(jnp.stack([before[-1], after[-1]]), "slab", 1, False)
    corner_right = around(jnp.stack([before[0], after[0]]), "slab", -1, False)

    at_left = own
    at_right = at_left + own_phases
    at_before = at_right + own_phases
    at_after = at_before + slab_blocks
    at_corner = at_after + slab_blocks
    slots = at_corner + 4
    assert own == at_before - at_left == slots - at_before

    total_phases, depth_blocks = own_phases * phases, slab_blocks * slabs
    p = (block_list // depth_blocks - lax.axis_index("phase") * own_phases + 1) % total_phases - 1
    z = block_list % depth_blocks - slab * slab_blocks
    is_left, is_right = z < 0, z >= slab_blocks
    is_before, is_after = p < 0, p >= own_phases
    inner = jnp.where(is_left, at_left + p, jnp.where(is_right, at_right + p, p * slab_blocks + z))
    outer = jnp.where(
        is_left | is_right,
        at_corner + jnp.where(is_right, 2, 0) + jnp.where(is_after, 1, 0),
        jnp.where(is_after, at_after, at_before) + z,
    )
    slot_list = jnp.where(is_before | is_after, outer, inner).astype(jnp.int32).reshape(-1)

    rows = normed.reshape(-1, width)
    table, reg_kv, keep, send, token = own_project(
        (slab & 1).reshape(1),
        rows,
        registers,
        w_query,
        w_key,
        w_value,
        slots,
        blk,
        head_width,
        2 * lanes,
        scale,
        [],
    )
    rounds = register_rounds(slab, keep, send, w_out)
    next(rounds)
    queries, token = query_project(
        rows, w_query, 2 * lanes, scale, [token, left, right, before, after]
    )
    token = rounds.send([token])

    def windows(table, at, loaded, pieces, mixed, deps):
        return attend(
            queries,
            table,
            reg_kv,
            slot_list,
            slab_blocks,
            at,
            loaded,
            pieces,
            w_key,
            w_value,
            w_out,
            head_width,
            mixed,
            deps,
        )

    inner, outer = list(range(1, own_phases - 1)), [0, own_phases - 1]
    table, mixed, token = windows(table, inner, at_left, [left, right], None, [token])
    token = rounds.send([token])
    corners = [before, after, corner_left, corner_right]
    _, mixed, token = windows(table, outer, at_before, corners, mixed, [token])
    token = rounds.send([token])
    token = rounds.send([])
    return mixed.reshape(own_phases, slab_blocks, blk, width), token


def solution(mesh):
    placed = (P("phase", "slab", None, None), P("phase", "slab", None), P(), P(), P(), P(), P())
    return jax.shard_map(
        shards,
        mesh=mesh,
        in_specs=placed,
        out_specs=(P("phase", "slab", None, None), P()),
        check_vma=False,
    )
```

```python
import functools

import jax
import jax.numpy as jnp
from jax import lax
from jax.experimental import pallas as pl
from jax.experimental.pallas import tpu as pltpu
from jax.sharding import PartitionSpec as P

HEADS = 16
LIST = 5
QUAD = 4
TILE_QUADS = 2
LOG2E = 1.4426950408889634
F32, BF16 = jnp.float32, jnp.bfloat16
ANY = pl.BlockSpec(memory_space=pl.ANY)
VMEM = pl.BlockSpec(memory_space=pltpu.VMEM)
TOKEN = jax.ShapeDtypeStruct((8, 128), jnp.float32)


def params(mib):
    return pltpu.CompilerParams(vmem_limit_bytes=mib << 20)


def cost():
    return pl.CostEstimate(flops=1 << 20, bytes_accessed=1 << 16, transcendentals=0)


def matmul(a, b):
    return jnp.dot(a, b, preferred_element_type=F32)


def matmul_t(a, b):
    return lax.dot_general(a, b, (((1,), (1,)), ((), ())), preferred_element_type=F32)


def t_matmul(a, b):
    return lax.dot_general(a, b, (((0,), (0,)), ((), ())), preferred_element_type=F32)


def spread_heads(q, head_width, heads):
    lane = lax.broadcasted_iota(jnp.int32, q.shape, 1) // head_width
    return jnp.concatenate([jnp.where(lane == h, q, jnp.zeros_like(q)) for h in heads], axis=0)


def soften(s):
    peak = jnp.max(s, axis=0, keepdims=True)
    p = jnp.exp2(s - peak)
    total = jnp.sum(p, axis=0, keepdims=True)
    return p.astype(BF16), peak, total


def pair_context(v, p, inverse, head_width):
    o = t_matmul(v, p)
    count = p.shape[1] // 2
    return [
        o[j * head_width : (j + 1) * head_width, j * count : (j + 1) * count]
        * inverse[:, j * count : (j + 1) * count]
        for j in range(2)
    ]


def pack_levels(level):
    hi = level.astype(BF16)
    rest = level - hi.astype(F32)
    mid = rest.astype(BF16)
    low = (rest - mid.astype(F32)).astype(BF16)
    pad = jnp.zeros((level.shape[0], 128 - 3 * level.shape[1]), BF16)
    return jnp.concatenate([hi, mid, low, pad], axis=1)


def unpack_levels(cols):
    wide = cols.astype(F32)
    return wide[:, :HEADS] + wide[:, HEADS : 2 * HEADS] + wide[:, 2 * HEADS : 3 * HEADS]


def own_kernel(scale, head_width, core_ref, *refs):
    x_ref, reg_ref, wq_ref, wk_ref, wv_ref = refs[:5]
    kv_ref, reg_kv_ref, keep_ref, send_ref, _, rows_ref, ctx_ref, level_ref = refs[-8:]
    step = pl.program_id(0)
    count, width = x_ref.shape
    regs = reg_ref.shape[0]
    blk, lanes = kv_ref.shape[2:]
    each = lanes // head_width

    @pl.when(step == 0)
    def _():
        rows_ref[:count] = x_ref[...]
        rows_ref[count:] = reg_ref[...]

    tile = pl.ds(pl.multiple_of(step * lanes, lanes), lanes)
    k = matmul(rows_ref[...], wk_ref[...]).astype(BF16)
    q_reg = (matmul(reg_ref[...], wq_ref[...]) * scale).astype(BF16)
    pairs = [(h, h + 1) for h in range(0, each, 2)]

    def score(pair):
        quad = pair[0] // QUAD * QUAD
        at = slice(quad * head_width, (quad + QUAD) * head_width)
        return matmul_t(
            k[:count, at], spread_heads(q_reg[:, at], head_width, [h - quad for h in pair])
        )

    outs, levels = [], []

    def context(pair, p, peak, total):
        at = slice(pair[0] * head_width, (pair[1] + 1) * head_width)
        outs.extend(pair_context(v[:count, at], p, 1.0 / total, head_width))
        level = peak + jnp.log2(total)
        levels.extend([level[:, :regs], level[:, regs:]])

    following, pending = score(pairs[0]), None
    v = matmul(rows_ref[...], wv_ref[...]).astype(BF16)
    for n, pair in enumerate(pairs):
        s = following
        if n + 1 < len(pairs):
            following = score(pairs[n + 1])
        if pending is not None:
            context(*pending)
        pending = (pair, *soften(s))
    context(*pending)
    for n in range(kv_ref.shape[1]):
        kv_ref[0, n] = k[n * blk : (n + 1) * blk]
        kv_ref[1, n] = v[n * blk : (n + 1) * blk]
    for n in range(reg_kv_ref.shape[1]):
        kv_at = slice(count + n * blk, count + (n + 1) * blk)
        reg_kv_ref[0, n] = k[kv_at]
        reg_kv_ref[1, n] = v[kv_at]
    ctx_ref[:, tile] = jnp.concatenate(outs, axis=0).astype(BF16).T
    level_ref[step] = jnp.concatenate(levels, axis=0)

    @pl.when(step == width // lanes - 1)
    def _():
        stacked = jnp.concatenate([level_ref[g] for g in range(width // lanes)], axis=0)
        ctx_ref[:, width:] = pack_levels(stacked.T)
        half = regs // 2
        core = core_ref[0]
        keep_ref[...] = ctx_ref[pl.ds(pl.multiple_of(core * half, half), half)]
        send_ref[...] = ctx_ref[pl.ds(pl.multiple_of((1 - core) * half, half), half)]


def own_project(core, rows, registers, w_query, w_key, w_value, slots, blk, head_width, lanes, scale, deps):
    count, width = rows.shape
    regs = registers.shape[0]
    half = jax.ShapeDtypeStruct((regs // 2, width + 128), BF16)
    return pl.pallas_call(
        functools.partial(own_kernel, scale, head_width),
        grid_spec=pltpu.PrefetchScalarGridSpec(
            num_scalar_prefetch=1,
            grid=(width // lanes,),
            in_specs=[pl.BlockSpec((count, width), lambda i, s: (0, 0)), pl.BlockSpec((regs, width), lambda i, s: (0, 0))]
            + [pl.BlockSpec((width, lanes), lambda i, s: (0, i))] * 3
            + [ANY] * len(deps),
            out_specs=[
                pl.BlockSpec((2, count // blk, blk, lanes), lambda i, s: (0, 0, 0, i)),
                pl.BlockSpec((2, regs // blk, blk, lanes), lambda i, s: (0, 0, 0, i)),
                pl.BlockSpec(half.shape, lambda i, s: (0, 0)),
                pl.BlockSpec(half.shape, lambda i, s: (0, 0)),
                ANY,
            ],
            scratch_shapes=[
                pltpu.VMEM((count + regs, width), BF16),
                pltpu.VMEM((regs, width + 128), BF16),
                pltpu.VMEM((width // lanes, lanes // head_width, regs), F32),
            ],
        ),
        out_shape=[
            pltpu.HBM((2, slots, blk, width), BF16),
            jax.ShapeDtypeStruct((2, regs // blk, blk, width), BF16),
            half,
            half,
            TOKEN,
        ],
        compiler_params=params(52),
        cost_estimate=cost(),
        name="own_project",
    )(core, rows, registers, w_query, w_key, w_value, *deps)


def query_kernel(scale, x_ref, w_ref, *refs):
    lanes = refs[-2].shape[1]
    at = pl.ds(pl.multiple_of(pl.program_id(0) * lanes, lanes), lanes)
    refs[-2][...] = (matmul(x_ref[...], w_ref[:, at]) * scale).astype(BF16)


def query_project(rows, w_query, lanes, scale, deps):
    count, width = rows.shape
    return pl.pallas_call(
        functools.partial(query_kernel, scale),
        grid=(width // lanes,),
        in_specs=[
            VMEM,
            VMEM,
        ]
        + [ANY] * len(deps),
        out_specs=[pl.BlockSpec((count, lanes), lambda i: (0, i)), ANY],
        out_shape=[pltpu.HBM((count, width), BF16), TOKEN],
        compiler_params=params(20),
        cost_estimate=cost(),
        name="query_project",
    )(rows, w_query, *deps)


def attend_kernel(head_width, phases, loaded, pieces, skipped, idx_ref, *refs):
    refs = iter(refs)

    def take(count):
        return [next(refs) for _ in range(count)]

    q_refs = take(len(phases))
    (reg_ref,) = take(1)
    xs, w_refs = take(pieces), take(2 if pieces else 0)
    table_ref, wo_ref = take(2)
    take(skipped)
    (new_table_ref,) = take(1) if pieces else (None,)
    o_ref, _ = take(2)
    tabs = take(2)
    ctx_ref, wo_scratch, in_sems, wo_sem, o_sems = take(5)
    if pieces:
        rows_ref, x_sems, out_sems = take(3)
    step, last = pl.program_id(0), pl.num_programs(0) - 1
    buf = lax.rem(step, 2)
    slots, blk, lanes = tabs[0].shape[1:]
    each = q_refs[0].shape[0] // blk
    blocks = each * len(phases)

    def columns(g):
        return pl.ds(pl.multiple_of(g * lanes, lanes), lanes)

    def bring(g, b):
        return [
            pltpu.make_async_copy(
                table_ref.at[side, pl.ds(0, loaded), :, columns(g)],
                tabs[side].at[b, pl.ds(0, loaded)],
                in_sems.at[side, b],
            )
            for side in range(2)
        ]

    def give(g, b):
        return [
            pltpu.make_async_copy(
                tabs[side].at[b, pl.ds(loaded, slots - loaded)],
                new_table_ref.at[side, pl.ds(loaded, slots - loaded), :, columns(g)],
                out_sems.at[side, b],
            )
            for side in range(2)
        ]

    def output_weight():
        return pltpu.make_async_copy(wo_ref, wo_scratch, wo_sem.at[0])

    @pl.when(step == 0)
    def _():
        copies, at = [], 0
        for n, x in enumerate(xs):
            copies.append(pltpu.make_async_copy(x, rows_ref.at[pl.ds(at, x.shape[0])], x_sems.at[n]))
            at += x.shape[0]
        for c in copies + bring(0, 0):
            c.start()
        output_weight().start()
        for c in copies:
            c.wait()

    @pl.when(step < last)
    def _():
        for c in bring(step + 1, 1 - buf):
            c.start()

    if pieces:

        @pl.when(step >= 2)
        def _():
            for c in give(step - 2, buf):
                c.wait()

    def project(side):
        if pieces:
            new = matmul(rows_ref[...], w_refs[side][...]).astype(BF16)
            for n in range(slots - loaded):
                tabs[side][buf, loaded + n] = new[n * blk : (n + 1) * blk]

    project(0)
    for c in bring(step, buf):
        c.wait()

    def gathered(side, block, at):
        place = phases[block // each] * each + block % each
        listed = [idx_ref[place * LIST + e] for e in range(LIST)]
        return jnp.concatenate(
            [tabs[side][buf, slot, :, at] for slot in listed]
            + [reg_ref[side, n, :, at] for n in range(reg_ref.shape[1])],
            axis=0,
        )

    quad = QUAD * head_width

    def score(block, group):
        at = slice(group * quad, (group + 1) * quad)
        inner = block % each * blk
        q = q_refs[block // each][inner : inner + blk, at]
        return matmul_t(gathered(0, block, at), spread_heads(q, head_width, range(QUAD)))

    def context(unit, p, inverse):
        block, group = unit
        outs = []
        for h in range(0, QUAD, 2):
            at = slice(h * blk, (h + 2) * blk)
            first = group * quad + h * head_width
            v = gathered(1, block, slice(first, first + 2 * head_width))
            outs += pair_context(v, p[:, at], inverse[:, at], head_width)
        at = pl.ds(pl.multiple_of(step * lanes + group * quad, quad), quad)
        ctx_ref[block * blk : (block + 1) * blk, at] = jnp.concatenate(outs, axis=0).astype(BF16).T

    units = [(block, group) for group in range(lanes // quad) for block in range(blocks)]
    following, pending = score(*units[0]), None
    project(1)
    for n, unit in enumerate(units):
        s = following
        if n + 1 < len(units):
            following = score(*units[n + 1])
        if pending is not None:
            context(*pending)
        p, _, total = soften(s)
        pending = (unit, p, 1.0 / total)
    context(*pending)
    if pieces:
        for c in give(step, buf):
            c.start()

    @pl.when(step == last)
    def _():
        output_weight().wait()
        ctx_ref[...] = matmul(ctx_ref[...], wo_scratch[...]).astype(BF16)
        rows = each * blk
        copies = [
            pltpu.make_async_copy(
                ctx_ref.at[pl.ds(n * rows, rows)], o_ref.at[pl.ds(phase * rows, rows)], o_sems.at[n]
            )
            for n, phase in enumerate(phases)
        ]
        for c in copies:
            c.start()
        for c in copies:
            c.wait()
        if pieces:
            for c in give(step, buf):
                c.wait()

    if pieces:

        @pl.when((step == last) & (last > 0))
        def _():
            for c in give(step - 1, 1 - buf):
                c.wait()


def attend(
    queries, table, reg_kv, slot_list, each, phases, loaded, pieces, w_key, w_value, w_out, head_width, previous, deps
):
    _, all_slots, blk, width = table.shape
    lanes = TILE_QUADS * QUAD * head_width
    rows = each * blk
    pieces = [x.reshape(-1, width) for x in pieces]
    new_rows = sum(x.shape[0] for x in pieces)
    slots = loaded + new_rows // blk
    assert width % lanes == 0
    operands = [slot_list, *[queries] * len(phases), reg_kv, *pieces]
    in_specs = [
        pl.BlockSpec((rows, lanes), functools.partial(lambda p, i, idx: (p, i), phase)) for phase in phases
    ] + [
        pl.BlockSpec((*reg_kv.shape[:3], lanes), lambda i, idx: (0, 0, 0, i)),
    ] + [ANY] * len(pieces)
    if pieces:
        operands += [w_key, w_value]
        in_specs += [pl.BlockSpec((width, lanes), lambda i, idx: (0, i))] * 2
    aliases, out_specs, out_shape = {}, [], []
    if pieces:
        aliases[len(operands)] = 0
        out_specs.append(pl.BlockSpec(memory_space=pltpu.HBM))
        out_shape.append(pltpu.HBM(table.shape, BF16))
    operands += [table, w_out]
    in_specs += [pl.BlockSpec(memory_space=pltpu.HBM), ANY]
    if previous is not None:
        aliases[len(operands)] = len(out_specs)
        operands.append(previous)
        in_specs.append(ANY)
    operands += deps
    in_specs += [ANY] * len(deps)
    skipped = len(deps) + (previous is not None)
    out_specs += [pl.BlockSpec(memory_space=pltpu.HBM), ANY]
    out_shape += [pltpu.HBM(queries.shape, BF16), TOKEN]
    tab = pltpu.VMEM((2, slots, blk, lanes), BF16)
    sems = pltpu.SemaphoreType.DMA
    scratch = [tab, tab, pltpu.VMEM((rows * len(phases), width), BF16), pltpu.VMEM((width, width), BF16)]
    scratch += [sems((2, 2)), sems((1,)), sems((len(phases),))]
    if pieces:
        scratch += [pltpu.VMEM((new_rows, width), BF16), sems((len(pieces),)), sems((2, 2))]
    out = pl.pallas_call(
        functools.partial(attend_kernel, head_width, phases, loaded, len(pieces), skipped),
        grid_spec=pltpu.PrefetchScalarGridSpec(
            num_scalar_prefetch=1,
            grid=(width // lanes,),
            in_specs=in_specs,
            out_specs=out_specs,
            scratch_shapes=scratch,
        ),
        out_shape=out_shape,
        input_output_aliases=aliases,
        compiler_params=params(52),
        cost_estimate=cost(),
        name="attend",
    )(*operands)
    return out if pieces else [table, *out]


def tree(values):
    while len(values) > 1:
        values = [values[n] + values[n + 1] for n in range(0, len(values), 2)]
    return values[0]


def merged(place, refs, all_ref, width):
    for n, r in enumerate(refs):
        all_ref[place ^ n] = r[...]
    count, rows, _ = all_ref.shape
    levels = [unpack_levels(all_ref[n, :, width:]) for n in range(count)]
    top = functools.reduce(jnp.maximum, levels)
    weights = [jnp.exp2(level - top) for level in levels]
    total = tree(weights)
    weights = [w / total for w in weights]
    head_width = width // HEADS
    lower = lax.broadcasted_iota(jnp.int32, (rows, 2 * head_width), 1) < head_width
    cols = []
    for pair in range(HEADS // 2):
        at = slice(pair * 2 * head_width, (pair + 1) * 2 * head_width)

        def spread(w):
            return jnp.where(lower, w[:, 2 * pair : 2 * pair + 1], w[:, 2 * pair + 1 : 2 * pair + 2])

        mix = tree([all_ref[n, :, at].astype(F32) * spread(weights[n]) for n in range(count)])
        cols.append(mix.astype(BF16))
    return jnp.concatenate(cols, axis=1), top + jnp.log2(total)


def small_call(body, out_shape, scratch, name, flag, operands, deps):
    def wrapped(*refs):
        ins, outs = refs[: 1 + len(operands)], refs[1 + len(operands) + len(deps) :]
        body(*ins, outs[0], *outs[2:])

    return pl.pallas_call(
        wrapped,
        in_specs=[pl.BlockSpec(memory_space=pltpu.SMEM)] + [VMEM] * len(operands) + [ANY] * len(deps),
        out_specs=[VMEM, ANY],
        out_shape=[out_shape, TOKEN],
        scratch_shapes=scratch,
        compiler_params=params(16),
        cost_estimate=cost(),
        name=name,
    )(flag, *operands, *deps)


def register_rounds(slab, keep, send, w_out):
    half, wide = keep.shape
    width = wide - 128
    slabs, phases = lax.axis_size("slab"), lax.axis_size("phase")
    phase = lax.axis_index("phase").astype(jnp.int32)
    turns = [("slab", slab & 1, 0, 2), ("slab", slab >> 1, 1, slabs // 2)]
    turns += [("phase", phase, 0, phases)]

    def swap(x, axis, bit, n):
        return lax.ppermute(x, axis, [(i, i ^ (n << bit)) for i in range(lax.axis_size(axis))])

    def merge_body(place_ref, *refs):
        mix, level = merged(place_ref[0], refs[:-2], refs[-1], width)
        refs[-2][:, :width] = mix
        refs[-2][:, width:] = pack_levels(level)

    def last_body(place_ref, *refs):
        mix, _ = merged(place_ref[0], refs[:-3], refs[-1], width)
        refs[-2][...] = matmul(mix, refs[-3][...]).astype(BF16)

    def join_body(core_ref, mine_ref, got_ref, out_ref):
        core = core_ref[0]
        out_ref[pl.ds(pl.multiple_of(core * half, half), half)] = mine_ref[...]
        out_ref[pl.ds(pl.multiple_of((1 - core) * half, half), half)] = got_ref[...]

    mine, token = keep, None
    for n, (axis, place, bit, size) in enumerate(turns):
        got = [swap(send if n == 0 else mine, axis, bit, j) for j in range(1, size)]
        deps = yield token
        scratch = [pltpu.VMEM((size, half, wide), BF16)]
        place = place.reshape(1)
        if n + 1 < len(turns):
            shape = jax.ShapeDtypeStruct((half, wide), BF16)
            mine, token = small_call(merge_body, shape, scratch, "register_merge", place, [mine, *got], deps)
        else:
            shape = jax.ShapeDtypeStruct((half, width), BF16)
            mine, token = small_call(
                last_body, shape, scratch, "register_out", place, [mine, *got, w_out], deps
            )
    got = swap(mine, "slab", 0, 1)
    deps = yield token
    shape = jax.ShapeDtypeStruct((2 * half, width), BF16)
    out, _ = small_call(join_body, shape, [], "register_join", (slab & 1).reshape(1), [mine, got], deps)
    yield out


def shards(normed, block_list, registers, w_query, w_key, w_value, w_out):
    own_phases, slab_blocks, blk, width = normed.shape
    head_width = width // HEADS
    lanes = QUAD * head_width
    phases, slabs = lax.axis_size("phase"), lax.axis_size("slab")
    own = own_phases * slab_blocks
    slab = lax.axis_index("slab").astype(jnp.int32)
    scale = head_width ** (-0.5) * LOG2E

    def around(x, axis, step, closed):
        n = lax.axis_size(axis)
        return lax.ppermute(
            x, axis, [(i, (i + step) % n) for i in range(n) if closed or 0 <= i + step < n]
        )

    before = around(normed[-1], "phase", 1, True)
    after = around(normed[0], "phase", -1, True)
    left = around(normed[:, -1], "slab", 1, False)
    right = around(normed[:, 0], "slab", -1, False)
    corner_left = around(jnp.stack([before[-1], after[-1]]), "slab", 1, False)
    corner_right = around(jnp.stack([before[0], after[0]]), "slab", -1, False)

    at_left = own
    at_right = at_left + own_phases
    at_before = at_right + own_phases
    at_after = at_before + slab_blocks
    at_corner = at_after + slab_blocks
    slots = at_corner + 4
    assert own == at_before - at_left == slots - at_before

    total_phases, depth_blocks = own_phases * phases, slab_blocks * slabs
    p = (block_list // depth_blocks - lax.axis_index("phase") * own_phases + 1) % total_phases - 1
    z = block_list % depth_blocks - slab * slab_blocks
    is_left, is_right = z < 0, z >= slab_blocks
    is_before, is_after = p < 0, p >= own_phases
    inner = jnp.where(is_left, at_left + p, jnp.where(is_right, at_right + p, p * slab_blocks + z))
    outer = jnp.where(
        is_left | is_right,
        at_corner + jnp.where(is_right, 2, 0) + jnp.where(is_after, 1, 0),
        jnp.where(is_after, at_after, at_before) + z,
    )
    slot_list = jnp.where(is_before | is_after, outer, inner).astype(jnp.int32).reshape(-1)

    rows = normed.reshape(-1, width)
    table, reg_kv, keep, send, token = own_project(
        (slab & 1).reshape(1),
        rows,
        registers,
        w_query,
        w_key,
        w_value,
        slots,
        blk,
        head_width,
        2 * lanes,
        scale,
        [],
    )
    rounds = register_rounds(slab, keep, send, w_out)
    next(rounds)
    queries, token = query_project(
        rows, w_query, 2 * lanes, scale, [token, left, right, before, after]
    )
    token = rounds.send([token])

    def windows(table, at, loaded, pieces, mixed, deps):
        return attend(
            queries,
            table,
            reg_kv,
            slot_list,
            slab_blocks,
            at,
            loaded,
            pieces,
            w_key,
            w_value,
            w_out,
            head_width,
            mixed,
            deps,
        )

    inner, outer = list(range(1, own_phases - 1)), [0, own_phases - 1]
    table, mixed, token = windows(table, inner, at_left, [left, right], None, [token])
    token = rounds.send([token])
    corners = [before, after, corner_left, corner_right]
    _, mixed, token = windows(table, outer, at_before, corners, mixed, [token])
    token = rounds.send([token])
    token = rounds.send([])
    return mixed.reshape(own_phases, slab_blocks, blk, width), token


def solution(mesh):
    placed = (P("phase", "slab", None, None), P("phase", "slab", None), P(), P(), P(), P(), P())
    return jax.shard_map(
        shards,
        mesh=mesh,
        in_specs=placed,
        out_specs=(P("phase", "slab", None, None), P()),
        check_vma=False,
    )
```

```python
import functools

import jax
import jax.numpy as jnp
from jax import lax
from jax.experimental import pallas as pl
from jax.experimental.pallas import tpu as pltpu
from jax.sharding import PartitionSpec as P

HEADS = 16
LIST = 5
QUAD = 4
TILE_QUADS = 2
LOG2E = 1.4426950408889634
F32, BF16 = jnp.float32, jnp.bfloat16
ANY = pl.BlockSpec(memory_space=pl.ANY)
VMEM = pl.BlockSpec(memory_space=pltpu.VMEM)
TOKEN = jax.ShapeDtypeStruct((8, 128), jnp.float32)


def params(mib):
    return pltpu.CompilerParams(vmem_limit_bytes=mib << 20)


def cost():
    return pl.CostEstimate(flops=1 << 20, bytes_accessed=1 << 16, transcendentals=0)


def matmul(a, b):
    return jnp.dot(a, b, preferred_element_type=F32)


def matmul_t(a, b):
    return lax.dot_general(a, b, (((1,), (1,)), ((), ())), preferred_element_type=F32)


def t_matmul(a, b):
    return lax.dot_general(a, b, (((0,), (0,)), ((), ())), preferred_element_type=F32)


def spread_heads(q, head_width, heads):
    lane = lax.broadcasted_iota(jnp.int32, q.shape, 1) // head_width
    return jnp.concatenate([jnp.where(lane == h, q, jnp.zeros_like(q)) for h in heads], axis=0)


def soften(s):
    peak = jnp.max(s, axis=0, keepdims=True)
    return jnp.exp2(s - peak).astype(BF16), peak


def pair_context(v, p, head_width):
    wide = 2 * head_width
    ones = jnp.ones((16, v.shape[0]), BF16)
    o = matmul(jnp.concatenate([v.T, ones], axis=0), p)
    total = o[wide : wide + 1]
    inverse = 1.0 / total
    count = p.shape[1] // 2
    outs = [
        o[j * head_width : (j + 1) * head_width, j * count : (j + 1) * count]
        * inverse[:, j * count : (j + 1) * count]
        for j in range(2)
    ]
    return outs, total


def pack_levels(level):
    hi = level.astype(BF16)
    rest = level - hi.astype(F32)
    mid = rest.astype(BF16)
    low = (rest - mid.astype(F32)).astype(BF16)
    pad = jnp.zeros((level.shape[0], 128 - 3 * level.shape[1]), BF16)
    return jnp.concatenate([hi, mid, low, pad], axis=1)


def unpack_levels(cols):
    wide = cols.astype(F32)
    return wide[:, :HEADS] + wide[:, HEADS : 2 * HEADS] + wide[:, 2 * HEADS : 3 * HEADS]


def own_kernel(scale, head_width, core_ref, *refs):
    x_ref, reg_ref, wq_ref, wk_ref, wv_ref = refs[:5]
    kv_ref, reg_kv_ref, keep_ref, send_ref, _, rows_ref, ctx_ref, level_ref = refs[-8:]
    step = pl.program_id(0)
    count, width = x_ref.shape
    regs = reg_ref.shape[0]
    blk, lanes = kv_ref.shape[2:]
    each = lanes // head_width

    @pl.when(step == 0)
    def _():
        rows_ref[:count] = x_ref[...]
        rows_ref[count:] = reg_ref[...]

    tile = pl.ds(pl.multiple_of(step * lanes, lanes), lanes)
    k = matmul(rows_ref[...], wk_ref[...]).astype(BF16)
    q_reg = (matmul(reg_ref[...], wq_ref[...]) * scale).astype(BF16)
    pairs = [(h, h + 1) for h in range(0, each, 2)]

    def score(pair):
        quad = pair[0] // QUAD * QUAD
        at = slice(quad * head_width, (quad + QUAD) * head_width)
        return matmul_t(
            k[:count, at], spread_heads(q_reg[:, at], head_width, [h - quad for h in pair])
        )

    outs, levels = [], []

    def context(pair, p, peak):
        at = slice(pair[0] * head_width, (pair[1] + 1) * head_width)
        found, total = pair_context(v[:count, at], p, head_width)
        outs.extend(found)
        level = peak + jnp.log2(total)
        levels.extend([level[:, :regs], level[:, regs:]])

    following, pending = score(pairs[0]), None
    v = matmul(rows_ref[...], wv_ref[...]).astype(BF16)
    for n, pair in enumerate(pairs):
        s = following
        if n + 1 < len(pairs):
            following = score(pairs[n + 1])
        if pending is not None:
            context(*pending)
        pending = (pair, *soften(s))
    context(*pending)
    for n in range(kv_ref.shape[1]):
        kv_ref[0, n] = k[n * blk : (n + 1) * blk]
        kv_ref[1, n] = v[n * blk : (n + 1) * blk]
    for n in range(reg_kv_ref.shape[1]):
        kv_at = slice(count + n * blk, count + (n + 1) * blk)
        reg_kv_ref[0, n] = k[kv_at]
        reg_kv_ref[1, n] = v[kv_at]
    ctx_ref[:, tile] = jnp.concatenate(outs, axis=0).astype(BF16).T
    level_ref[step] = jnp.concatenate(levels, axis=0)

    @pl.when(step == width // lanes - 1)
    def _():
        stacked = jnp.concatenate([level_ref[g] for g in range(width // lanes)], axis=0)
        ctx_ref[:, width:] = pack_levels(stacked.T)
        half = regs // 2
        core = core_ref[0]
        keep_ref[...] = ctx_ref[pl.ds(pl.multiple_of(core * half, half), half)]
        send_ref[...] = ctx_ref[pl.ds(pl.multiple_of((1 - core) * half, half), half)]


def own_project(core, rows, registers, w_query, w_key, w_value, slots, blk, head_width, lanes, scale, deps):
    count, width = rows.shape
    regs = registers.shape[0]
    half = jax.ShapeDtypeStruct((regs // 2, width + 128), BF16)
    return pl.pallas_call(
        functools.partial(own_kernel, scale, head_width),
        grid_spec=pltpu.PrefetchScalarGridSpec(
            num_scalar_prefetch=1,
            grid=(width // lanes,),
            in_specs=[pl.BlockSpec((count, width), lambda i, s: (0, 0)), pl.BlockSpec((regs, width), lambda i, s: (0, 0))]
            + [pl.BlockSpec((width, lanes), lambda i, s: (0, i))] * 3
            + [ANY] * len(deps),
            out_specs=[
                pl.BlockSpec((2, count // blk, blk, lanes), lambda i, s: (0, 0, 0, i)),
                pl.BlockSpec((2, regs // blk, blk, lanes), lambda i, s: (0, 0, 0, i)),
                pl.BlockSpec(half.shape, lambda i, s: (0, 0)),
                pl.BlockSpec(half.shape, lambda i, s: (0, 0)),
                ANY,
            ],
            scratch_shapes=[
                pltpu.VMEM((count + regs, width), BF16),
                pltpu.VMEM((regs, width + 128), BF16),
                pltpu.VMEM((width // lanes, lanes // head_width, regs), F32),
            ],
        ),
        out_shape=[
            pltpu.HBM((2, slots, blk, width), BF16),
            jax.ShapeDtypeStruct((2, regs // blk, blk, width), BF16),
            half,
            half,
            TOKEN,
        ],
        compiler_params=params(52),
        cost_estimate=cost(),
        name="own_project",
    )(core, rows, registers, w_query, w_key, w_value, *deps)


def query_kernel(scale, x_ref, w_ref, *refs):
    lanes = refs[-2].shape[1]
    at = pl.ds(pl.multiple_of(pl.program_id(0) * lanes, lanes), lanes)
    refs[-2][...] = (matmul(x_ref[...], w_ref[:, at]) * scale).astype(BF16)


def query_project(rows, w_query, lanes, scale, deps):
    count, width = rows.shape
    return pl.pallas_call(
        functools.partial(query_kernel, scale),
        grid=(width // lanes,),
        in_specs=[
            VMEM,
            VMEM,
        ]
        + [ANY] * len(deps),
        out_specs=[pl.BlockSpec((count, lanes), lambda i: (0, i)), ANY],
        out_shape=[pltpu.HBM((count, width), BF16), TOKEN],
        compiler_params=params(20),
        cost_estimate=cost(),
        name="query_project",
    )(rows, w_query, *deps)


def attend_kernel(head_width, phases, loaded, pieces, skipped, idx_ref, *refs):
    refs = iter(refs)

    def take(count):
        return [next(refs) for _ in range(count)]

    q_refs = take(len(phases))
    (reg_ref,) = take(1)
    xs, w_refs = take(pieces), take(2 if pieces else 0)
    table_ref, wo_ref = take(2)
    take(skipped)
    (new_table_ref,) = take(1) if pieces else (None,)
    o_ref, _ = take(2)
    tabs = take(2)
    ctx_ref, wo_scratch, in_sems, wo_sem, o_sems = take(5)
    if pieces:
        rows_ref, x_sems, out_sems = take(3)
    step, last = pl.program_id(0), pl.num_programs(0) - 1
    buf = lax.rem(step, 2)
    slots, blk, lanes = tabs[0].shape[1:]
    each = q_refs[0].shape[0] // blk
    blocks = each * len(phases)

    def columns(g):
        return pl.ds(pl.multiple_of(g * lanes, lanes), lanes)

    def bring(g, b):
        return [
            pltpu.make_async_copy(
                table_ref.at[side, pl.ds(0, loaded), :, columns(g)],
                tabs[side].at[b, pl.ds(0, loaded)],
                in_sems.at[side, b],
            )
            for side in range(2)
        ]

    def give(g, b):
        return [
            pltpu.make_async_copy(
                tabs[side].at[b, pl.ds(loaded, slots - loaded)],
                new_table_ref.at[side, pl.ds(loaded, slots - loaded), :, columns(g)],
                out_sems.at[side, b],
            )
            for side in range(2)
        ]

    def output_weight():
        return pltpu.make_async_copy(wo_ref, wo_scratch, wo_sem.at[0])

    @pl.when(step == 0)
    def _():
        copies, at = [], 0
        for n, x in enumerate(xs):
            copies.append(pltpu.make_async_copy(x, rows_ref.at[pl.ds(at, x.shape[0])], x_sems.at[n]))
            at += x.shape[0]
        for c in copies + bring(0, 0):
            c.start()
        output_weight().start()
        for c in copies:
            c.wait()

    @pl.when(step < last)
    def _():
        for c in bring(step + 1, 1 - buf):
            c.start()

    if pieces:

        @pl.when(step >= 2)
        def _():
            for c in give(step - 2, buf):
                c.wait()

    def project(side):
        if pieces:
            new = matmul(rows_ref[...], w_refs[side][...]).astype(BF16)
            for n in range(slots - loaded):
                tabs[side][buf, loaded + n] = new[n * blk : (n + 1) * blk]

    project(0)
    for c in bring(step, buf):
        c.wait()

    def gathered(side, block, at):
        place = phases[block // each] * each + block % each
        listed = [idx_ref[place * LIST + e] for e in range(LIST)]
        return jnp.concatenate(
            [tabs[side][buf, slot, :, at] for slot in listed]
            + [reg_ref[side, n, :, at] for n in range(reg_ref.shape[1])],
            axis=0,
        )

    quad = QUAD * head_width

    def score(block, group):
        at = slice(group * quad, (group + 1) * quad)
        inner = block % each * blk
        q = q_refs[block // each][inner : inner + blk, at]
        return matmul_t(gathered(0, block, at), spread_heads(q, head_width, range(QUAD)))

    def context(unit, p):
        block, group = unit
        outs = []
        for h in range(0, QUAD, 2):
            at = slice(h * blk, (h + 2) * blk)
            first = group * quad + h * head_width
            v = gathered(1, block, slice(first, first + 2 * head_width))
            outs += pair_context(v, p[:, at], head_width)[0]
        at = pl.ds(pl.multiple_of(step * lanes + group * quad, quad), quad)
        ctx_ref[block * blk : (block + 1) * blk, at] = jnp.concatenate(outs, axis=0).astype(BF16).T

    units = [(block, group) for group in range(lanes // quad) for block in range(blocks)]
    following, pending = score(*units[0]), None
    project(1)
    for n, unit in enumerate(units):
        s = following
        if n + 1 < len(units):
            following = score(*units[n + 1])
        if pending is not None:
            context(*pending)
        p, _ = soften(s)
        pending = (unit, p)
    context(*pending)
    if pieces:
        for c in give(step, buf):
            c.start()

    @pl.when(step == last)
    def _():
        output_weight().wait()
        ctx_ref[...] = matmul(ctx_ref[...], wo_scratch[...]).astype(BF16)
        rows = each * blk
        copies = [
            pltpu.make_async_copy(
                ctx_ref.at[pl.ds(n * rows, rows)], o_ref.at[pl.ds(phase * rows, rows)], o_sems.at[n]
            )
            for n, phase in enumerate(phases)
        ]
        for c in copies:
            c.start()
        for c in copies:
            c.wait()
        if pieces:
            for c in give(step, buf):
                c.wait()

    if pieces:

        @pl.when((step == last) & (last > 0))
        def _():
            for c in give(step - 1, 1 - buf):
                c.wait()


def attend(
    queries, table, reg_kv, slot_list, each, phases, loaded, pieces, w_key, w_value, w_out, head_width, previous, deps
):
    _, all_slots, blk, width = table.shape
    lanes = TILE_QUADS * QUAD * head_width
    rows = each * blk
    pieces = [x.reshape(-1, width) for x in pieces]
    new_rows = sum(x.shape[0] for x in pieces)
    slots = loaded + new_rows // blk
    assert width % lanes == 0
    operands = [slot_list, *[queries] * len(phases), reg_kv, *pieces]
    in_specs = [
        pl.BlockSpec((rows, lanes), functools.partial(lambda p, i, idx: (p, i), phase)) for phase in phases
    ] + [
        pl.BlockSpec((*reg_kv.shape[:3], lanes), lambda i, idx: (0, 0, 0, i)),
    ] + [ANY] * len(pieces)
    if pieces:
        operands += [w_key, w_value]
        in_specs += [pl.BlockSpec((width, lanes), lambda i, idx: (0, i))] * 2
    aliases, out_specs, out_shape = {}, [], []
    if pieces:
        aliases[len(operands)] = 0
        out_specs.append(pl.BlockSpec(memory_space=pltpu.HBM))
        out_shape.append(pltpu.HBM(table.shape, BF16))
    operands += [table, w_out]
    in_specs += [pl.BlockSpec(memory_space=pltpu.HBM), ANY]
    if previous is not None:
        aliases[len(operands)] = len(out_specs)
        operands.append(previous)
        in_specs.append(ANY)
    operands += deps
    in_specs += [ANY] * len(deps)
    skipped = len(deps) + (previous is not None)
    out_specs += [pl.BlockSpec(memory_space=pltpu.HBM), ANY]
    out_shape += [pltpu.HBM(queries.shape, BF16), TOKEN]
    tab = pltpu.VMEM((2, slots, blk, lanes), BF16)
    sems = pltpu.SemaphoreType.DMA
    scratch = [tab, tab, pltpu.VMEM((rows * len(phases), width), BF16), pltpu.VMEM((width, width), BF16)]
    scratch += [sems((2, 2)), sems((1,)), sems((len(phases),))]
    if pieces:
        scratch += [pltpu.VMEM((new_rows, width), BF16), sems((len(pieces),)), sems((2, 2))]
    out = pl.pallas_call(
        functools.partial(attend_kernel, head_width, phases, loaded, len(pieces), skipped),
        grid_spec=pltpu.PrefetchScalarGridSpec(
            num_scalar_prefetch=1,
            grid=(width // lanes,),
            in_specs=in_specs,
            out_specs=out_specs,
            scratch_shapes=scratch,
        ),
        out_shape=out_shape,
        input_output_aliases=aliases,
        compiler_params=params(52),
        cost_estimate=cost(),
        name="attend",
    )(*operands)
    return out if pieces else [table, *out]


def tree(values):
    while len(values) > 1:
        values = [values[n] + values[n + 1] for n in range(0, len(values), 2)]
    return values[0]


def merged(place, refs, all_ref, width):
    for n, r in enumerate(refs):
        all_ref[place ^ n] = r[...]
    count, rows, _ = all_ref.shape
    levels = [unpack_levels(all_ref[n, :, width:]) for n in range(count)]
    top = functools.reduce(jnp.maximum, levels)
    weights = [jnp.exp2(level - top) for level in levels]
    total = tree(weights)
    weights = [w / total for w in weights]
    head_width = width // HEADS
    lower = lax.broadcasted_iota(jnp.int32, (rows, 2 * head_width), 1) < head_width
    cols = []
    for pair in range(HEADS // 2):
        at = slice(pair * 2 * head_width, (pair + 1) * 2 * head_width)

        def spread(w):
            return jnp.where(lower, w[:, 2 * pair : 2 * pair + 1], w[:, 2 * pair + 1 : 2 * pair + 2])

        mix = tree([all_ref[n, :, at].astype(F32) * spread(weights[n]) for n in range(count)])
        cols.append(mix.astype(BF16))
    return jnp.concatenate(cols, axis=1), top + jnp.log2(total)


def small_call(body, out_shape, scratch, name, flag, operands, deps):
    def wrapped(*refs):
        ins, outs = refs[: 1 + len(operands)], refs[1 + len(operands) + len(deps) :]
        body(*ins, outs[0], *outs[2:])

    return pl.pallas_call(
        wrapped,
        in_specs=[pl.BlockSpec(memory_space=pltpu.SMEM)] + [VMEM] * len(operands) + [ANY] * len(deps),
        out_specs=[VMEM, ANY],
        out_shape=[out_shape, TOKEN],
        scratch_shapes=scratch,
        compiler_params=params(16),
        cost_estimate=cost(),
        name=name,
    )(flag, *operands, *deps)


def register_rounds(slab, keep, send, w_out):
    half, wide = keep.shape
    width = wide - 128
    slabs, phases = lax.axis_size("slab"), lax.axis_size("phase")
    phase = lax.axis_index("phase").astype(jnp.int32)
    turns = [("slab", slab & 1, 0, 2), ("slab", slab >> 1, 1, slabs // 2)]
    turns += [("phase", phase, 0, phases)]

    def swap(x, axis, bit, n):
        return lax.ppermute(x, axis, [(i, i ^ (n << bit)) for i in range(lax.axis_size(axis))])

    def merge_body(place_ref, *refs):
        mix, level = merged(place_ref[0], refs[:-2], refs[-1], width)
        refs[-2][:, :width] = mix
        refs[-2][:, width:] = pack_levels(level)

    def last_body(place_ref, *refs):
        mix, _ = merged(place_ref[0], refs[:-3], refs[-1], width)
        refs[-2][...] = matmul(mix, refs[-3][...]).astype(BF16)

    def join_body(core_ref, mine_ref, got_ref, out_ref):
        core = core_ref[0]
        out_ref[pl.ds(pl.multiple_of(core * half, half), half)] = mine_ref[...]
        out_ref[pl.ds(pl.multiple_of((1 - core) * half, half), half)] = got_ref[...]

    mine, token = keep, None
    for n, (axis, place, bit, size) in enumerate(turns):
        got = [swap(send if n == 0 else mine, axis, bit, j) for j in range(1, size)]
        deps = yield token
        scratch = [pltpu.VMEM((size, half, wide), BF16)]
        place = place.reshape(1)
        if n + 1 < len(turns):
            shape = jax.ShapeDtypeStruct((half, wide), BF16)
            mine, token = small_call(merge_body, shape, scratch, "register_merge", place, [mine, *got], deps)
        else:
            shape = jax.ShapeDtypeStruct((half, width), BF16)
            mine, token = small_call(
                last_body, shape, scratch, "register_out", place, [mine, *got, w_out], deps
            )
    got = swap(mine, "slab", 0, 1)
    deps = yield token
    shape = jax.ShapeDtypeStruct((2 * half, width), BF16)
    out, _ = small_call(join_body, shape, [], "register_join", (slab & 1).reshape(1), [mine, got], deps)
    yield out


def shards(normed, block_list, registers, w_query, w_key, w_value, w_out):
    own_phases, slab_blocks, blk, width = normed.shape
    head_width = width // HEADS
    lanes = QUAD * head_width
    phases, slabs = lax.axis_size("phase"), lax.axis_size("slab")
    own = own_phases * slab_blocks
    slab = lax.axis_index("slab").astype(jnp.int32)
    scale = head_width ** (-0.5) * LOG2E

    def around(x, axis, step, closed):
        n = lax.axis_size(axis)
        return lax.ppermute(
            x, axis, [(i, (i + step) % n) for i in range(n) if closed or 0 <= i + step < n]
        )

    before = around(normed[-1], "phase", 1, True)
    after = around(normed[0], "phase", -1, True)
    left = around(normed[:, -1], "slab", 1, False)
    right = around(normed[:, 0], "slab", -1, False)
    corner_left = around(jnp.stack([before[-1], after[-1]]), "slab", 1, False)
    corner_right = around(jnp.stack([before[0], after[0]]), "slab", -1, False)

    at_left = own
    at_right = at_left + own_phases
    at_before = at_right + own_phases
    at_after = at_before + slab_blocks
    at_corner = at_after + slab_blocks
    slots = at_corner + 4
    assert own == at_before - at_left == slots - at_before

    total_phases, depth_blocks = own_phases * phases, slab_blocks * slabs
    p = (block_list // depth_blocks - lax.axis_index("phase") * own_phases + 1) % total_phases - 1
    z = block_list % depth_blocks - slab * slab_blocks
    is_left, is_right = z < 0, z >= slab_blocks
    is_before, is_after = p < 0, p >= own_phases
    inner = jnp.where(is_left, at_left + p, jnp.where(is_right, at_right + p, p * slab_blocks + z))
    outer = jnp.where(
        is_left | is_right,
        at_corner + jnp.where(is_right, 2, 0) + jnp.where(is_after, 1, 0),
        jnp.where(is_after, at_after, at_before) + z,
    )
    slot_list = jnp.where(is_before | is_after, outer, inner).astype(jnp.int32).reshape(-1)

    rows = normed.reshape(-1, width)
    table, reg_kv, keep, send, token = own_project(
        (slab & 1).reshape(1),
        rows,
        registers,
        w_query,
        w_key,
        w_value,
        slots,
        blk,
        head_width,
        2 * lanes,
        scale,
        [],
    )
    rounds = register_rounds(slab, keep, send, w_out)
    next(rounds)
    queries, token = query_project(
        rows, w_query, 2 * lanes, scale, [token, left, right, before, after]
    )
    token = rounds.send([token])

    def windows(table, at, loaded, pieces, mixed, deps):
        return attend(
            queries,
            table,
            reg_kv,
            slot_list,
            slab_blocks,
            at,
            loaded,
            pieces,
            w_key,
            w_value,
            w_out,
            head_width,
            mixed,
            deps,
        )

    inner, outer = list(range(1, own_phases - 1)), [0, own_phases - 1]
    table, mixed, token = windows(table, inner, at_left, [left, right], None, [token])
    token = rounds.send([token])
    corners = [before, after, corner_left, corner_right]
    _, mixed, token = windows(table, outer, at_before, corners, mixed, [token])
    token = rounds.send([token])
    token = rounds.send([])
    return mixed.reshape(own_phases, slab_blocks, blk, width), token


def solution(mesh):
    placed = (P("phase", "slab", None, None), P("phase", "slab", None), P(), P(), P(), P(), P())
    return jax.shard_map(
        shards,
        mesh=mesh,
        in_specs=placed,
        out_specs=(P("phase", "slab", None, None), P()),
        check_vma=False,
    )
```
